32 devices in a mesh: groups: 2 (over x), blk: 8 (over z, core), dim: 2 (over y).
Axes of the slice: x: 2, y: 2, z: 4, core: 2. Of those that a mesh axis runs over, the one named last changes fastest.
Arguments:
- grad_codes: bfloat16 [32768, 16384], P(('groups', 'blk'), 'dim'), parts along dimension 0, may hold values from -6 to 6
- scale_exps: int32 [32768, 128], P(('groups', 'blk'), 'dim'), parts along dimension 0, may hold values from -2 to 2
- val_grads: bfloat16 [2048, 16384], P(('groups', 'blk'), 'dim'), parts along dimension 0, may hold values from -0.046875 to 0.046875
- fisher: float32 [16384], P('dim'), may hold values from 0.5 to 4
Outputs:
- scores: float32 [1024, 32768], P('dim', ('groups', 'blk')), parts along dimension 1
The draws below stay inside these ranges and needn't reach their ends.
There are 2 independent parts, one for each index of `groups`. The reference program is written for one: setup_inputs(seed, part) draws one part's arguments, and reference() takes and returns one part's arrays. A program takes and returns all parts, laid end to end along the dimension named above; an argument that names none is the same for every part. Nothing has to cross between parts.
All inputs are finite; a program needn't handle non-finite values.
Results may differ from the reference program's by a relative error of at most 0.0029.
Values may be sent and summed in bfloat16 or wider, within the bound.
No kernel may reach another device: no remote copies, remote signals or barrier semaphores. Data moves between devices by JAX's collectives and lax.ppermute only.
A program may use at most 320 MiB of HBM per device.

```python
import math
import jax
import jax.numpy as jnp
from jax import lax

QUERIES = 1024
KDIMS = 16384
NTRAIN = 16384
NBLOCKS = 128


def place_ends(result, stream_key, least, high):
    spot = [jax.random.randint(jax.random.fold_in(stream_key, axis), (), 0, length) for axis, length in enumerate(result.shape)]
    main_axis = result.shape.index(max(result.shape))
    beside = spot[:main_axis] + [(spot[main_axis] + 1) % result.shape[main_axis]] + spot[main_axis + 1:]
    return result.at[tuple(spot)].set(least).at[tuple(beside)].set(high)


def block_levels(own_key, dims, cuts, least, high):
    factor_of, own = 1.0, jax.random.fold_in(own_key, 6)
    for dim, parts in cuts:
        heights = jnp.exp(jax.random.uniform(jax.random.fold_in(own, dim), (parts,), jnp.float32, least / len(cuts), high / len(cuts)))
        factor_of = factor_of * jnp.repeat(heights, dims[dim] // parts).reshape([-1 if axis == dim else 1 for axis in range(len(dims))])
    return factor_of


def centred(stream_key, extent, scale, bound, shards=(), held_as=jnp.bfloat16):
    values = jax.random.normal(stream_key, extent, jnp.float32) * scale
    if len(shards) > 0:
        values = block_levels(stream_key, extent, shards, -0.22, 0.18) * values
    return jnp.clip(values, min=-bound, max=bound).astype(held_as)


def setup_inputs(seed: int = 0, part: int = 0) -> dict:
    streams_of = jax.random.split(jax.random.key(seed), 5)
    part_splits = jax.random.split(jax.random.fold_in(streams_of[4], part), 5)
    return {
        "grad_codes": centred(part_splits[0], (NTRAIN, KDIMS), 1.0, 6.0, ((0, 8), (1, 2))),
        "scale_exps": place_ends(jax.random.randint(part_splits[1], (NTRAIN, NBLOCKS), -2, 3), jax.random.fold_in(part_splits[1], 1), -2, 2).astype(jnp.int32),
        "val_grads": centred(part_splits[2], (QUERIES, KDIMS), KDIMS ** -0.5, 0.046875, ((0, 8), (1, 2))),
        "fisher": jnp.clip(jnp.exp(math.log(4.0) - 2.0794415 * jax.random.uniform(streams_of[3], (KDIMS,), jnp.float32) ** block_levels(streams_of[3], (KDIMS,), ((0, 2),), -0.2, 0.2)), 0.5, 4.0),
    }


damping = 0.05


def dequantize(grad_codes, scale_exps):
    count, width = grad_codes.shape
    factor = jnp.exp2(scale_exps.astype(jnp.float32))
    blocks = grad_codes.astype(jnp.float32).reshape(count, width // 128, 128) * factor[:, :, None]
    return blocks.reshape(count, width).astype(jnp.bfloat16)


def reference(grad_codes, scale_exps, val_grads, fisher):
    train = dequantize(grad_codes, scale_exps)
    precond = (val_grads.astype(jnp.float32) / (fisher + damping)[None, :]).astype(jnp.bfloat16)
    return jnp.dot(precond.astype(jnp.float32), train.astype(jnp.float32).T, precision=lax.Precision.HIGHEST)
```

```python
import functools

import jax
import jax.numpy as jnp
from jax import lax
from jax.experimental import pallas as pl
from jax.experimental.pallas import tpu as pltpu
from jax.sharding import PartitionSpec as P

damping = 0.05
lanes = 128
mib = 1 << 20


def dequantize_kernel(codes_ref, exps_ref, train_ref):
    exps = exps_ref[...]
    up = jnp.left_shift(1, jnp.maximum(exps, 0)).astype(jnp.float32)
    down = jnp.left_shift(1, jnp.maximum(-exps, 0)).astype(jnp.float32)
    factor = up / down
    for block in range(exps.shape[1]):
        cols = slice(block * lanes, (block + 1) * lanes)
        codes = codes_ref[:, cols].astype(jnp.float32)
        train_ref[:, cols] = (codes * factor[:, block:block + 1]).astype(jnp.bfloat16)


def dequantize(codes, exps):
    count, width = codes.shape
    rows = min(count, 256)
    return pl.pallas_call(
        dequantize_kernel,
        grid=(count // rows,),
        in_specs=[
            pl.BlockSpec((rows, width), lambda i: (i, 0)),
            pl.BlockSpec((rows, width // lanes), lambda i: (i, 0)),
        ],
        out_specs=pl.BlockSpec((rows, width), lambda i: (i, 0)),
        out_shape=jax.ShapeDtypeStruct((count, width), jnp.bfloat16),
        compiler_params=pltpu.CompilerParams(vmem_limit_bytes=40 * mib),
        cost_estimate=pl.CostEstimate(
            flops=2 * count * width, bytes_accessed=4 * count * width, transcendentals=0
        ),
        name="dequantize",
    )(codes, exps)


def partial_kernel(owners, me_ref, *refs):
    panels = refs[:owners]
    fisher_ref, train_ref, keep_ref, send_ref, left = refs[owners:]
    rows = panels[0].shape[0]

    @pl.when(pl.program_id(0) == 0)
    def _():
        scale = 1.0 / (fisher_ref[...] + damping)
        for owner in range(owners):
            vals = panels[owner][...].astype(jnp.float32)
            left[owner * rows:(owner + 1) * rows, :] = (vals * scale).astype(jnp.bfloat16)

    sums = lax.dot_general(
        left[...], train_ref[...], (((1,), (1,)), ((), ())), preferred_element_type=jnp.float32
    )
    keep_ref[...] = sums[:rows]
    send_ref[...] = sums[rows:].astype(jnp.bfloat16)


def partials(me, owners, panel, fisher, train):
    count, width = train.shape
    queries = panel.shape[0]
    rows = queries // owners
    tile = min(count, 256)

    def of_owner(step):
        return pl.BlockSpec((rows, width), lambda i, me_ref: (lax.rem(me_ref[0] + step, owners), 0))

    return pl.pallas_call(
        functools.partial(partial_kernel, owners),
        grid_spec=pltpu.PrefetchScalarGridSpec(
            num_scalar_prefetch=1,
            grid=(count // tile,),
            in_specs=[of_owner(step) for step in range(owners)] + [
                pl.BlockSpec((1, width), lambda i, me_ref: (0, 0)),
                pl.BlockSpec((tile, width), lambda i, me_ref: (i, 0)),
            ],
            out_specs=[
                pl.BlockSpec((rows, tile), lambda i, me_ref: (0, i)),
                pl.BlockSpec((queries - rows, tile), lambda i, me_ref: (0, i)),
            ],
            scratch_shapes=[pltpu.VMEM((queries, width), jnp.bfloat16)],
        ),
        out_shape=[
            jax.ShapeDtypeStruct((rows, count), jnp.float32),
            jax.ShapeDtypeStruct((queries - rows, count), jnp.bfloat16),
        ],
        compiler_params=pltpu.CompilerParams(vmem_limit_bytes=40 * mib),
        cost_estimate=pl.CostEstimate(
            flops=2 * queries * count * width, bytes_accessed=2 * count * width, transcendentals=0
        ),
        name="partials",
    )(me, *([panel] * owners), fisher, train)


def shards(blks, owners, grad_codes, scale_exps, val_grads, fisher):
    me = lax.axis_index("dim")[None]
    own, width = val_grads.shape
    count = grad_codes.shape[0]
    per_owner = blks // owners
    chunks = 4
    rows = own // chunks
    fisher = fisher[None, :]
    gathered = [
        lax.all_gather(val_grads[chunk * rows:(chunk + 1) * rows], "blk", axis=0, tiled=True)
        for chunk in range(chunks)
    ]
    train = dequantize(grad_codes, scale_exps)
    scores = jnp.zeros((per_owner, own, count), jnp.float32)
    for chunk in range(chunks):
        keep, send = partials(me, owners, gathered[chunk], fisher, train)
        total = keep
        for step in range(1, owners):
            part = send[(step - 1) * per_owner * rows:step * per_owner * rows]
            pairs = [(dev, (dev + step) % owners) for dev in range(owners)]
            total = total + lax.ppermute(part, "dim", pairs).astype(jnp.float32)
        scores = lax.dynamic_update_slice(
            scores, total.reshape(per_owner, rows, count), (0, chunk * rows, 0)
        )
    return scores.reshape(per_owner * own, count)


def solution(mesh):
    in_specs = (
        P(("groups", "blk"), "dim"),
        P(("groups", "blk"), "dim"),
        P(("groups", "blk"), "dim"),
        P("dim"),
    )
    out_specs = P("dim", ("groups", "blk"))
    body = functools.partial(shards, mesh.shape["blk"], mesh.shape["dim"])
    return jax.shard_map(body, mesh=mesh, in_specs=in_specs, out_specs=out_specs, check_vma=False)
```

```python
import functools

import jax
import jax.numpy as jnp
from jax import lax
from jax.experimental import pallas as pl
from jax.experimental.pallas import tpu as pltpu
from jax.sharding import PartitionSpec as P

damping = 0.05
lanes = 128
cores = 2
mib = 1 << 20


def dequantize_kernel(codes_ref, exps_ref, train_ref):
    exps = exps_ref[...]
    up = jnp.left_shift(1, jnp.maximum(exps, 0)).astype(jnp.float32)
    down = jnp.left_shift(1, jnp.maximum(-exps, 0)).astype(jnp.float32)
    factor = up / down
    for block in range(exps.shape[1]):
        cols = slice(block * lanes, (block + 1) * lanes)
        codes = codes_ref[:, cols].astype(jnp.float32)
        train_ref[:, cols] = (codes * factor[:, block:block + 1]).astype(jnp.bfloat16)


def dequantize(codes, exps):
    count, width = codes.shape
    rows = min(count, 256)
    return pl.pallas_call(
        dequantize_kernel,
        grid=(count // rows,),
        in_specs=[
            pl.BlockSpec((rows, width), lambda i: (i, 0)),
            pl.BlockSpec((rows, width // lanes), lambda i: (i, 0)),
        ],
        out_specs=pl.BlockSpec((rows, width), lambda i: (i, 0)),
        out_shape=jax.ShapeDtypeStruct((count, width), jnp.bfloat16),
        compiler_params=pltpu.CompilerParams(vmem_limit_bytes=40 * mib),
        cost_estimate=pl.CostEstimate(
            flops=2 * count * width, bytes_accessed=4 * count * width, transcendentals=0
        ),
        name="dequantize",
    )(codes, exps)


def partial_kernel(keep_rows, spots_ref, *refs):
    panels = refs[:-6]
    fisher_ref, train_ref, keep_ref, send_ref, left, sums = refs[-6:]
    rows = panels[0].shape[0]
    step = pl.program_id(0)

    scale = 1.0 / (fisher_ref[...] + damping)
    for index, panel in enumerate(panels):
        spot = pl.ds(pl.multiple_of(spots_ref[index] * rows, rows), rows)
        left[spot, :] = (panel[...].astype(jnp.float32) * scale).astype(jnp.bfloat16)
    term = lax.dot_general(
        train_ref[...], left[...], (((1,), (1,)), ((), ())), preferred_element_type=jnp.float32
    )

    @pl.when(step == 0)
    def _():
        sums[...] = term

    @pl.when(step > 0)
    def _():
        sums[...] += term

    @pl.when(step == pl.num_programs(0) - 1)
    def _():
        turned = sums[...].T
        keep_ref[...] = turned[:keep_rows]
        send_ref[...] = turned[keep_rows:].astype(jnp.bfloat16)


def partials(spots, panels, keep_rows, rows, fisher, train):
    count, width = train.shape
    queries = rows * len(panels)
    depth = min(width, 1024)

    def spec(block):
        return pl.BlockSpec((rows, depth), lambda k, spots_ref: (block, k))

    return pl.pallas_call(
        functools.partial(partial_kernel, keep_rows),
        grid_spec=pltpu.PrefetchScalarGridSpec(
            num_scalar_prefetch=1,
            grid=(width // depth,),
            in_specs=[spec(block) for _, block in panels] + [
                pl.BlockSpec((1, depth), lambda k, spots_ref: (0, k)),
                pl.BlockSpec((count, depth), lambda k, spots_ref: (0, k)),
            ],
            out_specs=[
                pl.BlockSpec((keep_rows, count), lambda k, spots_ref: (0, 0)),
                pl.BlockSpec((queries - keep_rows, count), lambda k, spots_ref: (0, 0)),
            ],
            scratch_shapes=[
                pltpu.VMEM((queries, depth), jnp.bfloat16),
                pltpu.VMEM((count, queries), jnp.float32),
            ],
        ),
        out_shape=[
            jax.ShapeDtypeStruct((keep_rows, count), jnp.float32),
            jax.ShapeDtypeStruct((queries - keep_rows, count), jnp.bfloat16),
        ],
        compiler_params=pltpu.CompilerParams(vmem_limit_bytes=40 * mib),
        cost_estimate=pl.CostEstimate(
            flops=2 * queries * count * width, bytes_accessed=2 * count * width, transcendentals=0
        ),
        name="partials",
    )(spots, *[panel for panel, _ in panels], fisher, train)


def shards(blks, owners, grad_codes, scale_exps, val_grads, fisher):
    chips = blks // cores
    per_owner = blks // owners
    me = lax.axis_index("dim")
    blk = lax.axis_index("blk")
    chip, core = blk // cores, lax.rem(blk, cores)
    own, width = val_grads.shape
    count = grad_codes.shape[0]
    fisher = fisher[None, :]

    def shift(panel, by):
        pairs = [
            (z * cores + c, (z + by) % chips * cores + c) for z in range(chips) for c in range(cores)
        ]
        return lax.ppermute(panel, "blk", pairs)

    def swap(panel):
        return lax.ppermute(panel, "blk", [(b, b ^ 1) for b in range(blks)])

    ups = chips // 2
    pieces = 4
    rows = own // pieces
    held = {0: val_grads}
    for by in range(1, ups):
        held[by] = shift(held[by - 1], 1)
    for by in range(1, chips - ups):
        held[-by] = shift(held[1 - by], -1)
    last = [shift(held[ups - 1][piece * rows:(piece + 1) * rows], 1) for piece in range(pieces)]
    other = {by: swap(panel) for by, panel in held.items()}
    last_other = [swap(panel) for panel in last]
    train = dequantize(grad_codes, scale_exps)

    spots = []
    for by in list(held) + [ups]:
        spot = lax.rem(chip - by + 2 * chips - me * (per_owner // cores), chips)
        spots += [spot * cores + core, spot * cores + 1 - core]
    spots = jnp.stack(spots).astype(jnp.int32)

    scores = jnp.zeros((per_owner, own, count), jnp.float32)
    for piece in range(pieces):
        panels = []
        for by in held:
            panels += [(held[by], piece), (other[by], piece)]
        panels += [(last[piece], 0), (last_other[piece], 0)]
        keep, send = partials(spots, panels, per_owner * rows, rows, fisher, train)
        total = keep
        for step in range(1, owners):
            part = send[(step - 1) * per_owner * rows:step * per_owner * rows]
            pairs = [(dev, (dev + step) % owners) for dev in range(owners)]
            total = total + lax.ppermute(part, "dim", pairs).astype(jnp.float32)
        scores = lax.dynamic_update_slice(
            scores, total.reshape(per_owner, rows, count), (0, piece * rows, 0)
        )
    return scores.reshape(per_owner * own, count)


def solution(mesh):
    in_specs = (
        P(("groups", "blk"), "dim"),
        P(("groups", "blk"), "dim"),
        P(("groups", "blk"), "dim"),
        P("dim"),
    )
    out_specs = P("dim", ("groups", "blk"))
    body = functools.partial(shards, mesh.shape["blk"], mesh.shape["dim"])
    return jax.shard_map(body, mesh=mesh, in_specs=in_specs, out_specs=out_specs, check_vma=False)
```

```python
import functools

import jax
import jax.numpy as jnp
from jax import lax
from jax.experimental import pallas as pl
from jax.experimental.pallas import tpu as pltpu
from jax.sharding import PartitionSpec as P

damping = 0.05
lanes = 128
cores = 2
mib = 1 << 20


def dequantize_kernel(codes_ref, exps_ref, train_ref):
    exps = exps_ref[...]
    up = jnp.left_shift(1, jnp.maximum(exps, 0)).astype(jnp.float32)
    down = jnp.left_shift(1, jnp.maximum(-exps, 0)).astype(jnp.float32)
    factor = up / down
    for block in range(exps.shape[1]):
        cols = slice(block * lanes, (block + 1) * lanes)
        codes = codes_ref[:, cols].astype(jnp.float32)
        train_ref[:, cols] = (codes * factor[:, block:block + 1]).astype(jnp.bfloat16)


def dequantize(codes, exps):
    count, width = codes.shape
    rows = min(count, 256)
    return pl.pallas_call(
        dequantize_kernel,
        grid=(count // rows,),
        in_specs=[
            pl.BlockSpec((rows, width), lambda i: (i, 0)),
            pl.BlockSpec((rows, width // lanes), lambda i: (i, 0)),
        ],
        out_specs=pl.BlockSpec((rows, width), lambda i: (i, 0)),
        out_shape=jax.ShapeDtypeStruct((count, width), jnp.bfloat16),
        compiler_params=pltpu.CompilerParams(vmem_limit_bytes=40 * mib),
        cost_estimate=pl.CostEstimate(
            flops=2 * count * width, bytes_accessed=4 * count * width, transcendentals=0
        ),
        name="dequantize",
    )(codes, exps)


def after(array, *others):
    return lax.optimization_barrier((array, *others))[0]


def shards(blks, owners, grad_codes, scale_exps, val_grads, fisher):
    chips = blks // cores
    chips_per_owner = chips // owners
    me = lax.axis_index("dim")
    blk = lax.axis_index("blk")
    chip, core = blk // cores, lax.rem(blk, cores)
    own, width = val_grads.shape
    count = grad_codes.shape[0]
    scale = 1.0 / (fisher + damping)[None, :]

    def shift(panel, by):
        pairs = [
            (z * cores + c, (z + by) % chips * cores + c) for z in range(chips) for c in range(cores)
        ]
        return lax.ppermute(panel, "blk", pairs)

    def swap(panel):
        return lax.ppermute(panel, "blk", [(b, b ^ 1) for b in range(blks)])

    def partial(mine, theirs, train):
        both = jnp.stack([jnp.where(core == 0, mine, theirs), jnp.where(core == 0, theirs, mine)])
        both = (both.astype(jnp.float32) * scale).astype(jnp.bfloat16).reshape(-1, width)
        return lax.dot_general(
            both, train, (((1,), (1,)), ((), ())), preferred_element_type=jnp.float32
        )

    def collect(scores, part, by, start):
        total = part
        sent = part.astype(jnp.bfloat16)
        for step in range(1, owners):
            pairs = []
            for b in range(blks):
                owner = (b // cores - by) % chips // chips_per_owner
                pairs.append((b * owners + (owner + step) % owners, b * owners + owner))
            total = total + lax.ppermute(sent, ("blk", "dim"), pairs).astype(jnp.float32)
        source = lax.rem(chip - by + chips, chips)
        spot = (lax.rem(source, chips_per_owner), 0, start, 0)
        total = total.reshape(1, cores, -1, count)
        before = lax.dynamic_slice(scores, spot, total.shape)
        total = jnp.where(source // chips_per_owner == me, total, before)
        return lax.dynamic_update_slice(scores, total, spot)

    ups = chips // 2
    pieces = 4
    rows = own // pieces
    scores = jnp.zeros((chips_per_owner, cores, own, count), jnp.float32)
    held = {0: val_grads}
    for by in range(1, chips - ups):
        held[by] = shift(held[by - 1], 1)
        held[-by] = shift(held[1 - by], -1)
    if ups - 1 not in held:
        held[ups - 1] = shift(held[ups - 2], 1)
    train = dequantize(grad_codes, scale_exps)
    part = partial(val_grads, swap(val_grads), train)
    scores = collect(scores, part, 0, 0)
    for by in [by for by in held if by != 0]:
        panel = after(held[by], part)
        if by == ups - 1:
            last = [shift(panel[piece * rows:(piece + 1) * rows], 1) for piece in range(pieces)]
        part = partial(panel, swap(panel), train)
        scores = collect(scores, part, by, 0)
    for piece in range(pieces):
        panel = after(last[piece], part)
        part = partial(panel, swap(panel), train)
        scores = collect(scores, part, ups, piece * rows)
    return scores.reshape(chips_per_owner * cores * own, count)


def solution(mesh):
    in_specs = (
        P(("groups", "blk"), "dim"),
        P(("groups", "blk"), "dim"),
        P(("groups", "blk"), "dim"),
        P("dim"),
    )
    out_specs = P("dim", ("groups", "blk"))
    body = functools.partial(shards, mesh.shape["blk"], mesh.shape["dim"])
    return jax.shard_map(body, mesh=mesh, in_specs=in_specs, out_specs=out_specs, check_vma=False)
```

```python
import functools

import jax
import jax.numpy as jnp
from jax import lax
from jax.experimental import pallas as pl
from jax.experimental.pallas import tpu as pltpu
from jax.sharding import PartitionSpec as P

damping = 0.05
lanes = 128
cores = 2
mib = 1 << 20
in_vmem = pl.BlockSpec(memory_space=pltpu.VMEM)
in_smem = pl.BlockSpec(memory_space=pltpu.SMEM)
anywhere = pl.BlockSpec(memory_space=pl.ANY)
small = pl.CostEstimate(flops=1, bytes_accessed=1, transcendentals=0)


def dequantize_kernel(codes_ref, exps_ref, train_ref):
    exps = exps_ref[...]
    up = jnp.left_shift(1, jnp.maximum(exps, 0)).astype(jnp.float32)
    down = jnp.left_shift(1, jnp.maximum(-exps, 0)).astype(jnp.float32)
    factor = up / down
    for block in range(exps.shape[1]):
        cols = slice(block * lanes, (block + 1) * lanes)
        codes = codes_ref[:, cols].astype(jnp.float32)
        train_ref[:, cols] = (codes * factor[:, block:block + 1]).astype(jnp.bfloat16)


def dequantize(codes, exps):
    count, width = codes.shape
    rows = min(count, 256)
    return pl.pallas_call(
        dequantize_kernel,
        grid=(count // rows,),
        in_specs=[
            pl.BlockSpec((rows, width), lambda i: (i, 0)),
            pl.BlockSpec((rows, width // lanes), lambda i: (i, 0)),
        ],
        out_specs=pl.BlockSpec((rows, width), lambda i: (i, 0)),
        out_shape=jax.ShapeDtypeStruct((count, width), jnp.bfloat16),
        compiler_params=pltpu.CompilerParams(vmem_limit_bytes=32 * mib),
        cost_estimate=small,
        name="dequantize",
    )(codes, exps)


def multiply_kernel(core_ref, *refs):
    mine_ref, *parts = refs[:-12]
    fisher_ref, train_ref, keep_ref, send_ref = refs[-12:-8]
    left, keep, send, held, in_sems, keep_sems, send_sems, train_sems = refs[-8:]
    rows, width = mine_ref.shape
    count = train_ref.shape[0]
    slots, tile, _ = held.shape
    tiles = count // tile
    half = tile // 2
    depth = min(width, 1024)
    core = core_ref[0]

    def fetches(i):
        slot = lax.rem(i, slots)
        return [
            pltpu.make_async_copy(
                train_ref.at[pl.ds(pl.multiple_of(i * tile, tile) + part * half, half)],
                held.at[slot, pl.ds(part * half, half)],
                train_sems.at[slot, part],
            )
            for part in range(2)
        ]

    mine_spot = pl.ds(pl.multiple_of(core * rows, rows), rows)
    loads = [pltpu.make_async_copy(mine_ref, left.at[mine_spot], in_sems.at[0])]
    offset = 0
    for index, ref in enumerate(parts):
        spot = pl.ds(pl.multiple_of((1 - core) * rows, rows) + offset, ref.shape[0])
        loads.append(pltpu.make_async_copy(ref, left.at[spot], in_sems.at[index + 1]))
        offset += ref.shape[0]
    for load in loads:
        load.start()
    for i in range(min(slots, tiles)):
        for fetch in fetches(i):
            fetch.start()
    for load in loads:
        load.wait()

    @pl.loop(0, width // depth)
    def _(k):
        cols = pl.ds(pl.multiple_of(k * depth, depth), depth)
        scale = 1.0 / (fisher_ref[:, cols] + damping)
        left[:, cols] = (left[:, cols].astype(jnp.float32) * scale).astype(jnp.bfloat16)

    def stores(i):
        cols = pl.ds(pl.multiple_of(i * tile, tile), tile)
        return (
            pltpu.make_async_copy(keep.at[:, cols], keep_ref.at[:, cols], keep_sems.at[i]),
            pltpu.make_async_copy(send.at[:, cols], send_ref.at[:, cols], send_sems.at[i]),
        )

    @pl.loop(0, tiles)
    def _(i):
        cols = pl.ds(pl.multiple_of(i * tile, tile), tile)
        for fetch in fetches(i):
            fetch.wait()
        sums = lax.dot_general(
            left[...], held[lax.rem(i, slots)], (((1,), (1,)), ((), ())),
            preferred_element_type=jnp.float32,
        )
        keep[:, cols] = sums
        send[:, cols] = sums.astype(jnp.bfloat16)
        for store in stores(i):
            store.start()

        @pl.when(i + slots < tiles)
        def _():
            for fetch in fetches(i + slots):
                fetch.start()

    @pl.loop(0, tiles)
    def _(i):
        for store in stores(i):
            store.wait()


def multiply(core, mine, parts, fisher, train):
    rows, width = mine.shape
    count = train.shape[0]
    tile = min(count, 256)
    shape = (cores * rows, count)
    return pl.pallas_call(
        multiply_kernel,
        in_specs=[in_smem] + [anywhere] * (1 + len(parts)) + [in_vmem, anywhere],
        out_specs=[anywhere] * 2,
        out_shape=[
            jax.ShapeDtypeStruct(shape, jnp.float32), jax.ShapeDtypeStruct(shape, jnp.bfloat16),
        ],
        scratch_shapes=[
            pltpu.VMEM((cores * rows, width), jnp.bfloat16),
            pltpu.VMEM(shape, jnp.float32),
            pltpu.VMEM(shape, jnp.bfloat16),
            pltpu.VMEM((4, tile, width), jnp.bfloat16),
            pltpu.SemaphoreType.DMA((1 + len(parts),)),
            pltpu.SemaphoreType.DMA((count // tile,)),
            pltpu.SemaphoreType.DMA((count // tile,)),
            pltpu.SemaphoreType.DMA((4, 2)),
        ],
        compiler_params=pltpu.CompilerParams(vmem_limit_bytes=32 * mib),
        cost_estimate=small,
        name="multiply",
    )(core, mine, *parts, fisher, train)


def place_kernel(start, parts, mine_ref, spot_ref, *refs):
    keep_ref, received = refs[0], refs[1:1 + parts]
    scores_ref, total, terms, in_sems, out_sems = refs[-5:]
    rows = keep_ref.shape[0] // cores

    @pl.when(mine_ref[0] == 1)
    def _():
        loads = [pltpu.make_async_copy(keep_ref, total, in_sems.at[0])]
        for index, ref in enumerate(received):
            loads.append(pltpu.make_async_copy(ref, terms.at[index], in_sems.at[index + 1]))
        for load in loads:
            load.start()
        for load in loads:
            load.wait()
        for index in range(parts):
            total[...] += terms[index].astype(jnp.float32)
        copies = [
            pltpu.make_async_copy(
                total.at[pl.ds(c * rows, rows)],
                scores_ref.at[spot_ref[0], c, pl.ds(start, rows)],
                out_sems.at[c],
            )
            for c in range(cores)
        ]
        for copy in copies:
            copy.start()
        for copy in copies:
            copy.wait()


def place(scores, shape, mine, spot, keep, received, start):
    given = [] if scores is None else [scores]
    parts = len(received)
    return pl.pallas_call(
        functools.partial(place_kernel, start, parts),
        in_specs=[in_smem] * 2 + [anywhere] * (1 + parts + len(given)),
        out_specs=anywhere,
        out_shape=jax.ShapeDtypeStruct(shape, jnp.float32),
        scratch_shapes=[
            pltpu.VMEM(keep.shape, jnp.float32),
            pltpu.VMEM((parts, *keep.shape), jnp.bfloat16),
            pltpu.SemaphoreType.DMA((1 + parts,)),
            pltpu.SemaphoreType.DMA((cores,)),
        ],
        input_output_aliases={3 + parts: 0} if given else {},
        compiler_params=pltpu.CompilerParams(vmem_limit_bytes=12 * mib),
        cost_estimate=small,
        name="place",
    )(mine, spot, keep, *received, *given)


def cut_kernel(lows, whole_ref, *refs):
    sems = refs[-1]
    copies = [
        pltpu.make_async_copy(whole_ref.at[pl.ds(low, ref.shape[0])], ref, sems.at[index])
        for index, (low, ref) in enumerate(zip(lows, refs[:-1]))
    ]
    for copy in copies:
        copy.start()
    for copy in copies:
        copy.wait()


def cut(whole, cuts):
    return pl.pallas_call(
        functools.partial(cut_kernel, [low for low, _ in cuts]),
        in_specs=[anywhere],
        out_specs=[anywhere] * len(cuts),
        out_shape=[
            jax.ShapeDtypeStruct((high - low, whole.shape[1]), whole.dtype) for low, high in cuts
        ],
        scratch_shapes=[pltpu.SemaphoreType.DMA((len(cuts),))],
        compiler_params=pltpu.CompilerParams(vmem_limit_bytes=2 * mib),
        cost_estimate=small,
        name="cut",
    )(whole)


def after(array, *others):
    return lax.optimization_barrier((array, *others))[0]


def shards(blks, owners, grad_codes, scale_exps, val_grads, fisher):
    chips = blks // cores
    chips_per_owner = chips // owners
    me = lax.axis_index("dim")
    blk = lax.axis_index("blk")
    chip, core = blk // cores, lax.rem(blk, cores)[None]
    own = val_grads.shape[0]
    count = grad_codes.shape[0]
    fisher = fisher[None, :]
    shape = (chips_per_owner, cores, own, count)

    def shift(panel, by):
        pairs = [
            (z * cores + c, (z + by) % chips * cores + c) for z in range(chips) for c in range(cores)
        ]
        return lax.ppermute(panel, "blk", pairs)

    def swap(parts):
        pairs = [(b, b ^ 1) for b in range(blks)]
        return [lax.ppermute(part, "blk", pairs) for part in parts]

    def collect(scores, part, by, start):
        keep, send = part
        received = []
        for step in range(1, owners):
            pairs = []
            for b in range(blks):
                owner = (b // cores - by) % chips // chips_per_owner
                pairs.append((b * owners + (owner + step) % owners, b * owners + owner))
            received.append(lax.ppermute(send, ("blk", "dim"), pairs))
        source = lax.rem(chip - by + chips, chips)
        mine = (source // chips_per_owner == me).astype(jnp.int32)[None]
        return place(scores, shape, mine, lax.rem(source, chips_per_owner)[None], keep, received, start)

    ups = chips // 2
    cuts = [0, own * 3 // 4, own]
    held = {0: val_grads}
    for by in range(1, chips - ups):
        held[by] = shift(held[by - 1], 1)
        held[-by] = shift(held[1 - by], -1)
    if ups - 1 not in held:
        held[ups - 1] = shift(held[ups - 2], 1)
    train = dequantize(grad_codes, scale_exps)
    part = multiply(core, val_grads, swap([val_grads]), fisher, train)
    pending = [(part, 0, 0)]
    scores = None
    order = [by for by in held if by != 0] + [ups] * (len(cuts) - 1)
    lows = [0] * (len(held) - 1) + cuts[:-1]
    halves = [(0, own // 2), (own // 2, own)]
    for by, lo in zip(order, lows):
        panel = held[by] if by != ups else last[cuts.index(lo)]
        panel = after(panel, part) if scores is None else after(panel, part, scores)
        if by == ups - 1:
            *parts, low_part, high_part = cut(panel, halves + list(zip(cuts, cuts[1:])))
            last = [shift(low_part, 1), shift(high_part, 1)]
        elif by == ups and lo > 0:
            parts = [panel]
        else:
            half = max(panel.shape[0] // 32 * 16, 16)
            parts = cut(panel, [(0, half), (half, panel.shape[0])])
        part = multiply(core, panel, swap(parts), fisher, train)
        scores = collect(scores, *pending.pop())
        pending.append((part, by, lo))
    scores = collect(scores, *pending.pop())
    return scores.reshape(chips_per_owner * cores * own, count)


def solution(mesh):
    in_specs = (
        P(("groups", "blk"), "dim"),
        P(("groups", "blk"), "dim"),
        P(("groups", "blk"), "dim"),
        P("dim"),
    )
    out_specs = P("dim", ("groups", "blk"))
    body = functools.partial(shards, mesh.shape["blk"], mesh.shape["dim"])
    return jax.shard_map(body, mesh=mesh, in_specs=in_specs, out_specs=out_specs, check_vma=False)
```

```python
import functools

import jax
import jax.numpy as jnp
from jax import lax
from jax.experimental import pallas as pl
from jax.experimental.pallas import tpu as pltpu
from jax.sharding import PartitionSpec as P

damping = 0.05
lanes = 128
cores = 2
mib = 1 << 20
in_vmem = pl.BlockSpec(memory_space=pltpu.VMEM)
in_smem = pl.BlockSpec(memory_space=pltpu.SMEM)
anywhere = pl.BlockSpec(memory_space=pl.ANY)
small = pl.CostEstimate(flops=1, bytes_accessed=1, transcendentals=0)


def dequantize_kernel(codes_ref, exps_ref, train_ref):
    exps = exps_ref[...]
    up = jnp.left_shift(1, jnp.maximum(exps, 0)).astype(jnp.float32)
    down = jnp.left_shift(1, jnp.maximum(-exps, 0)).astype(jnp.float32)
    factor = up / down
    for block in range(exps.shape[1]):
        cols = slice(block * lanes, (block + 1) * lanes)
        codes = codes_ref[:, cols].astype(jnp.float32)
        train_ref[:, cols] = (codes * factor[:, block:block + 1]).astype(jnp.bfloat16)


def dequantize(codes, exps):
    count, width = codes.shape
    rows = min(count, 256)
    return pl.pallas_call(
        dequantize_kernel,
        grid=(count // rows,),
        in_specs=[
            pl.BlockSpec((rows, width), lambda i: (i, 0)),
            pl.BlockSpec((rows, width // lanes), lambda i: (i, 0)),
        ],
        out_specs=pl.BlockSpec((rows, width), lambda i: (i, 0)),
        out_shape=jax.ShapeDtypeStruct((count, width), jnp.bfloat16),
        compiler_params=pltpu.CompilerParams(vmem_limit_bytes=32 * mib),
        cost_estimate=small,
        name="dequantize",
    )(codes, exps)


def multiply_kernel(core_ref, *refs):
    mine_ref, *parts = refs[:-12]
    fisher_ref, train_ref, keep_ref, send_ref = refs[-12:-8]
    left, keep, send, held, in_sems, keep_sems, send_sems, train_sems = refs[-8:]
    rows, width = mine_ref.shape
    count = train_ref.shape[0]
    slots, tile, _ = held.shape
    tiles = count // tile
    half = tile // 2
    depth = min(width, 1024)
    core = core_ref[0]

    def fetches(i):
        slot = lax.rem(i, slots)
        return [
            pltpu.make_async_copy(
                train_ref.at[pl.ds(pl.multiple_of(i * tile, tile) + part * half, half)],
                held.at[slot, pl.ds(part * half, half)],
                train_sems.at[slot, part],
            )
            for part in range(2)
        ]

    mine_spot = pl.ds(pl.multiple_of(core * rows, rows), rows)
    loads = [pltpu.make_async_copy(mine_ref, left.at[mine_spot], in_sems.at[0])]
    offset = 0
    for index, ref in enumerate(parts):
        spot = pl.ds(pl.multiple_of((1 - core) * rows, rows) + offset, ref.shape[0])
        loads.append(pltpu.make_async_copy(ref, left.at[spot], in_sems.at[index + 1]))
        offset += ref.shape[0]
    for load in loads:
        load.start()
    for i in range(min(slots, tiles)):
        for fetch in fetches(i):
            fetch.start()
    for load in loads:
        load.wait()

    @pl.loop(0, width // depth)
    def _(k):
        cols = pl.ds(pl.multiple_of(k * depth, depth), depth)
        scale = 1.0 / (fisher_ref[:, cols] + damping)
        left[:, cols] = (left[:, cols].astype(jnp.float32) * scale).astype(jnp.bfloat16)

    def stores(i):
        cols = pl.ds(pl.multiple_of(i * tile, tile), tile)
        return (
            pltpu.make_async_copy(keep.at[:, cols], keep_ref.at[:, cols], keep_sems.at[i]),
            pltpu.make_async_copy(send.at[:, cols], send_ref.at[:, cols], send_sems.at[i]),
        )

    @pl.loop(0, tiles)
    def _(i):
        cols = pl.ds(pl.multiple_of(i * tile, tile), tile)
        for fetch in fetches(i):
            fetch.wait()
        sums = lax.dot_general(
            left[...], held[lax.rem(i, slots)], (((1,), (1,)), ((), ())),
            preferred_element_type=jnp.float32,
        )
        keep[:, cols] = sums
        send[:, cols] = sums.astype(jnp.bfloat16)
        for store in stores(i):
            store.start()

        @pl.when(i + slots < tiles)
        def _():
            for fetch in fetches(i + slots):
                fetch.start()

    @pl.loop(0, tiles)
    def _(i):
        for store in stores(i):
            store.wait()


def multiply(core, mine, parts, fisher, train):
    rows, width = mine.shape
    count = train.shape[0]
    tile = min(count, 256)
    shape = (cores * rows, count)
    return pl.pallas_call(
        multiply_kernel,
        in_specs=[in_smem] + [anywhere] * (1 + len(parts)) + [in_vmem, anywhere],
        out_specs=[anywhere] * 2,
        out_shape=[
            jax.ShapeDtypeStruct(shape, jnp.float32), jax.ShapeDtypeStruct(shape, jnp.bfloat16),
        ],
        scratch_shapes=[
            pltpu.VMEM((cores * rows, width), jnp.bfloat16),
            pltpu.VMEM(shape, jnp.float32),
            pltpu.VMEM(shape, jnp.bfloat16),
            pltpu.VMEM((4, tile, width), jnp.bfloat16),
            pltpu.SemaphoreType.DMA((1 + len(parts),)),
            pltpu.SemaphoreType.DMA((count // tile,)),
            pltpu.SemaphoreType.DMA((count // tile,)),
            pltpu.SemaphoreType.DMA((4, 2)),
        ],
        compiler_params=pltpu.CompilerParams(vmem_limit_bytes=32 * mib),
        cost_estimate=small,
        name="multiply",
    )(core, mine, *parts, fisher, train)


def place_kernel(start, parts, mine_ref, spot_ref, *refs):
    keep_ref, received = refs[0], refs[1:1 + parts]
    scores_ref, total, terms, in_sems, out_sems = refs[-5:]
    rows = keep_ref.shape[0] // cores

    @pl.when(mine_ref[0] == 1)
    def _():
        loads = [pltpu.make_async_copy(keep_ref, total, in_sems.at[0])]
        for index, ref in enumerate(received):
            loads.append(pltpu.make_async_copy(ref, terms.at[index], in_sems.at[index + 1]))
        for load in loads:
            load.start()
        for load in loads:
            load.wait()
        for index in range(parts):
            total[...] += terms[index].astype(jnp.float32)
        copies = [
            pltpu.make_async_copy(
                total.at[pl.ds(c * rows, rows)],
                scores_ref.at[spot_ref[0], c, pl.ds(start, rows)],
                out_sems.at[c],
            )
            for c in range(cores)
        ]
        for copy in copies:
            copy.start()
        for copy in copies:
            copy.wait()


def place(scores, shape, mine, spot, keep, received, start):
    given = [] if scores is None else [scores]
    parts = len(received)
    return pl.pallas_call(
        functools.partial(place_kernel, start, parts),
        in_specs=[in_smem] * 2 + [anywhere] * (1 + parts + len(given)),
        out_specs=anywhere,
        out_shape=jax.ShapeDtypeStruct(shape, jnp.float32),
        scratch_shapes=[
            pltpu.VMEM(keep.shape, jnp.float32),
            pltpu.VMEM((parts, *keep.shape), jnp.bfloat16),
            pltpu.SemaphoreType.DMA((1 + parts,)),
            pltpu.SemaphoreType.DMA((cores,)),
        ],
        input_output_aliases={3 + parts: 0} if given else {},
        compiler_params=pltpu.CompilerParams(vmem_limit_bytes=12 * mib),
        cost_estimate=small,
        name="place",
    )(mine, spot, keep, *received, *given)


def cut(whole, cuts):
    return [whole[low:high] for low, high in cuts]


def after(array, *others):
    return lax.optimization_barrier((array, *others))[0]


def shards(blks, owners, grad_codes, scale_exps, val_grads, fisher):
    chips = blks // cores
    chips_per_owner = chips // owners
    me = lax.axis_index("dim")
    blk = lax.axis_index("blk")
    chip, core = blk // cores, lax.rem(blk, cores)[None]
    own = val_grads.shape[0]
    count = grad_codes.shape[0]
    fisher = fisher[None, :]
    shape = (chips_per_owner, cores, own, count)

    def shift(panel, by):
        pairs = [
            (z * cores + c, (z + by) % chips * cores + c) for z in range(chips) for c in range(cores)
        ]
        return lax.ppermute(panel, "blk", pairs)

    def swap(parts):
        pairs = [(b, b ^ 1) for b in range(blks)]
        return [lax.ppermute(part, "blk", pairs) for part in parts]

    def collect(scores, part, by, start):
        keep, send = part
        received = []
        for step in range(1, owners):
            pairs = []
            for b in range(blks):
                owner = (b // cores - by) % chips // chips_per_owner
                pairs.append((b * owners + (owner + step) % owners, b * owners + owner))
            received.append(lax.ppermute(send, ("blk", "dim"), pairs))
        source = lax.rem(chip - by + chips, chips)
        mine = (source // chips_per_owner == me).astype(jnp.int32)[None]
        return place(scores, shape, mine, lax.rem(source, chips_per_owner)[None], keep, received, start)

    ups = chips // 2
    cuts = [0, own * 3 // 4, own]
    held = {0: val_grads}
    for by in range(1, chips - ups):
        held[by] = shift(held[by - 1], 1)
        held[-by] = shift(held[1 - by], -1)
    if ups - 1 not in held:
        held[ups - 1] = shift(held[ups - 2], 1)
    train = dequantize(grad_codes, scale_exps)
    part = multiply(core, val_grads, swap([val_grads]), fisher, train)
    pending = [(part, 0, 0)]
    scores = None
    order = [by for by in held if by != 0] + [ups] * (len(cuts) - 1)
    lows = [0] * (len(held) - 1) + cuts[:-1]
    halves = [(0, own // 2), (own // 2, own)]
    for by, lo in zip(order, lows):
        panel = held[by] if by != ups else last[cuts.index(lo)]
        panel = after(panel, part) if scores is None else after(panel, part, scores)
        if by == ups - 1:
            *parts, low_part, high_part = cut(panel, halves + list(zip(cuts, cuts[1:])))
            last = [shift(low_part, 1), shift(high_part, 1)]
        elif by == ups and lo > 0:
            parts = [panel]
        else:
            half = max(panel.shape[0] // 32 * 16, 16)
            parts = cut(panel, [(0, half), (half, panel.shape[0])])
        part = multiply(core, panel, swap(parts), fisher, train)
        scores = collect(scores, *pending.pop())
        pending.append((part, by, lo))
    scores = collect(scores, *pending.pop())
    return scores.reshape(chips_per_owner * cores * own, count)


def solution(mesh):
    in_specs = (
        P(("groups", "blk"), "dim"),
        P(("groups", "blk"), "dim"),
        P(("groups", "blk"), "dim"),
        P("dim"),
    )
    out_specs = P("dim", ("groups", "blk"))
    body = functools.partial(shards, mesh.shape["blk"], mesh.shape["dim"])
    return jax.shard_map(body, mesh=mesh, in_specs=in_specs, out_specs=out_specs, check_vma=False)
```

```python
import functools

import jax
import jax.numpy as jnp
from jax import lax
from jax.experimental import pallas as pl
from jax.experimental.pallas import tpu as pltpu
from jax.sharding import PartitionSpec as P

damping = 0.05
lanes = 128
cores = 2
mib = 1 << 20
in_vmem = pl.BlockSpec(memory_space=pltpu.VMEM)
in_smem = pl.BlockSpec(memory_space=pltpu.SMEM)
anywhere = pl.BlockSpec(memory_space=pl.ANY)
small = pl.CostEstimate(flops=1, bytes_accessed=1, transcendentals=0)


def dequantize_kernel(codes_ref, exps_ref, train_ref):
    exps = exps_ref[...]
    up = jnp.left_shift(1, jnp.maximum(exps, 0)).astype(jnp.float32)
    down = jnp.left_shift(1, jnp.maximum(-exps, 0)).astype(jnp.float32)
    factor = up / down
    for block in range(exps.shape[1]):
        cols = slice(block * lanes, (block + 1) * lanes)
        codes = codes_ref[:, cols].astype(jnp.float32)
        train_ref[:, cols] = (codes * factor[:, block:block + 1]).astype(jnp.bfloat16)


def dequantize(codes, exps):
    count, width = codes.shape
    rows = min(count, 256)
    return pl.pallas_call(
        dequantize_kernel,
        grid=(count // rows,),
        in_specs=[
            pl.BlockSpec((rows, width), lambda i: (i, 0)),
            pl.BlockSpec((rows, width // lanes), lambda i: (i, 0)),
        ],
        out_specs=pl.BlockSpec((rows, width), lambda i: (i, 0)),
        out_shape=jax.ShapeDtypeStruct((count, width), jnp.bfloat16),
        compiler_params=pltpu.CompilerParams(vmem_limit_bytes=32 * mib),
        cost_estimate=small,
        name="dequantize",
    )(codes, exps)


def multiply_kernel(core_ref, *refs):
    mine_ref, *parts = refs[:-12]
    fisher_ref, train_ref, keep_ref, send_ref = refs[-12:-8]
    left, keep, send, held, in_sems, keep_sems, send_sems, train_sems = refs[-8:]
    rows, width = mine_ref.shape
    count = train_ref.shape[0]
    slots, tile, _ = held.shape
    tiles = count // tile
    half = tile // 2
    depth = min(width, 1024)
    core = core_ref[0]

    def fetches(i):
        slot = lax.rem(i, slots)
        return [
            pltpu.make_async_copy(
                train_ref.at[pl.ds(pl.multiple_of(i * tile, tile) + part * half, half)],
                held.at[slot, pl.ds(part * half, half)],
                train_sems.at[slot, part],
            )
            for part in range(2)
        ]

    mine_spot = pl.ds(pl.multiple_of(core * rows, rows), rows)
    loads = [pltpu.make_async_copy(mine_ref, left.at[mine_spot], in_sems.at[0])]
    offset = 0
    for index, ref in enumerate(parts):
        spot = pl.ds(pl.multiple_of((1 - core) * rows, rows) + offset, ref.shape[0])
        loads.append(pltpu.make_async_copy(ref, left.at[spot], in_sems.at[index + 1]))
        offset += ref.shape[0]
    for load in loads:
        load.start()
    for i in range(min(slots, tiles)):
        for fetch in fetches(i):
            fetch.start()
    for load in loads:
        load.wait()

    @pl.loop(0, width // depth)
    def _(k):
        cols = pl.ds(pl.multiple_of(k * depth, depth), depth)
        scale = 1.0 / (fisher_ref[:, cols] + damping)
        left[:, cols] = (left[:, cols].astype(jnp.float32) * scale).astype(jnp.bfloat16)

    def stores(i):
        cols = pl.ds(pl.multiple_of(i * tile, tile), tile)
        return (
            pltpu.make_async_copy(keep.at[:, cols], keep_ref.at[:, cols], keep_sems.at[i]),
            pltpu.make_async_copy(send.at[:, cols], send_ref.at[:, cols], send_sems.at[i]),
        )

    @pl.loop(0, tiles)
    def _(i):
        cols = pl.ds(pl.multiple_of(i * tile, tile), tile)
        for fetch in fetches(i):
            fetch.wait()
        sums = lax.dot_general(
            left[...], held[lax.rem(i, slots)], (((1,), (1,)), ((), ())),
            preferred_element_type=jnp.float32,
        )
        keep[:, cols] = sums
        send[:, cols] = sums.astype(jnp.bfloat16)
        for store in stores(i):
            store.start()

        @pl.when(i + slots < tiles)
        def _():
            for fetch in fetches(i + slots):
                fetch.start()

    @pl.loop(0, tiles)
    def _(i):
        for store in stores(i):
            store.wait()


def multiply(core, mine, parts, fisher, train):
    rows, width = mine.shape
    count = train.shape[0]
    tile = min(count, 256)
    shape = (cores * rows, count)
    return pl.pallas_call(
        multiply_kernel,
        in_specs=[in_smem] + [anywhere] * (1 + len(parts)) + [in_vmem, anywhere],
        out_specs=[anywhere] * 2,
        out_shape=[
            jax.ShapeDtypeStruct(shape, jnp.float32), jax.ShapeDtypeStruct(shape, jnp.bfloat16),
        ],
        scratch_shapes=[
            pltpu.VMEM((cores * rows, width), jnp.bfloat16),
            pltpu.VMEM(shape, jnp.float32),
            pltpu.VMEM(shape, jnp.bfloat16),
            pltpu.VMEM((4, tile, width), jnp.bfloat16),
            pltpu.SemaphoreType.DMA((1 + len(parts),)),
            pltpu.SemaphoreType.DMA((count // tile,)),
            pltpu.SemaphoreType.DMA((count // tile,)),
            pltpu.SemaphoreType.DMA((4, 2)),
        ],
        compiler_params=pltpu.CompilerParams(vmem_limit_bytes=32 * mib),
        cost_estimate=small,
        name="multiply",
    )(core, mine, *parts, fisher, train)


def place_kernel(start, parts, mine_ref, spot_ref, *refs):
    keep_ref, received = refs[0], refs[1:1 + parts]
    scores_ref, total, terms, in_sems, out_sems = refs[-5:]
    rows = keep_ref.shape[0] // cores

    @pl.when(mine_ref[0] == 1)
    def _():
        loads = [pltpu.make_async_copy(keep_ref, total, in_sems.at[0])]
        for index, ref in enumerate(received):
            loads.append(pltpu.make_async_copy(ref, terms.at[index], in_sems.at[index + 1]))
        for load in loads:
            load.start()
        for load in loads:
            load.wait()
        for index in range(parts):
            total[...] += terms[index].astype(jnp.float32)
        copies = [
            pltpu.make_async_copy(
                total.at[pl.ds(c * rows, rows)],
                scores_ref.at[spot_ref[0], c, pl.ds(start, rows)],
                out_sems.at[c],
            )
            for c in range(cores)
        ]
        for copy in copies:
            copy.start()
        for copy in copies:
            copy.wait()


def place(scores, shape, mine, spot, keep, received, start):
    given = [] if scores is None else [scores]
    parts = len(received)
    return pl.pallas_call(
        functools.partial(place_kernel, start, parts),
        in_specs=[in_smem] * 2 + [anywhere] * (1 + parts + len(given)),
        out_specs=anywhere,
        out_shape=jax.ShapeDtypeStruct(shape, jnp.float32),
        scratch_shapes=[
            pltpu.VMEM(keep.shape, jnp.float32),
            pltpu.VMEM((parts, *keep.shape), jnp.bfloat16),
            pltpu.SemaphoreType.DMA((1 + parts,)),
            pltpu.SemaphoreType.DMA((cores,)),
        ],
        input_output_aliases={3 + parts: 0} if given else {},
        compiler_params=pltpu.CompilerParams(vmem_limit_bytes=12 * mib),
        cost_estimate=small,
        name="place",
    )(mine, spot, keep, *received, *given)


def cut(whole, cuts):
    return [whole[low:high] for low, high in cuts]


def after(array, *others):
    return lax.optimization_barrier((array, *others))[0]


def shards(blks, owners, grad_codes, scale_exps, val_grads, fisher):
    chips = blks // cores
    chips_per_owner = chips // owners
    me = lax.axis_index("dim")
    blk = lax.axis_index("blk")
    chip, core = blk // cores, lax.rem(blk, cores)[None]
    own = val_grads.shape[0]
    count = grad_codes.shape[0]
    fisher = fisher[None, :]
    shape = (chips_per_owner, cores, own, count)

    def shift(panel, by):
        pairs = [
            (z * cores + c, (z + by) % chips * cores + c) for z in range(chips) for c in range(cores)
        ]
        return lax.ppermute(panel, "blk", pairs)

    def swap(parts):
        pairs = [(b, b ^ 1) for b in range(blks)]
        return [lax.ppermute(part, "blk", pairs) for part in parts]

    def collect(scores, part, by, start):
        keep, send = part
        received = []
        for step in range(1, owners):
            pairs = []
            for b in range(blks):
                owner = (b // cores - by) % chips // chips_per_owner
                pairs.append((b * owners + (owner + step) % owners, b * owners + owner))
            received.append(lax.ppermute(send, ("blk", "dim"), pairs))
        source = lax.rem(chip - by + chips, chips)
        mine = (source // chips_per_owner == me).astype(jnp.int32)[None]
        return place(scores, shape, mine, lax.rem(source, chips_per_owner)[None], keep, received, start)

    ups = chips // 2
    order = list(range(1, ups + 1)) + list(range(-1, ups - chips, -1))
    pieces = [(0, own * 3 // 4), (own * 3 // 4, own)]
    halves = [(0, own // 2), (own // 2, own)]

    arriving = shift(val_grads, 1)
    beside = swap([val_grads])
    train = dequantize(grad_codes, scale_exps)
    scores, part, pending = None, train, []
    for index, by in enumerate(order[:-1]):
        panel = after(arriving, part, *([] if scores is None else [scores]))
        if index == 0:
            part = multiply(core, after(val_grads, panel), beside, fisher, train)
            pending.append((part, 0, 0))
        following = order[index + 1]
        source = panel if abs(following) > 1 else val_grads
        parts = swap(cut(panel, halves))
        if index + 2 < len(order):
            arriving = shift(source, 1 if following > 0 else -1)
        done = part
        part = multiply(core, after(panel, part), parts, fisher, train)
        if index + 2 == len(order):
            arriving = [shift(after(piece, done), 1 if following > 0 else -1) for piece in cut(source, pieces)]
        scores = collect(scores, *pending.pop())
        pending.append((part, by, 0))
    by = order[-1]
    for (low, high), panel in zip(pieces, arriving):
        panel = after(panel, part, scores)
        half = max((high - low) // 32 * 16, 16)
        parts = [panel] if low > 0 else cut(panel, [(0, half), (half, high - low)])
        part = multiply(core, panel, swap(parts), fisher, train)
        scores = collect(scores, *pending.pop())
        pending.append((part, by, low))
    scores = collect(scores, *pending.pop())
    return scores.reshape(chips_per_owner * cores * own, count)


def solution(mesh):
    in_specs = (
        P(("groups", "blk"), "dim"),
        P(("groups", "blk"), "dim"),
        P(("groups", "blk"), "dim"),
        P("dim"),
    )
    out_specs = P("dim", ("groups", "blk"))
    body = functools.partial(shards, mesh.shape["blk"], mesh.shape["dim"])
    return jax.shard_map(body, mesh=mesh, in_specs=in_specs, out_specs=out_specs, check_vma=False)
```

```python
import functools

import jax
import jax.numpy as jnp
from jax import lax
from jax.experimental import pallas as pl
from jax.experimental.pallas import tpu as pltpu
from jax.sharding import PartitionSpec as P

damping = 0.05
lanes = 128
cores = 2
mib = 1 << 20
in_vmem = pl.BlockSpec(memory_space=pltpu.VMEM)
in_smem = pl.BlockSpec(memory_space=pltpu.SMEM)
anywhere = pl.BlockSpec(memory_space=pl.ANY)
small = pl.CostEstimate(flops=1, bytes_accessed=1, transcendentals=0)


def first_kernel(core_ref, mine_ref, other_ref, fisher_ref, codes_ref, exps_ref, train_ref, keep_ref,
                 send_ref, left, spread):
    rows, width = mine_ref.shape
    depth = min(width, 1024)
    core = core_ref[0]

    @pl.when(pl.program_id(0) == 0)
    def _():
        block = lax.broadcasted_iota(jnp.int32, spread.shape, 0)
        col = lax.broadcasted_iota(jnp.int32, spread.shape, 1)
        spread[...] = jnp.where(col // lanes == block, 1.0, 0.0).astype(jnp.bfloat16)
        for ref, place in ((mine_ref, core), (other_ref, 1 - core)):
            spot = pl.ds(pl.multiple_of(place * rows, rows), rows)
            for start in range(0, width, depth):
                cols = slice(start, start + depth)
                scale = 1.0 / (fisher_ref[:, cols] + damping)
                left[spot, cols] = (ref[:, cols].astype(jnp.float32) * scale).astype(jnp.bfloat16)

    exps = exps_ref[...]
    up = jnp.left_shift(1, jnp.maximum(exps, 0)).astype(jnp.float32)
    down = jnp.left_shift(1, jnp.maximum(-exps, 0)).astype(jnp.float32)
    factor = (up / down).astype(jnp.bfloat16)
    for start in range(0, width, depth):
        cols = slice(start, start + depth)
        wide = jnp.dot(factor, spread[:, cols], preferred_element_type=jnp.float32)
        train_ref[:, cols] = codes_ref[:, cols] * wide.astype(jnp.bfloat16)
    sums = lax.dot_general(
        left[...], train_ref[...], (((1,), (1,)), ((), ())), preferred_element_type=jnp.float32
    )
    keep_ref[...] = sums
    send_ref[...] = sums.astype(jnp.bfloat16)


def first(core, mine, other, fisher, codes, exps):
    rows, width = mine.shape
    count = codes.shape[0]
    blocks = width // lanes
    tile = min(count, 256)
    shape = (cores * rows, count)
    return pl.pallas_call(
        first_kernel,
        grid=(count // tile,),
        in_specs=[
            in_smem,
            pl.BlockSpec((rows, width), lambda i: (0, 0)),
            pl.BlockSpec((rows, width), lambda i: (0, 0)),
            pl.BlockSpec((1, width), lambda i: (0, 0)),
            pl.BlockSpec((tile, width), lambda i: (i, 0)),
            pl.BlockSpec((tile, blocks), lambda i: (i, 0)),
        ],
        out_specs=[
            pl.BlockSpec((tile, width), lambda i: (i, 0)),
            pl.BlockSpec((cores * rows, tile), lambda i: (0, i)),
            pl.BlockSpec((cores * rows, tile), lambda i: (0, i)),
        ],
        out_shape=[
            jax.ShapeDtypeStruct((count, width), jnp.bfloat16),
            jax.ShapeDtypeStruct(shape, jnp.float32),
            jax.ShapeDtypeStruct(shape, jnp.bfloat16),
        ],
        scratch_shapes=[
            pltpu.VMEM((cores * rows, width), jnp.bfloat16),
            pltpu.VMEM((blocks, width), jnp.bfloat16),
        ],
        compiler_params=pltpu.CompilerParams(vmem_limit_bytes=40 * mib),
        cost_estimate=small,
        name="first",
    )(core, mine, other, fisher, codes, exps)


def multiply_kernel(core_ref, *refs):
    mine_ref, *parts = refs[:-12]
    fisher_ref, train_ref, keep_ref, send_ref = refs[-12:-8]
    left, keep, send, held, in_sems, keep_sems, send_sems, train_sems = refs[-8:]
    rows, width = mine_ref.shape
    count = train_ref.shape[0]
    slots, tile, _ = held.shape
    tiles = count // tile
    half = tile // 2
    depth = min(width, 1024)
    core = core_ref[0]

    def fetches(i):
        slot = lax.rem(i, slots)
        return [
            pltpu.make_async_copy(
                train_ref.at[pl.ds(pl.multiple_of(i * tile, tile) + part * half, half)],
                held.at[slot, pl.ds(part * half, half)],
                train_sems.at[slot, part],
            )
            for part in range(2)
        ]

    mine_spot = pl.ds(pl.multiple_of(core * rows, rows), rows)
    loads = [pltpu.make_async_copy(mine_ref, left.at[mine_spot], in_sems.at[0])]
    offset = 0
    for index, ref in enumerate(parts):
        spot = pl.ds(pl.multiple_of((1 - core) * rows, rows) + offset, ref.shape[0])
        loads.append(pltpu.make_async_copy(ref, left.at[spot], in_sems.at[index + 1]))
        offset += ref.shape[0]
    for load in loads:
        load.start()
    for i in range(min(slots, tiles)):
        for fetch in fetches(i):
            fetch.start()
    for load in loads:
        load.wait()

    @pl.loop(0, width // depth)
    def _(k):
        cols = pl.ds(pl.multiple_of(k * depth, depth), depth)
        scale = 1.0 / (fisher_ref[:, cols] + damping)
        left[:, cols] = (left[:, cols].astype(jnp.float32) * scale).astype(jnp.bfloat16)

    def stores(i):
        cols = pl.ds(pl.multiple_of(i * tile, tile), tile)
        return (
            pltpu.make_async_copy(keep.at[:, cols], keep_ref.at[:, cols], keep_sems.at[i]),
            pltpu.make_async_copy(send.at[:, cols], send_ref.at[:, cols], send_sems.at[i]),
        )

    @pl.loop(0, tiles)
    def _(i):
        cols = pl.ds(pl.multiple_of(i * tile, tile), tile)
        for fetch in fetches(i):
            fetch.wait()
        sums = lax.dot_general(
            left[...], held[lax.rem(i, slots)], (((1,), (1,)), ((), ())),
            preferred_element_type=jnp.float32,
        )
        keep[:, cols] = sums
        send[:, cols] = sums.astype(jnp.bfloat16)
        for store in stores(i):
            store.start()

        @pl.when(i + slots < tiles)
        def _():
            for fetch in fetches(i + slots):
                fetch.start()

    @pl.loop(0, tiles)
    def _(i):
        for store in stores(i):
            store.wait()


def multiply(core, mine, parts, fisher, train):
    rows, width = mine.shape
    count = train.shape[0]
    tile = min(count, 256)
    shape = (cores * rows, count)
    return pl.pallas_call(
        multiply_kernel,
        in_specs=[in_smem] + [anywhere] * (1 + len(parts)) + [in_vmem, anywhere],
        out_specs=[anywhere] * 2,
        out_shape=[
            jax.ShapeDtypeStruct(shape, jnp.float32), jax.ShapeDtypeStruct(shape, jnp.bfloat16),
        ],
        scratch_shapes=[
            pltpu.VMEM((cores * rows, width), jnp.bfloat16),
            pltpu.VMEM(shape, jnp.float32),
            pltpu.VMEM(shape, jnp.bfloat16),
            pltpu.VMEM((4, tile, width), jnp.bfloat16),
            pltpu.SemaphoreType.DMA((1 + len(parts),)),
            pltpu.SemaphoreType.DMA((count // tile,)),
            pltpu.SemaphoreType.DMA((count // tile,)),
            pltpu.SemaphoreType.DMA((4, 2)),
        ],
        compiler_params=pltpu.CompilerParams(vmem_limit_bytes=32 * mib),
        cost_estimate=small,
        name="multiply",
    )(core, mine, *parts, fisher, train)


def place_kernel(start, parts, mine_ref, spot_ref, *refs):
    keep_ref, received = refs[0], refs[1:1 + parts]
    scores_ref, total, terms, in_sems, out_sems = refs[-5:]
    rows = keep_ref.shape[0] // cores

    @pl.when(mine_ref[0] == 1)
    def _():
        loads = [pltpu.make_async_copy(keep_ref, total, in_sems.at[0])]
        for index, ref in enumerate(received):
            loads.append(pltpu.make_async_copy(ref, terms.at[index], in_sems.at[index + 1]))
        for load in loads:
            load.start()
        for load in loads:
            load.wait()
        for index in range(parts):
            total[...] += terms[index].astype(jnp.float32)
        copies = [
            pltpu.make_async_copy(
                total.at[pl.ds(c * rows, rows)],
                scores_ref.at[spot_ref[0], c, pl.ds(start, rows)],
                out_sems.at[c],
            )
            for c in range(cores)
        ]
        for copy in copies:
            copy.start()
        for copy in copies:
            copy.wait()


def place(scores, shape, mine, spot, keep, received, start):
    given = [] if scores is None else [scores]
    parts = len(received)
    return pl.pallas_call(
        functools.partial(place_kernel, start, parts),
        in_specs=[in_smem] * 2 + [anywhere] * (1 + parts + len(given)),
        out_specs=anywhere,
        out_shape=jax.ShapeDtypeStruct(shape, jnp.float32),
        scratch_shapes=[
            pltpu.VMEM(keep.shape, jnp.float32),
            pltpu.VMEM((parts, *keep.shape), jnp.bfloat16),
            pltpu.SemaphoreType.DMA((1 + parts,)),
            pltpu.SemaphoreType.DMA((cores,)),
        ],
        input_output_aliases={3 + parts: 0} if given else {},
        compiler_params=pltpu.CompilerParams(vmem_limit_bytes=12 * mib),
        cost_estimate=small,
        name="place",
    )(mine, spot, keep, *received, *given)


def cut(whole, cuts):
    return [whole[low:high] for low, high in cuts]


def after(array, *others):
    return lax.optimization_barrier((array, *others))[0]


def shards(blks, owners, grad_codes, scale_exps, val_grads, fisher):
    chips = blks // cores
    chips_per_owner = chips // owners
    me = lax.axis_index("dim")
    blk = lax.axis_index("blk")
    chip, core = blk // cores, lax.rem(blk, cores)[None]
    own = val_grads.shape[0]
    count = grad_codes.shape[0]
    fisher = fisher[None, :]
    shape = (chips_per_owner, cores, own, count)

    def shift(panel, by):
        pairs = [
            (z * cores + c, (z + by) % chips * cores + c) for z in range(chips) for c in range(cores)
        ]
        return lax.ppermute(panel, "blk", pairs)

    def swap(parts):
        pairs = [(b, b ^ 1) for b in range(blks)]
        return [lax.ppermute(part, "blk", pairs) for part in parts]

    def collect(scores, part, by, start):
        keep, send = part
        received = []
        for step in range(1, owners):
            pairs = []
            for b in range(blks):
                owner = (b // cores - by) % chips // chips_per_owner
                pairs.append((b * owners + (owner + step) % owners, b * owners + owner))
            received.append(lax.ppermute(send, ("blk", "dim"), pairs))
        source = lax.rem(chip - by + chips, chips)
        mine = (source // chips_per_owner == me).astype(jnp.int32)[None]
        return place(scores, shape, mine, lax.rem(source, chips_per_owner)[None], keep, received, start)

    ups = chips // 2
    order = list(range(1, ups + 1)) + list(range(-1, ups - chips, -1))
    pieces = [(0, own * 3 // 4), (own * 3 // 4, own)]
    halves = [(0, own // 2), (own // 2, own)]

    arriving = shift(val_grads, 1)
    train, *part = first(core, val_grads, *swap([val_grads]), fisher, grad_codes, scale_exps)
    scores, pending = None, [(part, 0, 0)]
    for index, by in enumerate(order[:-1]):
        last = index + 2 == len(order)
        following = 1 if order[index + 1] > 0 else -1
        if last:
            scores = collect(scores, *pending.pop())
        panel = after(arriving, part)
        source = panel if abs(order[index + 1]) > 1 else val_grads
        if last:
            arriving = [shift(after(piece, scores), following) for piece in cut(source, pieces)]
        else:
            arriving = shift(source, following)
        part = multiply(core, panel, swap(cut(panel, halves)), fisher, train)
        if not last:
            scores = collect(scores, *pending.pop())
        pending.append((part, by, 0))
    by = order[-1]
    for (low, high), panel in zip(pieces, arriving):
        panel = after(panel, part, scores)
        half = max((high - low) // 32 * 16, 16)
        parts = [panel] if low > 0 else cut(panel, [(0, half), (half, high - low)])
        part = multiply(core, panel, swap(parts), fisher, train)
        scores = collect(scores, *pending.pop())
        pending.append((part, by, low))
    scores = collect(scores, *pending.pop())
    return scores.reshape(chips_per_owner * cores * own, count)


def solution(mesh):
    in_specs = (
        P(("groups", "blk"), "dim"),
        P(("groups", "blk"), "dim"),
        P(("groups", "blk"), "dim"),
        P("dim"),
    )
    out_specs = P("dim", ("groups", "blk"))
    body = functools.partial(shards, mesh.shape["blk"], mesh.shape["dim"])
    return jax.shard_map(body, mesh=mesh, in_specs=in_specs, out_specs=out_specs, check_vma=False)
```

```python
import functools
import math

import jax
import jax.numpy as jnp
from jax import lax
from jax.experimental import pallas as pl
from jax.experimental.pallas import tpu as pltpu
from jax.sharding import PartitionSpec as P

damping = 0.05
lanes = 128
cores = 2
mib = 1 << 20
in_vmem = pl.BlockSpec(memory_space=pltpu.VMEM)
in_smem = pl.BlockSpec(memory_space=pltpu.SMEM)
anywhere = pl.BlockSpec(memory_space=pl.ANY)
small = pl.CostEstimate(flops=1, bytes_accessed=1, transcendentals=0)


def first_kernel(core_ref, mine_ref, other_ref, fisher_ref, codes_ref, exps_ref, train_ref, keep_ref,
                 send_ref, left, spread):
    rows, width = mine_ref.shape
    depth = min(width, 1024)
    core = core_ref[0]

    @pl.when(pl.program_id(0) == 0)
    def _():
        block = lax.broadcasted_iota(jnp.int32, spread.shape, 0)
        col = lax.broadcasted_iota(jnp.int32, spread.shape, 1)
        spread[...] = jnp.where(col // lanes == block, 1.0, 0.0).astype(jnp.bfloat16)
        for ref, place in ((mine_ref, core), (other_ref, 1 - core)):
            spot = pl.ds(pl.multiple_of(place * rows, rows), rows)
            for start in range(0, width, depth):
                cols = slice(start, start + depth)
                scale = 1.0 / (fisher_ref[:, cols] + damping)
                left[spot, cols] = (ref[:, cols].astype(jnp.float32) * scale).astype(jnp.bfloat16)

    exps = exps_ref[...]
    up = jnp.left_shift(1, jnp.maximum(exps, 0)).astype(jnp.float32)
    down = jnp.left_shift(1, jnp.maximum(-exps, 0)).astype(jnp.float32)
    factor = (up / down).astype(jnp.bfloat16)
    for start in range(0, width, depth):
        cols = slice(start, start + depth)
        wide = jnp.dot(factor, spread[:, cols], preferred_element_type=jnp.float32)
        train_ref[:, cols] = codes_ref[:, cols] * wide.astype(jnp.bfloat16)
    sums = lax.dot_general(
        left[...], train_ref[...], (((1,), (1,)), ((), ())), preferred_element_type=jnp.float32
    )
    keep_ref[...] = sums
    send_ref[...] = sums.astype(jnp.bfloat16)


def first(core, mine, other, fisher, codes, exps):
    rows, width = mine.shape
    count = codes.shape[0]
    blocks = width // lanes
    tile = min(count, 256)
    shape = (cores * rows, count)
    return pl.pallas_call(
        first_kernel,
        grid=(count // tile,),
        in_specs=[
            in_smem,
            pl.BlockSpec((rows, width), lambda i: (0, 0)),
            pl.BlockSpec((rows, width), lambda i: (0, 0)),
            pl.BlockSpec((1, width), lambda i: (0, 0)),
            pl.BlockSpec((tile, width), lambda i: (i, 0)),
            pl.BlockSpec((tile, blocks), lambda i: (i, 0)),
        ],
        out_specs=[
            pl.BlockSpec((tile, width), lambda i: (i, 0)),
            pl.BlockSpec((cores * rows, tile), lambda i: (0, i)),
            pl.BlockSpec((cores * rows, tile), lambda i: (0, i)),
        ],
        out_shape=[
            jax.ShapeDtypeStruct((count, width), jnp.bfloat16),
            jax.ShapeDtypeStruct(shape, jnp.float32),
            jax.ShapeDtypeStruct(shape, jnp.bfloat16),
        ],
        scratch_shapes=[
            pltpu.VMEM((cores * rows, width), jnp.bfloat16),
            pltpu.VMEM((blocks, width), jnp.bfloat16),
        ],
        compiler_params=pltpu.CompilerParams(vmem_limit_bytes=40 * mib),
        cost_estimate=small,
        name="first",
    )(core, mine, other, fisher, codes, exps)


def multiply_kernel(counts, low, core_ref, *refs):
    refs = list(refs)
    mine_refs, other_refs, given = [[refs.pop(0) for _ in range(size)] for size in counts]
    fisher_ref, train_ref, keep_ref, send_ref = refs[:4]
    left, held, keep, send, in_sems, train_sems, keep_sems, send_sems = refs[4:]
    rows = sum(ref.shape[0] for ref in mine_refs)
    slots, tile, width = held.shape
    tiles = train_ref.shape[0] // tile
    half = tile // 2
    depth = math.gcd(width, 1024)
    core = core_ref[0]

    def fetches(i):
        slot = lax.rem(i, slots)
        return [
            pltpu.make_async_copy(
                train_ref.at[
                    pl.ds(pl.multiple_of(i * tile, tile) + part * half, half), pl.ds(low, width)
                ],
                held.at[slot, pl.ds(part * half, half)],
                train_sems.at[slot, part],
            )
            for part in range(2)
        ]

    loads = []
    for group, place in ((mine_refs, core), (other_refs, 1 - core)):
        offset = 0
        for ref in group:
            spot = pl.ds(pl.multiple_of(place * rows, rows) + offset, ref.shape[0])
            loads.append(pltpu.make_async_copy(ref, left.at[spot], in_sems.at[len(loads)]))
            offset += ref.shape[0]
    for ref in given:
        loads.append(pltpu.make_async_copy(ref, keep, in_sems.at[len(loads)]))
    for load in loads:
        load.start()
    for i in range(min(slots, tiles)):
        for fetch in fetches(i):
            fetch.start()
    for load in loads:
        load.wait()

    @pl.loop(0, width // depth)
    def _(k):
        cols = pl.ds(pl.multiple_of(k * depth, depth), depth)
        scale = 1.0 / (fisher_ref[:, cols] + damping)
        left[:, cols] = (left[:, cols].astype(jnp.float32) * scale).astype(jnp.bfloat16)

    def stores(i):
        cols = pl.ds(pl.multiple_of(i * tile, tile), tile)
        return (
            pltpu.make_async_copy(keep.at[:, cols], keep_ref.at[:, cols], keep_sems.at[i]),
            pltpu.make_async_copy(send.at[:, cols], send_ref.at[:, cols], send_sems.at[i]),
        )

    @pl.loop(0, tiles)
    def _(i):
        cols = pl.ds(pl.multiple_of(i * tile, tile), tile)
        for fetch in fetches(i):
            fetch.wait()
        sums = lax.dot_general(
            left[...], held[lax.rem(i, slots)], (((1,), (1,)), ((), ())),
            preferred_element_type=jnp.float32,
        )
        if given:
            sums += keep[:, cols]
        keep[:, cols] = sums
        send[:, cols] = sums.astype(jnp.bfloat16)
        for store in stores(i):
            store.start()

        @pl.when(i + slots < tiles)
        def _():
            for fetch in fetches(i + slots):
                fetch.start()

    @pl.loop(0, tiles)
    def _(i):
        for store in stores(i):
            store.wait()


def multiply(core, mine, other, fisher, train, low=0, given=()):
    rows = sum(part.shape[0] for part in mine)
    width = mine[0].shape[1]
    count = train.shape[0]
    tile = min(count, 256)
    slots = 4
    shape = (cores * rows, count)
    counts = (len(mine), len(other), len(given))
    return pl.pallas_call(
        functools.partial(multiply_kernel, counts, low),
        in_specs=[in_smem] + [anywhere] * sum(counts) + [in_vmem, anywhere],
        out_specs=[anywhere] * 2,
        out_shape=[
            jax.ShapeDtypeStruct(shape, jnp.float32), jax.ShapeDtypeStruct(shape, jnp.bfloat16),
        ],
        scratch_shapes=[
            pltpu.VMEM((cores * rows, width), jnp.bfloat16),
            pltpu.VMEM((slots, tile, width), jnp.bfloat16),
            pltpu.VMEM(shape, jnp.float32),
            pltpu.VMEM(shape, jnp.bfloat16),
            pltpu.SemaphoreType.DMA((sum(counts),)),
            pltpu.SemaphoreType.DMA((slots, 2)),
            pltpu.SemaphoreType.DMA((count // tile,)),
            pltpu.SemaphoreType.DMA((count // tile,)),
        ],
        compiler_params=pltpu.CompilerParams(vmem_limit_bytes=32 * mib),
        cost_estimate=small,
        name="multiply",
    )(core, *mine, *other, *given, fisher[:, low:low + width], train)


def place_kernel(start, parts, mine_ref, spot_ref, *refs):
    keep_ref, received = refs[0], refs[1:1 + parts]
    scores_ref, total, terms, in_sems, out_sems = refs[-5:]
    rows = keep_ref.shape[0] // cores

    @pl.when(mine_ref[0] == 1)
    def _():
        loads = [pltpu.make_async_copy(keep_ref, total, in_sems.at[0])]
        for index, ref in enumerate(received):
            loads.append(pltpu.make_async_copy(ref, terms.at[index], in_sems.at[index + 1]))
        for load in loads:
            load.start()
        for load in loads:
            load.wait()
        for index in range(parts):
            total[...] += terms[index].astype(jnp.float32)
        copies = [
            pltpu.make_async_copy(
                total.at[pl.ds(c * rows, rows)],
                scores_ref.at[spot_ref[0], c, pl.ds(start, rows)],
                out_sems.at[c],
            )
            for c in range(cores)
        ]
        for copy in copies:
            copy.start()
        for copy in copies:
            copy.wait()


def place(scores, shape, mine, spot, keep, received, start):
    given = [] if scores is None else [scores]
    parts = len(received)
    return pl.pallas_call(
        functools.partial(place_kernel, start, parts),
        in_specs=[in_smem] * 2 + [anywhere] * (1 + parts + len(given)),
        out_specs=anywhere,
        out_shape=jax.ShapeDtypeStruct(shape, jnp.float32),
        scratch_shapes=[
            pltpu.VMEM(keep.shape, jnp.float32),
            pltpu.VMEM((parts, *keep.shape), jnp.bfloat16),
            pltpu.SemaphoreType.DMA((1 + parts,)),
            pltpu.SemaphoreType.DMA((cores,)),
        ],
        input_output_aliases={3 + parts: 0} if given else {},
        compiler_params=pltpu.CompilerParams(vmem_limit_bytes=12 * mib),
        cost_estimate=small,
        name="place",
    )(mine, spot, keep, *received, *given)


def cut(whole, count):
    rows = whole.shape[0] // count
    return [whole[part * rows:(part + 1) * rows] for part in range(count)]


def after(array, *others):
    return lax.optimization_barrier((array, *others))[0]


def shards(blks, owners, grad_codes, scale_exps, val_grads, fisher):
    chips = blks // cores
    chips_per_owner = chips // owners
    me = lax.axis_index("dim")
    blk = lax.axis_index("blk")
    chip, core = blk // cores, lax.rem(blk, cores)[None]
    own, width = val_grads.shape
    count = grad_codes.shape[0]
    fisher = fisher[None, :]
    shape = (chips_per_owner, cores, own, count)

    def shift(panel):
        pairs = [
            (z * cores + c, (z + 1) % chips * cores + c) for z in range(chips) for c in range(cores)
        ]
        return lax.ppermute(panel, "blk", pairs)

    def swap(parts):
        pairs = [(b, b ^ 1) for b in range(blks)]
        return [lax.ppermute(part, "blk", pairs) for part in parts]

    def exchange(part, by):
        received = []
        for step in range(1, owners):
            pairs = []
            for b in range(blks):
                owner = (b // cores - by) % chips // chips_per_owner
                pairs.append((b * owners + (owner + step) % owners, b * owners + owner))
            received.append(lax.ppermute(part[1], ("blk", "dim"), pairs))
        return received

    def collect(scores, latest, part, received, by, start):
        source = lax.rem(chip - by + chips, chips)
        mine = (source // chips_per_owner == me).astype(jnp.int32)[None]
        received = [after(term, latest) for term in received]
        return place(
            scores, shape, mine, lax.rem(source, chips_per_owner)[None], part[0], received, start
        )

    hops = chips - 1
    knee = width * 5 // 8
    low_flow, high_flow = [shift(piece) for piece in cut(val_grads, 2)]
    train, *part = first(core, val_grads, *swap([val_grads]), fisher, grad_codes, scale_exps)
    scores = None
    for hop in range(1, hops):
        before, received = part, exchange(part, hop - 1)
        low_piece = after(low_flow, part)
        low_flow = shift(low_piece)
        low_other = swap(cut(low_piece, 2))
        high_piece = after(high_flow, low_piece)
        if hop + 1 < hops:
            high_flow = shift(high_piece)
        else:
            high_flow = [shift(high_piece[:, :knee]), shift(high_piece[:, knee:])]
        high_other = swap(cut(high_piece, 2))
        low_piece = after(low_piece, *received)
        part = multiply(
            core, [low_piece, high_piece], [*low_other, *high_other], fisher, train
        )
        scores = collect(scores, part, before, received, hop - 1, 0)
    before, earlier = part, exchange(part, hops - 1)
    low_piece = after(low_flow, part, scores)
    small_cuts = cut(low_piece, max(1, min(4, low_piece.shape[0] // 16)))
    part = multiply(core, [low_piece], swap(small_cuts), fisher, train)
    scores = collect(scores, part, before, earlier, hops - 1, 0)
    before, received = part, exchange(part, hops)
    left_piece = after(high_flow[0], part)
    left_other = swap(cut(left_piece, 2))
    part = multiply(core, [after(left_piece, *earlier)], left_other, fisher, train)
    right_piece = after(high_flow[1], part)
    right_other = swap([right_piece])
    right_piece = after(right_piece, *received)
    part = multiply(core, [right_piece], right_other, fisher, train, knee, part[:1])
    scores = collect(scores, part, before, received, hops, 0)
    scores = collect(scores, part, part, exchange(part, hops), hops, own // 2)
    return scores.reshape(chips_per_owner * cores * own, count)


def solution(mesh):
    in_specs = (
        P(("groups", "blk"), "dim"),
        P(("groups", "blk"), "dim"),
        P(("groups", "blk"), "dim"),
        P("dim"),
    )
    out_specs = P("dim", ("groups", "blk"))
    body = functools.partial(shards, mesh.shape["blk"], mesh.shape["dim"])
    return jax.shard_map(body, mesh=mesh, in_specs=in_specs, out_specs=out_specs, check_vma=False)
```

```python
import functools
import math

import jax
import jax.numpy as jnp
from jax import lax
from jax.experimental import pallas as pl
from jax.experimental.pallas import tpu as pltpu
from jax.sharding import PartitionSpec as P

damping = 0.05
lanes = 128
cores = 2
mib = 1 << 20
in_vmem = pl.BlockSpec(memory_space=pltpu.VMEM)
in_smem = pl.BlockSpec(memory_space=pltpu.SMEM)
anywhere = pl.BlockSpec(memory_space=pl.ANY)
small = pl.CostEstimate(flops=1, bytes_accessed=1, transcendentals=0)


def first_kernel(core_ref, mine_ref, other_ref, fisher_ref, codes_ref, exps_ref, train_ref, keep_ref,
                 send_ref, left, spread):
    rows, width = mine_ref.shape
    depth = min(width, 1024)
    core = core_ref[0]

    @pl.when(pl.program_id(0) == 0)
    def _():
        block = lax.broadcasted_iota(jnp.int32, spread.shape, 0)
        col = lax.broadcasted_iota(jnp.int32, spread.shape, 1)
        spread[...] = jnp.where(col // lanes == block, 1.0, 0.0).astype(jnp.bfloat16)
        for ref, place in ((mine_ref, core), (other_ref, 1 - core)):
            spot = pl.ds(pl.multiple_of(place * rows, rows), rows)
            for start in range(0, width, depth):
                cols = slice(start, start + depth)
                scale = 1.0 / (fisher_ref[:, cols] + damping)
                left[spot, cols] = (ref[:, cols].astype(jnp.float32) * scale).astype(jnp.bfloat16)

    exps = exps_ref[...]
    up = jnp.left_shift(1, jnp.maximum(exps, 0)).astype(jnp.float32)
    down = jnp.left_shift(1, jnp.maximum(-exps, 0)).astype(jnp.float32)
    factor = (up / down).astype(jnp.bfloat16)
    for start in range(0, width, depth):
        cols = slice(start, start + depth)
        wide = jnp.dot(factor, spread[:, cols], preferred_element_type=jnp.float32)
        train_ref[:, cols] = codes_ref[:, cols] * wide.astype(jnp.bfloat16)
    sums = lax.dot_general(
        left[...], train_ref[...], (((1,), (1,)), ((), ())), preferred_element_type=jnp.float32
    )
    keep_ref[...] = sums
    send_ref[...] = sums.astype(jnp.bfloat16)


def first(core, mine, other, fisher, codes, exps):
    rows, width = mine.shape
    count = codes.shape[0]
    blocks = width // lanes
    tile = min(count, 256)
    shape = (cores * rows, count)
    return pl.pallas_call(
        first_kernel,
        grid=(count // tile,),
        in_specs=[
            in_smem,
            pl.BlockSpec((rows, width), lambda i: (0, 0)),
            pl.BlockSpec((rows, width), lambda i: (0, 0)),
            pl.BlockSpec((1, width), lambda i: (0, 0)),
            pl.BlockSpec((tile, width), lambda i: (i, 0)),
            pl.BlockSpec((tile, blocks), lambda i: (i, 0)),
        ],
        out_specs=[
            pl.BlockSpec((tile, width), lambda i: (i, 0)),
            pl.BlockSpec((cores * rows, tile), lambda i: (0, i)),
            pl.BlockSpec((cores * rows, tile), lambda i: (0, i)),
        ],
        out_shape=[
            jax.ShapeDtypeStruct((count, width), jnp.bfloat16),
            jax.ShapeDtypeStruct(shape, jnp.float32),
            jax.ShapeDtypeStruct(shape, jnp.bfloat16),
        ],
        scratch_shapes=[
            pltpu.VMEM((cores * rows, width), jnp.bfloat16),
            pltpu.VMEM((blocks, width), jnp.bfloat16),
        ],
        compiler_params=pltpu.CompilerParams(vmem_limit_bytes=36 * mib),
        cost_estimate=small,
        name="first",
    )(core, mine, other, fisher, codes, exps)


def multiply_kernel(counts, low, top, core_ref, *refs):
    refs = list(refs)
    mine_refs, other_refs, given = [[refs.pop(0) for _ in range(size)] for size in counts]
    fisher_ref, train_ref, keep_ref, send_ref = refs[:4]
    left, held, keep, send, in_sems, train_sems, keep_sems, send_sems = refs[4:]
    rows = sum(ref.shape[0] for ref in mine_refs)
    slots, tile, width = held.shape
    tiles = keep.shape[1] // tile
    half = tile // 2
    depth = math.gcd(width, 1024)
    core = core_ref[0]

    def fetches(i):
        slot = lax.rem(i, slots)
        return [
            pltpu.make_async_copy(
                train_ref.at[
                    pl.ds(pl.multiple_of(i * tile, tile) + top + part * half, half), pl.ds(low, width)
                ],
                held.at[slot, pl.ds(part * half, half)],
                train_sems.at[slot, part],
            )
            for part in range(2)
        ]

    loads = []
    for group, place in ((mine_refs, core), (other_refs, 1 - core)):
        offset = 0
        for ref in group:
            spot = pl.ds(pl.multiple_of(place * rows, rows) + offset, ref.shape[0])
            loads.append(pltpu.make_async_copy(ref, left.at[spot], in_sems.at[len(loads)]))
            offset += ref.shape[0]
    for ref in given:
        source = ref.at[:, pl.ds(top, keep.shape[1])]
        loads.append(pltpu.make_async_copy(source, keep, in_sems.at[len(loads)]))
    for load in loads:
        load.start()
    for i in range(min(slots, tiles)):
        for fetch in fetches(i):
            fetch.start()
    for load in loads:
        load.wait()

    @pl.loop(0, width // depth)
    def _(k):
        cols = pl.ds(pl.multiple_of(k * depth, depth), depth)
        scale = 1.0 / (fisher_ref[:, cols] + damping)
        left[:, cols] = (left[:, cols].astype(jnp.float32) * scale).astype(jnp.bfloat16)

    def stores(i):
        cols = pl.ds(pl.multiple_of(i * tile, tile), tile)
        return (
            pltpu.make_async_copy(keep.at[:, cols], keep_ref.at[:, cols], keep_sems.at[i]),
            pltpu.make_async_copy(send.at[:, cols], send_ref.at[:, cols], send_sems.at[i]),
        )

    @pl.loop(0, tiles)
    def _(i):
        cols = pl.ds(pl.multiple_of(i * tile, tile), tile)
        for fetch in fetches(i):
            fetch.wait()
        sums = lax.dot_general(
            left[...], held[lax.rem(i, slots)], (((1,), (1,)), ((), ())),
            preferred_element_type=jnp.float32,
        )
        if given:
            sums += keep[:, cols]
        keep[:, cols] = sums
        send[:, cols] = sums.astype(jnp.bfloat16)
        for store in stores(i):
            store.start()

        @pl.when(i + slots < tiles)
        def _():
            for fetch in fetches(i + slots):
                fetch.start()

    @pl.loop(0, tiles)
    def _(i):
        for store in stores(i):
            store.wait()


def multiply(core, mine, other, fisher, train, low=0, given=(), span=None):
    rows = sum(part.shape[0] for part in mine)
    width = mine[0].shape[1]
    top, bottom = span or (0, train.shape[0])
    count = bottom - top
    tile = min(count, 256)
    slots = 4
    shape = (cores * rows, count)
    counts = (len(mine), len(other), len(given))
    return pl.pallas_call(
        functools.partial(multiply_kernel, counts, low, top),
        in_specs=[in_smem] + [anywhere] * sum(counts) + [in_vmem, anywhere],
        out_specs=[anywhere] * 2,
        out_shape=[
            jax.ShapeDtypeStruct(shape, jnp.float32), jax.ShapeDtypeStruct(shape, jnp.bfloat16),
        ],
        scratch_shapes=[
            pltpu.VMEM((cores * rows, width), jnp.bfloat16),
            pltpu.VMEM((slots, tile, width), jnp.bfloat16),
            pltpu.VMEM(shape, jnp.float32),
            pltpu.VMEM(shape, jnp.bfloat16),
            pltpu.SemaphoreType.DMA((sum(counts),)),
            pltpu.SemaphoreType.DMA((slots, 2)),
            pltpu.SemaphoreType.DMA((count // tile,)),
            pltpu.SemaphoreType.DMA((count // tile,)),
        ],
        compiler_params=pltpu.CompilerParams(vmem_limit_bytes=27 * mib),
        cost_estimate=small,
        name="multiply",
    )(core, *mine, *other, *given, fisher[:, low:low + width], train)


def place_kernel(start, col, parts, mine_ref, spot_ref, *refs):
    keep_ref, received = refs[0], refs[1:1 + parts]
    scores_ref, total, terms, in_sems, out_sems = refs[-5:]
    rows = keep_ref.shape[0] // cores

    @pl.when(mine_ref[0] == 1)
    def _():
        loads = [pltpu.make_async_copy(keep_ref, total, in_sems.at[0])]
        for index, ref in enumerate(received):
            loads.append(pltpu.make_async_copy(ref, terms.at[index], in_sems.at[index + 1]))
        for load in loads:
            load.start()
        for load in loads:
            load.wait()
        for index in range(parts):
            total[...] += terms[index].astype(jnp.float32)
        copies = [
            pltpu.make_async_copy(
                total.at[pl.ds(c * rows, rows)],
                scores_ref.at[spot_ref[0], c, pl.ds(start, rows), pl.ds(col, keep_ref.shape[1])],
                out_sems.at[c],
            )
            for c in range(cores)
        ]
        for copy in copies:
            copy.start()
        for copy in copies:
            copy.wait()


def place(scores, shape, mine, spot, keep, received, start, col):
    given = [] if scores is None else [scores]
    parts = len(received)
    return pl.pallas_call(
        functools.partial(place_kernel, start, col, parts),
        in_specs=[in_smem] * 2 + [anywhere] * (1 + parts + len(given)),
        out_specs=anywhere,
        out_shape=jax.ShapeDtypeStruct(shape, jnp.float32),
        scratch_shapes=[
            pltpu.VMEM(keep.shape, jnp.float32),
            pltpu.VMEM((parts, *keep.shape), jnp.bfloat16),
            pltpu.SemaphoreType.DMA((1 + parts,)),
            pltpu.SemaphoreType.DMA((cores,)),
        ],
        input_output_aliases={3 + parts: 0} if given else {},
        compiler_params=pltpu.CompilerParams(vmem_limit_bytes=12 * mib),
        cost_estimate=small,
        name="place",
    )(mine, spot, keep, *received, *given)


def cut(whole, count):
    rows = whole.shape[0] // count
    return [whole[part * rows:(part + 1) * rows] for part in range(count)]


def after(array, *others):
    return lax.optimization_barrier((array, *others))[0]


def shards(blks, owners, grad_codes, scale_exps, val_grads, fisher):
    chips = blks // cores
    chips_per_owner = chips // owners
    me = lax.axis_index("dim")
    blk = lax.axis_index("blk")
    chip, core = blk // cores, lax.rem(blk, cores)[None]
    own, width = val_grads.shape
    count = grad_codes.shape[0]
    fisher = fisher[None, :]
    shape = (chips_per_owner, cores, own, count)

    def shift(panel):
        pairs = [
            (z * cores + c, (z + 1) % chips * cores + c) for z in range(chips) for c in range(cores)
        ]
        return lax.ppermute(panel, "blk", pairs)

    def swap(parts):
        pairs = [(b, b ^ 1) for b in range(blks)]
        return [lax.ppermute(part, "blk", pairs) for part in parts]

    def exchange(part, by):
        received = []
        for step in range(1, owners):
            pairs = []
            for b in range(blks):
                owner = (b // cores - by) % chips // chips_per_owner
                pairs.append((b * owners + (owner + step) % owners, b * owners + owner))
            received.append(lax.ppermute(part[1], ("blk", "dim"), pairs))
        return received

    def collect(scores, latest, part, received, by, start, col=0):
        source = lax.rem(chip - by + chips, chips)
        mine = (source // chips_per_owner == me).astype(jnp.int32)[None]
        received = [after(term, latest) for term in received]
        return place(
            scores, shape, mine, lax.rem(source, chips_per_owner)[None], part[0], received, start, col
        )

    hops = chips - 1
    knee = width * 5 // 8
    low_flow, high_flow = [shift(piece) for piece in cut(val_grads, 2)]
    train, *part = first(core, val_grads, *swap([val_grads]), fisher, grad_codes, scale_exps)
    scores, earlier = None, []
    for hop in range(1, hops):
        before, received = part, exchange(part, hop - 1)
        low_piece = after(low_flow, part, *earlier)
        low_flow = shift(low_piece)
        low_other = swap(cut(low_piece, 2))
        high_piece = after(high_flow, low_piece)
        if hop + 1 < hops:
            high_flow = shift(high_piece)
        else:
            high_flow = [shift(high_piece[:, :knee]), shift(high_piece[:, knee:])]
        high_other = swap(cut(high_piece, 2))
        if hop > 1:
            low_piece = after(low_piece, *received)
        part = multiply(
            core, [low_piece, high_piece], [*low_other, *high_other], fisher, train
        )
        scores = collect(scores, part, before, received, hop - 1, 0)
        earlier = received
    before, earlier = part, exchange(part, hops - 1)
    low_piece = after(low_flow, part, scores)
    small = max(1, min(4, low_piece.shape[0] // 16))
    part = multiply(core, [low_piece], swap(cut(low_piece, small)), fisher, train)
    low_part, received = part, exchange(part, hops)
    left_piece = after(high_flow[0], part)
    part = multiply(core, [left_piece], swap(cut(left_piece, small)), fisher, train)
    right_piece = after(high_flow[1], part)
    right_other = swap([right_piece])
    right_piece = after(right_piece, *earlier)
    half = count // 2
    parts = []
    for top in (0, half):
        if parts:
            right_piece = after(right_piece, *parts, *received)
        parts.append(multiply(
            core, [right_piece], right_other, fisher, train, knee, part[:1], (top, top + half)
        ))
    scores = collect(scores, parts[-1], before, earlier, hops - 1, 0)
    scores = collect(scores, parts[-1], low_part, received, hops, 0)
    for col, part in zip((0, half), parts):
        scores = collect(scores, parts[-1], part, exchange(part, hops), hops, own // 2, col)
    return scores.reshape(chips_per_owner * cores * own, count)


def solution(mesh):
    in_specs = (
        P(("groups", "blk"), "dim"),
        P(("groups", "blk"), "dim"),
        P(("groups", "blk"), "dim"),
        P("dim"),
    )
    out_specs = P("dim", ("groups", "blk"))
    body = functools.partial(shards, mesh.shape["blk"], mesh.shape["dim"])
    return jax.shard_map(body, mesh=mesh, in_specs=in_specs, out_specs=out_specs, check_vma=False)
```

```python
import functools

import jax
import jax.numpy as jnp
from jax import lax
from jax.experimental import pallas as pl
from jax.experimental.pallas import tpu as pltpu
from jax.sharding import PartitionSpec as P

damping = 0.05
lanes = 128
cores = 2
mib = 1 << 20
in_vmem = pl.BlockSpec(memory_space=pltpu.VMEM)
in_smem = pl.BlockSpec(memory_space=pltpu.SMEM)
anywhere = pl.BlockSpec(memory_space=pl.ANY)
small = pl.CostEstimate(flops=1, bytes_accessed=1, transcendentals=0)


def first_kernel(core_ref, mine_ref, other_ref, fisher_ref, codes_ref, exps_ref, train_ref, keep_ref,
                 send_ref, left, spread):
    rows, width = mine_ref.shape
    depth = min(width, 1024)
    core = core_ref[0]

    @pl.when(pl.program_id(0) == 0)
    def _():
        block = lax.broadcasted_iota(jnp.int32, spread.shape, 0)
        col = lax.broadcasted_iota(jnp.int32, spread.shape, 1)
        spread[...] = jnp.where(col // lanes == block, 1.0, 0.0).astype(jnp.bfloat16)
        for ref, place in ((mine_ref, core), (other_ref, 1 - core)):
            spot = pl.ds(pl.multiple_of(place * rows, rows), rows)
            for start in range(0, width, depth):
                cols = slice(start, start + depth)
                scale = 1.0 / (fisher_ref[:, cols] + damping)
                left[spot, cols] = (ref[:, cols].astype(jnp.float32) * scale).astype(jnp.bfloat16)

    exps = exps_ref[...]
    up = jnp.left_shift(1, jnp.maximum(exps, 0)).astype(jnp.float32)
    down = jnp.left_shift(1, jnp.maximum(-exps, 0)).astype(jnp.float32)
    factor = (up / down).astype(jnp.bfloat16)
    for start in range(0, width, depth):
        cols = slice(start, start + depth)
        wide = jnp.dot(factor, spread[:, cols], preferred_element_type=jnp.float32)
        train_ref[:, cols] = codes_ref[:, cols] * wide.astype(jnp.bfloat16)
    sums = lax.dot_general(
        left[...], train_ref[...], (((1,), (1,)), ((), ())), preferred_element_type=jnp.float32
    )
    keep_ref[...] = sums
    send_ref[...] = sums.astype(jnp.bfloat16)


def first(core, mine, other, fisher, codes, exps):
    rows, width = mine.shape
    count = codes.shape[0]
    blocks = width // lanes
    tile = min(count, 256)
    shape = (cores * rows, count)
    return pl.pallas_call(
        first_kernel,
        grid=(count // tile,),
        in_specs=[
            in_smem,
            pl.BlockSpec((rows, width), lambda i: (0, 0)),
            pl.BlockSpec((rows, width), lambda i: (0, 0)),
            pl.BlockSpec((1, width), lambda i: (0, 0)),
            pl.BlockSpec((tile, width), lambda i: (i, 0)),
            pl.BlockSpec((tile, blocks), lambda i: (i, 0)),
        ],
        out_specs=[
            pl.BlockSpec((tile, width), lambda i: (i, 0)),
            pl.BlockSpec((cores * rows, tile), lambda i: (0, i)),
            pl.BlockSpec((cores * rows, tile), lambda i: (0, i)),
        ],
        out_shape=[
            jax.ShapeDtypeStruct((count, width), jnp.bfloat16),
            jax.ShapeDtypeStruct(shape, jnp.float32),
            jax.ShapeDtypeStruct(shape, jnp.bfloat16),
        ],
        scratch_shapes=[
            pltpu.VMEM((cores * rows, width), jnp.bfloat16),
            pltpu.VMEM((blocks, width), jnp.bfloat16),
        ],
        compiler_params=pltpu.CompilerParams(vmem_limit_bytes=36 * mib),
        cost_estimate=small,
        name="first",
    )(core, mine, other, fisher, codes, exps)


def multiply_kernel(counts, start, top, mine_ref, spot_ref, core_ref, *refs):
    refs = list(refs)
    mine_refs, other_refs, _ = [[refs.pop(0) for _ in range(size)] for size in counts]
    fisher_ref, train_ref, scores_ref, send_ref = refs[:4]
    left, held, keep, send, in_sems, train_sems, keep_sems, send_sems = refs[4:]
    rows = sum(ref.shape[0] for ref in mine_refs)
    slots, tile, width = held.shape
    tiles = keep.shape[1] // tile
    half = tile // 2
    depth = min(width, 1024)
    core = core_ref[0]

    def fetches(i):
        slot = lax.rem(i, slots)
        return [
            pltpu.make_async_copy(
                train_ref.at[pl.ds(pl.multiple_of(i * tile, tile) + top + part * half, half)],
                held.at[slot, pl.ds(part * half, half)],
                train_sems.at[slot, part],
            )
            for part in range(2)
        ]

    loads = []
    for group, place in ((mine_refs, core), (other_refs, 1 - core)):
        offset = 0
        for ref in group:
            spot = pl.ds(pl.multiple_of(place * rows, rows) + offset, ref.shape[0])
            loads.append(pltpu.make_async_copy(ref, left.at[spot], in_sems.at[len(loads)]))
            offset += ref.shape[0]
    for load in loads:
        load.start()
    for i in range(min(slots, tiles)):
        for fetch in fetches(i):
            fetch.start()
    for load in loads:
        load.wait()

    @pl.loop(0, width // depth)
    def _(k):
        cols = pl.ds(pl.multiple_of(k * depth, depth), depth)
        scale = 1.0 / (fisher_ref[:, cols] + damping)
        left[:, cols] = (left[:, cols].astype(jnp.float32) * scale).astype(jnp.bfloat16)

    def keeps(i):
        cols = pl.ds(pl.multiple_of(i * tile, tile), tile)
        return [
            pltpu.make_async_copy(
                keep.at[pl.ds(c * rows, rows), cols],
                scores_ref.at[
                    spot_ref[0], c, pl.ds(start, rows),
                    pl.ds(pl.multiple_of(i * tile, tile) + top, tile),
                ],
                keep_sems.at[i, c],
            )
            for c in range(cores)
        ]

    def sends(i):
        cols = pl.ds(pl.multiple_of(i * tile, tile), tile)
        return [pltpu.make_async_copy(send.at[:, cols], send_ref.at[:, cols], send_sems.at[i])]

    @pl.loop(0, tiles)
    def _(i):
        cols = pl.ds(pl.multiple_of(i * tile, tile), tile)
        for fetch in fetches(i):
            fetch.wait()
        sums = lax.dot_general(
            left[...], held[lax.rem(i, slots)], (((1,), (1,)), ((), ())),
            preferred_element_type=jnp.float32,
        )

        @pl.when(mine_ref[0] == 1)
        def _():
            keep[:, cols] = sums
            for copy in keeps(i):
                copy.start()

        @pl.when(mine_ref[0] == 0)
        def _():
            send[:, cols] = sums.astype(jnp.bfloat16)
            for copy in sends(i):
                copy.start()

        @pl.when(i + slots < tiles)
        def _():
            for fetch in fetches(i + slots):
                fetch.start()

    @pl.loop(0, tiles)
    def _(i):
        @pl.when(mine_ref[0] == 1)
        def _():
            for copy in keeps(i):
                copy.wait()

        @pl.when(mine_ref[0] == 0)
        def _():
            for copy in sends(i):
                copy.wait()


def multiply(scores, shape, where, core, mine, other, fisher, train, start, span=None):
    rows = sum(part.shape[0] for part in mine)
    width = mine[0].shape[1]
    top, bottom = span or (0, train.shape[0])
    count = bottom - top
    tile = min(count, 256)
    slots = 4
    block = (cores * rows, count)
    given = [] if scores is None else [scores]
    counts = (len(mine), len(other), len(given))
    return pl.pallas_call(
        functools.partial(multiply_kernel, counts, start, top),
        in_specs=[in_smem] * 3 + [anywhere] * sum(counts) + [in_vmem, anywhere],
        out_specs=[anywhere] * 2,
        out_shape=[
            jax.ShapeDtypeStruct(shape, jnp.float32), jax.ShapeDtypeStruct(block, jnp.bfloat16),
        ],
        scratch_shapes=[
            pltpu.VMEM((cores * rows, width), jnp.bfloat16),
            pltpu.VMEM((slots, tile, width), jnp.bfloat16),
            pltpu.VMEM(block, jnp.float32),
            pltpu.VMEM(block, jnp.bfloat16),
            pltpu.SemaphoreType.DMA((len(mine) + len(other),)),
            pltpu.SemaphoreType.DMA((slots, 2)),
            pltpu.SemaphoreType.DMA((count // tile, cores)),
            pltpu.SemaphoreType.DMA((count // tile,)),
        ],
        input_output_aliases={3 + len(mine) + len(other): 0} if given else {},
        compiler_params=pltpu.CompilerParams(vmem_limit_bytes=27 * mib),
        cost_estimate=small,
        name="multiply",
    )(*where, core, *mine, *other, *given, fisher, train)


def place_kernel(start, cols, kept, mine_ref, spot_ref, *refs):
    first_ref, received = refs[:kept], refs[kept:kept + len(cols)]
    scores_ref, total, in_sems, out_sems, *terms = refs[kept + len(cols) + 1:]
    rows = total.shape[0] // cores

    def own(c):
        return scores_ref.at[spot_ref[0], c, pl.ds(start, rows)]

    @pl.when(mine_ref[0] == 1)
    def _():
        if kept:
            loads = [pltpu.make_async_copy(first_ref[0], total, in_sems.at[0])]
        else:
            loads = [
                pltpu.make_async_copy(own(c), total.at[pl.ds(c * rows, rows)], in_sems.at[c])
                for c in range(cores)
            ]
        for index, ref in enumerate(received):
            loads.append(pltpu.make_async_copy(ref, terms[index], in_sems.at[cores + index]))
        for load in loads:
            load.start()
        for load in loads:
            load.wait()
        for col, term in zip(cols, terms):
            span = slice(col, col + term.shape[1])
            total[:, span] += term[...].astype(jnp.float32)
        copies = [
            pltpu.make_async_copy(total.at[pl.ds(c * rows, rows)], own(c), out_sems.at[c])
            for c in range(cores)
        ]
        for copy in copies:
            copy.start()
        for copy in copies:
            copy.wait()


def place(scores, where, kept, received, cols, start):
    count = scores.shape[-1]
    rows = received[0].shape[0]
    operands = [*kept, *received, scores]
    return pl.pallas_call(
        functools.partial(place_kernel, start, cols, len(kept)),
        in_specs=[in_smem] * 2 + [anywhere] * len(operands),
        out_specs=anywhere,
        out_shape=jax.ShapeDtypeStruct(scores.shape, jnp.float32),
        scratch_shapes=[
            pltpu.VMEM((rows, count), jnp.float32),
            pltpu.SemaphoreType.DMA((cores + len(received),)),
            pltpu.SemaphoreType.DMA((cores,)),
        ] + [pltpu.VMEM(term.shape, jnp.bfloat16) for term in received],
        input_output_aliases={1 + len(operands): 0},
        compiler_params=pltpu.CompilerParams(vmem_limit_bytes=12 * mib),
        cost_estimate=small,
        name="place",
    )(*where, *operands)


def cut(whole, count):
    rows = whole.shape[0] // count
    return [whole[part * rows:(part + 1) * rows] for part in range(count)]


def after(array, *others):
    return lax.optimization_barrier((array, *others))[0]


def shards(blks, owners, grad_codes, scale_exps, val_grads, fisher):
    chips = blks // cores
    chips_per_owner = chips // owners
    me = lax.axis_index("dim")
    blk = lax.axis_index("blk")
    chip, core = blk // cores, lax.rem(blk, cores)[None]
    own, width = val_grads.shape
    count = grad_codes.shape[0]
    fisher = fisher[None, :]
    shape = (chips_per_owner, cores, own, count)

    def shift(panel):
        pairs = [
            (z * cores + c, (z + 1) % chips * cores + c) for z in range(chips) for c in range(cores)
        ]
        return lax.ppermute(panel, "blk", pairs)

    def swap(parts):
        pairs = [(b, b ^ 1) for b in range(blks)]
        return [lax.ppermute(part, "blk", pairs) for part in parts]

    def exchange(send, by):
        received = []
        for step in range(1, owners):
            pairs = []
            for b in range(blks):
                owner = (b // cores - by) % chips // chips_per_owner
                pairs.append((b * owners + (owner + step) % owners, b * owners + owner))
            received.append(lax.ppermute(send, ("blk", "dim"), pairs))
        return received

    def whose(by):
        source = lax.rem(chip - by + chips, chips)
        mine = (source // chips_per_owner == me).astype(jnp.int32)[None]
        return mine, lax.rem(source, chips_per_owner)[None]

    hops = chips - 1
    low_flow, high_flow = [shift(piece) for piece in cut(val_grads, 2)]
    train, keep, send = first(core, val_grads, *swap([val_grads]), fisher, grad_codes, scale_exps)
    scores, kept = None, [keep]
    for hop in range(1, hops):
        received = exchange(send, hop - 1)
        low_piece = after(low_flow, send, *([] if scores is None else [scores]))
        low_flow = shift(low_piece)
        low_other = swap(cut(low_piece, 2))
        high_piece = after(high_flow, low_piece)
        high_flow = shift(high_piece)
        high_other = swap(cut(high_piece, 2))
        if hop > 1:
            low_piece = after(low_piece, *received)
        scores, send = multiply(
            scores, shape, whose(hop), core, [low_piece, high_piece], [*low_other, *high_other],
            fisher, train, 0,
        )
        received = [after(term, send) for term in received]
        scores = place(scores, whose(hop - 1), kept, received, [0] * len(received), 0)
        kept = []
    earlier = exchange(send, hops - 1)
    low_piece = after(low_flow, send, scores)
    small = max(1, min(4, low_piece.shape[0] // 16))
    scores, send = multiply(
        scores, shape, whose(hops), core, [low_piece], swap(cut(low_piece, small)), fisher, train, 0
    )
    received = exchange(send, hops)
    high_piece = after(high_flow, send)
    high_other = swap(cut(high_piece, small))
    high_piece = after(high_piece, *earlier)
    half = count // 2
    halves = []
    for top in (0, half):
        if top:
            high_piece = after(high_piece, send, *received)
        scores, send = multiply(
            scores, shape, whose(hops), core, [high_piece], high_other, fisher, train, own // 2,
            (top, top + half),
        )
        halves.append(exchange(send, hops))
    earlier = [after(term, send) for term in earlier]
    scores = place(scores, whose(hops - 1), [], earlier, [0] * len(earlier), 0)
    received = [after(term, scores) for term in received]
    scores = place(scores, whose(hops), [], received, [0] * len(received), 0)
    cols = [0] * len(received) + [half] * len(received)
    scores = place(scores, whose(hops), [], halves[0] + halves[1], cols, own // 2)
    return scores.reshape(chips_per_owner * cores * own, count)


def solution(mesh):
    in_specs = (
        P(("groups", "blk"), "dim"),
        P(("groups", "blk"), "dim"),
        P(("groups", "blk"), "dim"),
        P("dim"),
    )
    out_specs = P("dim", ("groups", "blk"))
    body = functools.partial(shards, mesh.shape["blk"], mesh.shape["dim"])
    return jax.shard_map(body, mesh=mesh, in_specs=in_specs, out_specs=out_specs, check_vma=False)
```

```python
import functools

import jax
import jax.numpy as jnp
from jax import lax
from jax.experimental import pallas as pl
from jax.experimental.pallas import tpu as pltpu
from jax.sharding import PartitionSpec as P

damping = 0.05
lanes = 128
cores = 2
mib = 1 << 20
in_vmem = pl.BlockSpec(memory_space=pltpu.VMEM)
in_smem = pl.BlockSpec(memory_space=pltpu.SMEM)
anywhere = pl.BlockSpec(memory_space=pl.ANY)
small = pl.CostEstimate(flops=1, bytes_accessed=1, transcendentals=0)


def first_kernel(core_ref, mine_ref, other_ref, fisher_ref, codes_ref, exps_ref, train_ref, keep_ref,
                 send_ref, left, spread):
    rows, width = mine_ref.shape
    depth = min(width, 1024)
    core = core_ref[0]

    @pl.when(pl.program_id(0) == 0)
    def _():
        block = lax.broadcasted_iota(jnp.int32, spread.shape, 0)
        col = lax.broadcasted_iota(jnp.int32, spread.shape, 1)
        spread[...] = jnp.where(col // lanes == block, 1.0, 0.0).astype(jnp.bfloat16)
        for ref, place in ((mine_ref, core), (other_ref, 1 - core)):
            spot = pl.ds(pl.multiple_of(place * rows, rows), rows)
            for start in range(0, width, depth):
                cols = slice(start, start + depth)
                scale = 1.0 / (fisher_ref[:, cols] + damping)
                left[spot, cols] = (ref[:, cols].astype(jnp.float32) * scale).astype(jnp.bfloat16)

    exps = exps_ref[...]
    up = jnp.left_shift(1, jnp.maximum(exps, 0)).astype(jnp.float32)
    down = jnp.left_shift(1, jnp.maximum(-exps, 0)).astype(jnp.float32)
    factor = (up / down).astype(jnp.bfloat16)
    for start in range(0, width, depth):
        cols = slice(start, start + depth)
        wide = jnp.dot(factor, spread[:, cols], preferred_element_type=jnp.float32)
        train_ref[:, cols] = codes_ref[:, cols] * wide.astype(jnp.bfloat16)
    sums = lax.dot_general(
        left[...], train_ref[...], (((1,), (1,)), ((), ())), preferred_element_type=jnp.float32
    )
    keep_ref[...] = sums
    send_ref[...] = sums.astype(jnp.bfloat16)


def first(core, mine, other, fisher, codes, exps):
    rows, width = mine.shape
    count = codes.shape[0]
    blocks = width // lanes
    tile = min(count, 256)
    shape = (cores * rows, count)
    return pl.pallas_call(
        first_kernel,
        grid=(count // tile,),
        in_specs=[
            in_smem,
            pl.BlockSpec((rows, width), lambda i: (0, 0)),
            pl.BlockSpec((rows, width), lambda i: (0, 0)),
            pl.BlockSpec((1, width), lambda i: (0, 0)),
            pl.BlockSpec((tile, width), lambda i: (i, 0)),
            pl.BlockSpec((tile, blocks), lambda i: (i, 0)),
        ],
        out_specs=[
            pl.BlockSpec((tile, width), lambda i: (i, 0)),
            pl.BlockSpec((cores * rows, tile), lambda i: (0, i)),
            pl.BlockSpec((cores * rows, tile), lambda i: (0, i)),
        ],
        out_shape=[
            jax.ShapeDtypeStruct((count, width), jnp.bfloat16),
            jax.ShapeDtypeStruct(shape, jnp.float32),
            jax.ShapeDtypeStruct(shape, jnp.bfloat16),
        ],
        scratch_shapes=[
            pltpu.VMEM((cores * rows, width), jnp.bfloat16),
            pltpu.VMEM((blocks, width), jnp.bfloat16),
        ],
        compiler_params=pltpu.CompilerParams(vmem_limit_bytes=36 * mib),
        cost_estimate=small,
        name="first",
    )(core, mine, other, fisher, codes, exps)


def multiply_kernel(counts, start, top, mine_ref, spot_ref, core_ref, *refs):
    refs = list(refs)
    mine_refs, other_refs, _ = [[refs.pop(0) for _ in range(size)] for size in counts]
    fisher_ref, train_ref, scores_ref, send_ref = refs[:4]
    left, held, keep, send, in_sems, train_sems, keep_sems, send_sems = refs[4:]
    rows = sum(ref.shape[0] for ref in mine_refs)
    slots, tile, width = held.shape
    tiles = keep.shape[1] // tile
    half = tile // 2
    depth = min(width, 1024)
    core = core_ref[0]

    def fetches(i):
        slot = lax.rem(i, slots)
        return [
            pltpu.make_async_copy(
                train_ref.at[pl.ds(pl.multiple_of(i * tile, tile) + top + part * half, half)],
                held.at[slot, pl.ds(part * half, half)],
                train_sems.at[slot, part],
            )
            for part in range(2)
        ]

    loads = []
    for group, place in ((mine_refs, core), (other_refs, 1 - core)):
        offset = 0
        for ref in group:
            spot = pl.ds(pl.multiple_of(place * rows, rows) + offset, ref.shape[0])
            loads.append(pltpu.make_async_copy(ref, left.at[spot], in_sems.at[len(loads)]))
            offset += ref.shape[0]
    for load in loads:
        load.start()
    for i in range(min(slots, tiles)):
        for fetch in fetches(i):
            fetch.start()
    for load in loads:
        load.wait()

    @pl.loop(0, width // depth)
    def _(k):
        cols = pl.ds(pl.multiple_of(k * depth, depth), depth)
        scale = 1.0 / (fisher_ref[:, cols] + damping)
        left[:, cols] = (left[:, cols].astype(jnp.float32) * scale).astype(jnp.bfloat16)

    def keeps(i):
        cols = pl.ds(pl.multiple_of(i * tile, tile), tile)
        return [
            pltpu.make_async_copy(
                keep.at[pl.ds(c * rows, rows), cols],
                scores_ref.at[
                    spot_ref[0], c, pl.ds(start, rows),
                    pl.ds(pl.multiple_of(i * tile, tile) + top, tile),
                ],
                keep_sems.at[i, c],
            )
            for c in range(cores)
        ]

    def sends(i):
        cols = pl.ds(pl.multiple_of(i * tile, tile), tile)
        return [pltpu.make_async_copy(send.at[:, cols], send_ref.at[:, cols], send_sems.at[i])]

    @pl.loop(0, tiles)
    def _(i):
        cols = pl.ds(pl.multiple_of(i * tile, tile), tile)
        for fetch in fetches(i):
            fetch.wait()
        sums = lax.dot_general(
            left[...], held[lax.rem(i, slots)], (((1,), (1,)), ((), ())),
            preferred_element_type=jnp.float32,
        )

        @pl.when(mine_ref[0] == 1)
        def _():
            keep[:, cols] = sums
            for copy in keeps(i):
                copy.start()

        @pl.when(mine_ref[0] == 0)
        def _():
            send[:, cols] = sums.astype(jnp.bfloat16)
            for copy in sends(i):
                copy.start()

        @pl.when(i + slots < tiles)
        def _():
            for fetch in fetches(i + slots):
                fetch.start()

    @pl.loop(0, tiles)
    def _(i):
        @pl.when(mine_ref[0] == 1)
        def _():
            for copy in keeps(i):
                copy.wait()

        @pl.when(mine_ref[0] == 0)
        def _():
            for copy in sends(i):
                copy.wait()


def multiply(scores, shape, where, core, mine, other, fisher, train, start, span=None):
    rows = sum(part.shape[0] for part in mine)
    width = mine[0].shape[1]
    top, bottom = span or (0, train.shape[0])
    count = bottom - top
    tile = min(count, 256)
    slots = 4
    block = (cores * rows, count)
    given = [] if scores is None else [scores]
    counts = (len(mine), len(other), len(given))
    return pl.pallas_call(
        functools.partial(multiply_kernel, counts, start, top),
        in_specs=[in_smem] * 3 + [anywhere] * sum(counts) + [in_vmem, anywhere],
        out_specs=[anywhere] * 2,
        out_shape=[
            jax.ShapeDtypeStruct(shape, jnp.float32), jax.ShapeDtypeStruct(block, jnp.bfloat16),
        ],
        scratch_shapes=[
            pltpu.VMEM((cores * rows, width), jnp.bfloat16),
            pltpu.VMEM((slots, tile, width), jnp.bfloat16),
            pltpu.VMEM(block, jnp.float32),
            pltpu.VMEM(block, jnp.bfloat16),
            pltpu.SemaphoreType.DMA((len(mine) + len(other),)),
            pltpu.SemaphoreType.DMA((slots, 2)),
            pltpu.SemaphoreType.DMA((count // tile, cores)),
            pltpu.SemaphoreType.DMA((count // tile,)),
        ],
        input_output_aliases={3 + len(mine) + len(other): 0} if given else {},
        compiler_params=pltpu.CompilerParams(vmem_limit_bytes=26 * mib),
        cost_estimate=small,
        name="multiply",
    )(*where, core, *mine, *other, *given, fisher, train)


def place_kernel(start, cols, kept, mine_ref, spot_ref, *refs):
    first_ref, received = refs[:kept], refs[kept:kept + len(cols)]
    scores_ref, total, in_sems, out_sems, *terms = refs[kept + len(cols) + 1:]
    rows = total.shape[0] // cores

    def own(c):
        return scores_ref.at[spot_ref[0], c, pl.ds(start, rows)]

    @pl.when(mine_ref[0] == 1)
    def _():
        if kept:
            loads = [pltpu.make_async_copy(first_ref[0], total, in_sems.at[0])]
        else:
            loads = [
                pltpu.make_async_copy(own(c), total.at[pl.ds(c * rows, rows)], in_sems.at[c])
                for c in range(cores)
            ]
        for index, ref in enumerate(received):
            loads.append(pltpu.make_async_copy(ref, terms[index], in_sems.at[cores + index]))
        for load in loads:
            load.start()
        for load in loads:
            load.wait()
        for col, term in zip(cols, terms):
            span = slice(col, col + term.shape[1])
            total[:, span] += term[...].astype(jnp.float32)
        copies = [
            pltpu.make_async_copy(total.at[pl.ds(c * rows, rows)], own(c), out_sems.at[c])
            for c in range(cores)
        ]
        for copy in copies:
            copy.start()
        for copy in copies:
            copy.wait()


def place(scores, where, kept, received, cols, start):
    count = scores.shape[-1]
    rows = received[0].shape[0]
    operands = [*kept, *received, scores]
    return pl.pallas_call(
        functools.partial(place_kernel, start, cols, len(kept)),
        in_specs=[in_smem] * 2 + [anywhere] * len(operands),
        out_specs=anywhere,
        out_shape=jax.ShapeDtypeStruct(scores.shape, jnp.float32),
        scratch_shapes=[
            pltpu.VMEM((rows, count), jnp.float32),
            pltpu.SemaphoreType.DMA((cores + len(received),)),
            pltpu.SemaphoreType.DMA((cores,)),
        ] + [pltpu.VMEM(term.shape, jnp.bfloat16) for term in received],
        input_output_aliases={1 + len(operands): 0},
        compiler_params=pltpu.CompilerParams(vmem_limit_bytes=12 * mib),
        cost_estimate=small,
        name="place",
    )(*where, *operands)


def cut_kernel(whole_ref, *refs):
    rows = refs[0].shape[0]
    for part, ref in enumerate(refs):
        ref[...] = whole_ref[part * rows:(part + 1) * rows, :]


def cut(whole, count):
    if count == 1:
        return [whole]
    piece = jax.ShapeDtypeStruct((whole.shape[0] // count, whole.shape[1]), whole.dtype)
    return pl.pallas_call(
        cut_kernel,
        in_specs=[in_vmem],
        out_specs=[in_vmem] * count,
        out_shape=[piece] * count,
        compiler_params=pltpu.CompilerParams(vmem_limit_bytes=6 * mib),
        cost_estimate=small,
        name="cut",
    )(whole)


def after(array, *others):
    return lax.optimization_barrier((array, *others))[0]


def shards(blks, owners, grad_codes, scale_exps, val_grads, fisher):
    chips = blks // cores
    chips_per_owner = chips // owners
    me = lax.axis_index("dim")
    blk = lax.axis_index("blk")
    chip, core = blk // cores, lax.rem(blk, cores)[None]
    own, width = val_grads.shape
    count = grad_codes.shape[0]
    fisher = fisher[None, :]
    shape = (chips_per_owner, cores, own, count)

    def shift(panel):
        pairs = [
            (z * cores + c, (z + 1) % chips * cores + c) for z in range(chips) for c in range(cores)
        ]
        return lax.ppermute(panel, "blk", pairs)

    def swap(parts):
        pairs = [(b, b ^ 1) for b in range(blks)]
        return [lax.ppermute(part, "blk", pairs) for part in parts]

    def exchange(send, by):
        received = []
        for step in range(1, owners):
            pairs = []
            for b in range(blks):
                owner = (b // cores - by) % chips // chips_per_owner
                pairs.append((b * owners + (owner + step) % owners, b * owners + owner))
            received.append(lax.ppermute(send, ("blk", "dim"), pairs))
        return received

    def whose(by):
        source = lax.rem(chip - by + chips, chips)
        mine = (source // chips_per_owner == me).astype(jnp.int32)[None]
        return mine, lax.rem(source, chips_per_owner)[None]

    hops = chips - 1
    low_flow, high_flow = [shift(piece) for piece in cut(val_grads, 2)]
    train, keep, send = first(core, val_grads, *swap([val_grads]), fisher, grad_codes, scale_exps)
    scores, kept = None, [keep]
    for hop in range(1, hops):
        received = exchange(send, hop - 1)
        low_piece = after(low_flow, send, *([] if scores is None else [scores]))
        low_flow = shift(low_piece)
        low_other = swap(cut(low_piece, 2))
        high_piece = after(high_flow, low_piece)
        high_flow = shift(high_piece)
        high_other = swap(cut(high_piece, 2))
        if hop > 1:
            low_piece = after(low_piece, *received)
        scores, send = multiply(
            scores, shape, whose(hop), core, [low_piece, high_piece], [*low_other, *high_other],
            fisher, train, 0,
        )
        received = [after(term, send) for term in received]
        scores = place(scores, whose(hop - 1), kept, received, [0] * len(received), 0)
        kept = []
    earlier = exchange(send, hops - 1)
    low_piece = after(low_flow, send, scores)
    small = max(1, min(4, low_piece.shape[0] // 16))
    scores, send = multiply(
        scores, shape, whose(hops), core, [low_piece], swap(cut(low_piece, small)), fisher, train, 0
    )
    received = exchange(send, hops)
    high_piece = after(high_flow, send)
    high_other = swap(cut(high_piece, small))
    high_piece = after(high_piece, *earlier)
    half = count // 2
    halves = []
    for top in (0, half):
        if top:
            high_piece = after(high_piece, send, *received)
        scores, send = multiply(
            scores, shape, whose(hops), core, [high_piece], high_other, fisher, train, own // 2,
            (top, top + half),
        )
        halves.append(exchange(send, hops))
    earlier = [after(term, send) for term in earlier]
    scores = place(scores, whose(hops - 1), [], earlier, [0] * len(earlier), 0)
    received = [after(term, scores) for term in received]
    scores = place(scores, whose(hops), [], received, [0] * len(received), 0)
    cols = [0] * len(received) + [half] * len(received)
    scores = place(scores, whose(hops), [], halves[0] + halves[1], cols, own // 2)
    return scores.reshape(chips_per_owner * cores * own, count)


def solution(mesh):
    in_specs = (
        P(("groups", "blk"), "dim"),
        P(("groups", "blk"), "dim"),
        P(("groups", "blk"), "dim"),
        P("dim"),
    )
    out_specs = P("dim", ("groups", "blk"))
    body = functools.partial(shards, mesh.shape["blk"], mesh.shape["dim"])
    return jax.shard_map(body, mesh=mesh, in_specs=in_specs, out_specs=out_specs, check_vma=False)
```

```python
import functools

import jax
import jax.numpy as jnp
from jax import lax
from jax.experimental import pallas as pl
from jax.experimental.pallas import tpu as pltpu
from jax.sharding import PartitionSpec as P

damping = 0.05
lanes = 128
cores = 2
mib = 1 << 20
in_vmem = pl.BlockSpec(memory_space=pltpu.VMEM)
in_smem = pl.BlockSpec(memory_space=pltpu.SMEM)
anywhere = pl.BlockSpec(memory_space=pl.ANY)
small = pl.CostEstimate(flops=1, bytes_accessed=1, transcendentals=0)


def first_kernel(core_ref, mine_ref, other_ref, fisher_ref, codes_ref, exps_ref, train_ref, keep_ref,
                 send_ref, left, spread):
    rows, width = mine_ref.shape
    depth = min(width, 1024)
    core = core_ref[0]

    @pl.when(pl.program_id(0) == 0)
    def _():
        block = lax.broadcasted_iota(jnp.int32, spread.shape, 0)
        col = lax.broadcasted_iota(jnp.int32, spread.shape, 1)
        spread[...] = jnp.where(col // lanes == block, 1.0, 0.0).astype(jnp.bfloat16)
        for ref, place in ((mine_ref, core), (other_ref, 1 - core)):
            spot = pl.ds(pl.multiple_of(place * rows, rows), rows)
            for start in range(0, width, depth):
                cols = slice(start, start + depth)
                scale = 1.0 / (fisher_ref[:, cols] + damping)
                left[spot, cols] = (ref[:, cols].astype(jnp.float32) * scale).astype(jnp.bfloat16)

    exps = exps_ref[...]
    up = jnp.left_shift(1, jnp.maximum(exps, 0)).astype(jnp.float32)
    down = jnp.left_shift(1, jnp.maximum(-exps, 0)).astype(jnp.float32)
    factor = (up / down).astype(jnp.bfloat16)
    for start in range(0, width, depth):
        cols = slice(start, start + depth)
        wide = jnp.dot(factor, spread[:, cols], preferred_element_type=jnp.float32)
        train_ref[:, cols] = codes_ref[:, cols] * wide.astype(jnp.bfloat16)
    sums = lax.dot_general(
        left[...], train_ref[...], (((1,), (1,)), ((), ())), preferred_element_type=jnp.float32
    )
    keep_ref[...] = sums
    send_ref[...] = sums.astype(jnp.bfloat16)


def first(core, mine, other, fisher, codes, exps):
    rows, width = mine.shape
    count = codes.shape[0]
    blocks = width // lanes
    tile = min(count, 256)
    shape = (cores * rows, count)
    return pl.pallas_call(
        first_kernel,
        grid=(count // tile,),
        in_specs=[
            in_smem,
            pl.BlockSpec((rows, width), lambda i: (0, 0)),
            pl.BlockSpec((rows, width), lambda i: (0, 0)),
            pl.BlockSpec((1, width), lambda i: (0, 0)),
            pl.BlockSpec((tile, width), lambda i: (i, 0)),
            pl.BlockSpec((tile, blocks), lambda i: (i, 0)),
        ],
        out_specs=[
            pl.BlockSpec((tile, width), lambda i: (i, 0)),
            pl.BlockSpec((cores * rows, tile), lambda i: (0, i)),
            pl.BlockSpec((cores * rows, tile), lambda i: (0, i)),
        ],
        out_shape=[
            jax.ShapeDtypeStruct((count, width), jnp.bfloat16),
            jax.ShapeDtypeStruct(shape, jnp.float32),
            jax.ShapeDtypeStruct(shape, jnp.bfloat16),
        ],
        scratch_shapes=[
            pltpu.VMEM((cores * rows, width), jnp.bfloat16),
            pltpu.VMEM((blocks, width), jnp.bfloat16),
        ],
        compiler_params=pltpu.CompilerParams(vmem_limit_bytes=36 * mib),
        cost_estimate=small,
        name="first",
    )(core, mine, other, fisher, codes, exps)


def multiply_kernel(counts, start, top, mine_ref, spot_ref, core_ref, *refs):
    refs = list(refs)
    mine_refs, other_refs, _ = [[refs.pop(0) for _ in range(size)] for size in counts]
    fisher_ref, train_ref, scores_ref, send_ref = refs[:4]
    left, held, keep, send, in_sems, train_sems, keep_sems, send_sems = refs[4:]
    rows = sum(ref.shape[0] for ref in mine_refs)
    slots, tile, width = held.shape
    tiles = keep_sems.shape[0]
    half = tile // 2
    depth = min(width, 1024)
    core = core_ref[0]

    def fetches(i):
        slot = lax.rem(i, slots)
        return [
            pltpu.make_async_copy(
                train_ref.at[pl.ds(pl.multiple_of(i * tile, tile) + top + part * half, half)],
                held.at[slot, pl.ds(part * half, half)],
                train_sems.at[slot, part],
            )
            for part in range(2)
        ]

    loads = []
    for group, place in ((mine_refs, core), (other_refs, 1 - core)):
        offset = 0
        for ref in group:
            spot = pl.ds(pl.multiple_of(place * rows, rows) + offset, ref.shape[0])
            loads.append(pltpu.make_async_copy(ref, left.at[spot], in_sems.at[len(loads)]))
            offset += ref.shape[0]
    for load in loads:
        load.start()
    for i in range(min(slots, tiles)):
        for fetch in fetches(i):
            fetch.start()
    for load in loads:
        load.wait()

    @pl.loop(0, width // depth)
    def _(k):
        cols = pl.ds(pl.multiple_of(k * depth, depth), depth)
        scale = 1.0 / (fisher_ref[:, cols] + damping)
        left[:, cols] = (left[:, cols].astype(jnp.float32) * scale).astype(jnp.bfloat16)

    def stores(i, of_mine):
        slot = lax.rem(i, 2)
        cols = pl.ds(pl.multiple_of(i * tile, tile), tile)
        if not of_mine:
            return [pltpu.make_async_copy(send.at[slot], send_ref.at[:, cols], send_sems.at[i])]
        return [
            pltpu.make_async_copy(
                keep.at[slot, pl.ds(c * rows, rows)],
                scores_ref.at[
                    spot_ref[0], c, pl.ds(start, rows),
                    pl.ds(pl.multiple_of(i * tile, tile) + top, tile),
                ],
                keep_sems.at[i, c],
            )
            for c in range(cores)
        ]

    def wait_stores(i):
        for flag in (0, 1):
            @pl.when(mine_ref[0] == flag)
            def _():
                for store in stores(i, flag):
                    store.wait()

    @pl.loop(0, tiles)
    def _(i):
        for fetch in fetches(i):
            fetch.wait()
        sums = lax.dot_general(
            left[...], held[lax.rem(i, slots)], (((1,), (1,)), ((), ())),
            preferred_element_type=jnp.float32,
        )

        @pl.when(i >= 2)
        def _():
            wait_stores(i - 2)

        @pl.when(mine_ref[0] == 1)
        def _():
            keep[lax.rem(i, 2)] = sums
            for store in stores(i, True):
                store.start()

        @pl.when(mine_ref[0] == 0)
        def _():
            send[lax.rem(i, 2)] = sums.astype(jnp.bfloat16)
            for store in stores(i, False):
                store.start()

        @pl.when(i + slots < tiles)
        def _():
            for fetch in fetches(i + slots):
                fetch.start()

    for i in range(max(tiles - 2, 0), tiles):
        wait_stores(i)


def multiply(scores, shape, where, core, mine, other, fisher, train, start, span=None):
    rows = sum(part.shape[0] for part in mine)
    width = mine[0].shape[1]
    top, bottom = span or (0, train.shape[0])
    count = bottom - top
    tile = min(count, 256)
    slots = 3
    block = (cores * rows, count)
    given = [] if scores is None else [scores]
    counts = (len(mine), len(other), len(given))
    return pl.pallas_call(
        functools.partial(multiply_kernel, counts, start, top),
        in_specs=[in_smem] * 3 + [anywhere] * sum(counts) + [in_vmem, anywhere],
        out_specs=[anywhere] * 2,
        out_shape=[
            jax.ShapeDtypeStruct(shape, jnp.float32), jax.ShapeDtypeStruct(block, jnp.bfloat16),
        ],
        scratch_shapes=[
            pltpu.VMEM((cores * rows, width), jnp.bfloat16),
            pltpu.VMEM((slots, tile, width), jnp.bfloat16),
            pltpu.VMEM((2, cores * rows, tile), jnp.float32),
            pltpu.VMEM((2, cores * rows, tile), jnp.bfloat16),
            pltpu.SemaphoreType.DMA((len(mine) + len(other),)),
            pltpu.SemaphoreType.DMA((slots, 2)),
            pltpu.SemaphoreType.DMA((count // tile, cores)),
            pltpu.SemaphoreType.DMA((count // tile,)),
        ],
        input_output_aliases={3 + len(mine) + len(other): 0} if given else {},
        compiler_params=pltpu.CompilerParams(vmem_limit_bytes=20 * mib),
        cost_estimate=small,
        name="multiply",
    )(*where, core, *mine, *other, *given, fisher, train)


def place_kernel(start, cols, kept, mine_ref, spot_ref, *refs):
    first_ref, received = refs[:kept], refs[kept:kept + len(cols)]
    scores_ref, total, in_sems, out_sems, *terms = refs[kept + len(cols) + 1:]
    rows = total.shape[0] // cores

    def own(c):
        return scores_ref.at[spot_ref[0], c, pl.ds(start, rows)]

    @pl.when(mine_ref[0] == 1)
    def _():
        if kept:
            loads = [pltpu.make_async_copy(first_ref[0], total, in_sems.at[0])]
        else:
            loads = [
                pltpu.make_async_copy(own(c), total.at[pl.ds(c * rows, rows)], in_sems.at[c])
                for c in range(cores)
            ]
        for index, ref in enumerate(received):
            loads.append(pltpu.make_async_copy(ref, terms[index], in_sems.at[cores + index]))
        for load in loads:
            load.start()
        for load in loads:
            load.wait()
        for col, term in zip(cols, terms):
            span = slice(col, col + term.shape[1])
            total[:, span] += term[...].astype(jnp.float32)
        copies = [
            pltpu.make_async_copy(total.at[pl.ds(c * rows, rows)], own(c), out_sems.at[c])
            for c in range(cores)
        ]
        for copy in copies:
            copy.start()
        for copy in copies:
            copy.wait()


def place(scores, where, kept, received, cols, start):
    count = scores.shape[-1]
    rows = received[0].shape[0]
    operands = [*kept, *received, scores]
    return pl.pallas_call(
        functools.partial(place_kernel, start, cols, len(kept)),
        in_specs=[in_smem] * 2 + [anywhere] * len(operands),
        out_specs=anywhere,
        out_shape=jax.ShapeDtypeStruct(scores.shape, jnp.float32),
        scratch_shapes=[
            pltpu.VMEM((rows, count), jnp.float32),
            pltpu.SemaphoreType.DMA((cores + len(received),)),
            pltpu.SemaphoreType.DMA((cores,)),
        ] + [pltpu.VMEM(term.shape, jnp.bfloat16) for term in received],
        input_output_aliases={1 + len(operands): 0},
        compiler_params=pltpu.CompilerParams(vmem_limit_bytes=12 * mib),
        cost_estimate=small,
        name="place",
    )(*where, *operands)


def cut_kernel(whole_ref, *refs):
    rows = refs[0].shape[0]
    for part, ref in enumerate(refs):
        ref[...] = whole_ref[part * rows:(part + 1) * rows, :]


def cut(whole, count):
    if count == 1:
        return [whole]
    piece = jax.ShapeDtypeStruct((whole.shape[0] // count, whole.shape[1]), whole.dtype)
    return pl.pallas_call(
        cut_kernel,
        in_specs=[in_vmem],
        out_specs=[in_vmem] * count,
        out_shape=[piece] * count,
        compiler_params=pltpu.CompilerParams(vmem_limit_bytes=6 * mib),
        cost_estimate=small,
        name="cut",
    )(whole)


def after(array, *others):
    return lax.optimization_barrier((array, *others))[0]


def shards(blks, owners, grad_codes, scale_exps, val_grads, fisher):
    chips = blks // cores
    chips_per_owner = chips // owners
    me = lax.axis_index("dim")
    blk = lax.axis_index("blk")
    chip, core = blk // cores, lax.rem(blk, cores)[None]
    own, width = val_grads.shape
    count = grad_codes.shape[0]
    fisher = fisher[None, :]
    shape = (chips_per_owner, cores, own, count)

    def shift(panel):
        pairs = [
            (z * cores + c, (z + 1) % chips * cores + c) for z in range(chips) for c in range(cores)
        ]
        return lax.ppermute(panel, "blk", pairs)

    def swap(parts):
        pairs = [(b, b ^ 1) for b in range(blks)]
        return [lax.ppermute(part, "blk", pairs) for part in parts]

    def exchange(send, by):
        received = []
        for step in range(1, owners):
            pairs = []
            for b in range(blks):
                owner = (b // cores - by) % chips // chips_per_owner
                pairs.append((b * owners + (owner + step) % owners, b * owners + owner))
            received.append(lax.ppermute(send, ("blk", "dim"), pairs))
        return received

    def whose(by):
        source = lax.rem(chip - by + chips, chips)
        mine = (source // chips_per_owner == me).astype(jnp.int32)[None]
        return mine, lax.rem(source, chips_per_owner)[None]

    hops = chips - 1
    flow = shift(val_grads)
    train, keep, send = first(core, val_grads, *swap([val_grads]), fisher, grad_codes, scale_exps)
    scores, kept = None, [keep]
    for hop in range(1, hops):
        received = exchange(send, hop - 1)
        panel = after(flow, send, *([] if scores is None else [scores]))
        if hop + 1 < hops:
            flow = shift(panel)
        else:
            low_flow, high_piece = cut(panel, 2)
            low_flow = shift(low_flow)
        if hop > 1:
            panel = after(panel, *received)
        scores, send = multiply(
            scores, shape, whose(hop), core, [panel], swap([panel]), fisher, train, 0
        )
        received = [after(term, send) for term in received]
        scores = place(scores, whose(hop - 1), kept, received, [0] * len(received), 0)
        kept = []
    high_flow = shift(after(high_piece, send))
    earlier = exchange(send, hops - 1)
    low_piece = after(low_flow, send, scores)
    scores, send = multiply(
        scores, shape, whose(hops), core, [low_piece], swap(cut(low_piece, 2)), fisher, train, 0
    )
    received = exchange(send, hops)
    high_piece = after(high_flow, send, *earlier)
    high_other = swap([high_piece])
    knee = count * 5 // 8
    halves = []
    for top, bottom in ((0, knee), (knee, count)):
        if top:
            high_piece = after(high_piece, send, *received)
        scores, send = multiply(
            scores, shape, whose(hops), core, [high_piece], high_other, fisher, train, own // 2,
            (top, bottom),
        )
        halves.append(exchange(send, hops))
    earlier = [after(term, send) for term in earlier]
    scores = place(scores, whose(hops - 1), [], earlier, [0] * len(earlier), 0)
    received = [after(term, scores) for term in received]
    scores = place(scores, whose(hops), [], received, [0] * len(received), 0)
    cols = [0] * len(received) + [knee] * len(received)
    scores = place(scores, whose(hops), [], halves[0] + halves[1], cols, own // 2)
    return scores.reshape(chips_per_owner * cores * own, count)


def solution(mesh):
    in_specs = (
        P(("groups", "blk"), "dim"),
        P(("groups", "blk"), "dim"),
        P(("groups", "blk"), "dim"),
        P("dim"),
    )
    out_specs = P("dim", ("groups", "blk"))
    body = functools.partial(shards, mesh.shape["blk"], mesh.shape["dim"])
    return jax.shard_map(body, mesh=mesh, in_specs=in_specs, out_specs=out_specs, check_vma=False)
```

```python
import functools

import jax
import jax.numpy as jnp
from jax import lax
from jax.experimental import pallas as pl
from jax.experimental.pallas import tpu as pltpu
from jax.sharding import PartitionSpec as P

damping = 0.05
lanes = 128
cores = 2
mib = 1 << 20
in_vmem = pl.BlockSpec(memory_space=pltpu.VMEM)
in_smem = pl.BlockSpec(memory_space=pltpu.SMEM)
anywhere = pl.BlockSpec(memory_space=pl.ANY)
small = pl.CostEstimate(flops=1, bytes_accessed=1, transcendentals=0)


def first_kernel(core_ref, mine_ref, other_ref, fisher_ref, codes_ref, exps_ref, train_ref, keep_ref,
                 send_ref, left, spread):
    rows, width = mine_ref.shape
    depth = min(width, 1024)
    core = core_ref[0]

    @pl.when(pl.program_id(0) == 0)
    def _():
        block = lax.broadcasted_iota(jnp.int32, spread.shape, 0)
        col = lax.broadcasted_iota(jnp.int32, spread.shape, 1)
        spread[...] = jnp.where(col // lanes == block, 1.0, 0.0).astype(jnp.bfloat16)
        for ref, place in ((mine_ref, core), (other_ref, 1 - core)):
            spot = pl.ds(pl.multiple_of(place * rows, rows), rows)
            for start in range(0, width, depth):
                cols = slice(start, start + depth)
                scale = 1.0 / (fisher_ref[:, cols] + damping)
                left[spot, cols] = (ref[:, cols].astype(jnp.float32) * scale).astype(jnp.bfloat16)

    exps = exps_ref[...]
    up = jnp.left_shift(1, jnp.maximum(exps, 0)).astype(jnp.float32)
    down = jnp.left_shift(1, jnp.maximum(-exps, 0)).astype(jnp.float32)
    factor = (up / down).astype(jnp.bfloat16)
    for start in range(0, width, depth):
        cols = slice(start, start + depth)
        wide = jnp.dot(factor, spread[:, cols], preferred_element_type=jnp.float32)
        train_ref[:, cols] = codes_ref[:, cols] * wide.astype(jnp.bfloat16)
    sums = lax.dot_general(
        left[...], train_ref[...], (((1,), (1,)), ((), ())), preferred_element_type=jnp.float32
    )
    keep_ref[...] = sums
    send_ref[...] = sums.astype(jnp.bfloat16)


def first(core, mine, other, fisher, codes, exps):
    rows, width = mine.shape
    count = codes.shape[0]
    blocks = width // lanes
    tile = min(count, 256)
    shape = (cores * rows, count)
    return pl.pallas_call(
        first_kernel,
        grid=(count // tile,),
        in_specs=[
            in_smem,
            pl.BlockSpec((rows, width), lambda i: (0, 0)),
            pl.BlockSpec((rows, width), lambda i: (0, 0)),
            pl.BlockSpec((1, width), lambda i: (0, 0)),
            pl.BlockSpec((tile, width), lambda i: (i, 0)),
            pl.BlockSpec((tile, blocks), lambda i: (i, 0)),
        ],
        out_specs=[
            pl.BlockSpec((tile, width), lambda i: (i, 0)),
            pl.BlockSpec((cores * rows, tile), lambda i: (0, i)),
            pl.BlockSpec((cores * rows, tile), lambda i: (0, i)),
        ],
        out_shape=[
            jax.ShapeDtypeStruct((count, width), jnp.bfloat16),
            jax.ShapeDtypeStruct(shape, jnp.float32),
            jax.ShapeDtypeStruct(shape, jnp.bfloat16),
        ],
        scratch_shapes=[
            pltpu.VMEM((cores * rows, width), jnp.bfloat16),
            pltpu.VMEM((blocks, width), jnp.bfloat16),
        ],
        compiler_params=pltpu.CompilerParams(vmem_limit_bytes=36 * mib),
        cost_estimate=small,
        name="first",
    )(core, mine, other, fisher, codes, exps)


def multiply_kernel(counts, start, top, mine_ref, spot_ref, core_ref, *refs):
    refs = list(refs)
    mine_refs, other_refs, _ = [[refs.pop(0) for _ in range(size)] for size in counts]
    fisher_ref, train_ref, scores_ref, send_ref = refs[:4]
    left, held, keep, send, in_sems, train_sems, keep_sems, send_sems = refs[4:]
    rows = sum(ref.shape[0] for ref in mine_refs)
    slots, tile, width = held.shape
    tiles = keep_sems.shape[0]
    half = tile // 2
    depth = min(width, 1024)
    core = core_ref[0]

    def fetches(i):
        slot = lax.rem(i, slots)
        return [
            pltpu.make_async_copy(
                train_ref.at[pl.ds(pl.multiple_of(i * tile, tile) + top + part * half, half)],
                held.at[slot, pl.ds(part * half, half)],
                train_sems.at[slot, part],
            )
            for part in range(2)
        ]

    loads = []
    for group, place in ((mine_refs, core), (other_refs, 1 - core)):
        offset = 0
        for ref in group:
            spot = pl.ds(pl.multiple_of(place * rows, rows) + offset, ref.shape[0])
            loads.append(pltpu.make_async_copy(ref, left.at[spot], in_sems.at[len(loads)]))
            offset += ref.shape[0]
    for load in loads:
        load.start()
    for i in range(min(slots, tiles)):
        for fetch in fetches(i):
            fetch.start()
    for load in loads:
        load.wait()

    @pl.loop(0, width // depth)
    def _(k):
        cols = pl.ds(pl.multiple_of(k * depth, depth), depth)
        scale = 1.0 / (fisher_ref[:, cols] + damping)
        left[:, cols] = (left[:, cols].astype(jnp.float32) * scale).astype(jnp.bfloat16)

    def stores(i, of_mine):
        slot = lax.rem(i, 2)
        cols = pl.ds(pl.multiple_of(i * tile, tile), tile)
        if not of_mine:
            return [pltpu.make_async_copy(send.at[slot], send_ref.at[:, cols], send_sems.at[i])]
        return [
            pltpu.make_async_copy(
                keep.at[slot, pl.ds(c * rows, rows)],
                scores_ref.at[
                    spot_ref[0], c, pl.ds(start, rows),
                    pl.ds(pl.multiple_of(i * tile, tile) + top, tile),
                ],
                keep_sems.at[i, c],
            )
            for c in range(cores)
        ]

    def wait_stores(i):
        for flag in (0, 1):
            @pl.when(mine_ref[0] == flag)
            def _():
                for store in stores(i, flag):
                    store.wait()

    @pl.loop(0, tiles)
    def _(i):
        for fetch in fetches(i):
            fetch.wait()
        sums = lax.dot_general(
            left[...], held[lax.rem(i, slots)], (((1,), (1,)), ((), ())),
            preferred_element_type=jnp.float32,
        )

        @pl.when(i >= 2)
        def _():
            wait_stores(i - 2)

        @pl.when(mine_ref[0] == 1)
        def _():
            keep[lax.rem(i, 2)] = sums
            for store in stores(i, True):
                store.start()

        @pl.when(mine_ref[0] == 0)
        def _():
            send[lax.rem(i, 2)] = sums.astype(jnp.bfloat16)
            for store in stores(i, False):
                store.start()

        @pl.when(i + slots < tiles)
        def _():
            for fetch in fetches(i + slots):
                fetch.start()

    for i in range(max(tiles - 2, 0), tiles):
        wait_stores(i)


def multiply(scores, shape, where, core, mine, other, fisher, train, start, span=None):
    rows = sum(part.shape[0] for part in mine)
    width = mine[0].shape[1]
    top, bottom = span or (0, train.shape[0])
    count = bottom - top
    tile = min(count, 256)
    slots = 4
    block = (cores * rows, count)
    given = [] if scores is None else [scores]
    counts = (len(mine), len(other), len(given))
    return pl.pallas_call(
        functools.partial(multiply_kernel, counts, start, top),
        in_specs=[in_smem] * 3 + [anywhere] * sum(counts) + [in_vmem, anywhere],
        out_specs=[anywhere] * 2,
        out_shape=[
            jax.ShapeDtypeStruct(shape, jnp.float32), jax.ShapeDtypeStruct(block, jnp.bfloat16),
        ],
        scratch_shapes=[
            pltpu.VMEM((cores * rows, width), jnp.bfloat16),
            pltpu.VMEM((slots, tile, width), jnp.bfloat16),
            pltpu.VMEM((2, cores * rows, tile), jnp.float32),
            pltpu.VMEM((2, cores * rows, tile), jnp.bfloat16),
            pltpu.SemaphoreType.DMA((len(mine) + len(other),)),
            pltpu.SemaphoreType.DMA((slots, 2)),
            pltpu.SemaphoreType.DMA((count // tile, cores)),
            pltpu.SemaphoreType.DMA((count // tile,)),
        ],
        input_output_aliases={3 + len(mine) + len(other): 0} if given else {},
        compiler_params=pltpu.CompilerParams(vmem_limit_bytes=22 * mib),
        cost_estimate=small,
        name="multiply",
    )(*where, core, *mine, *other, *given, fisher, train)


def place_kernel(start, cols, kept, mine_ref, spot_ref, *refs):
    first_ref, received = refs[:kept], refs[kept:kept + len(cols)]
    scores_ref, total, in_sems, out_sems, *terms = refs[kept + len(cols) + 1:]
    rows = total.shape[0] // cores

    def own(c):
        return scores_ref.at[spot_ref[0], c, pl.ds(start, rows)]

    @pl.when(mine_ref[0] == 1)
    def _():
        if kept:
            loads = [pltpu.make_async_copy(first_ref[0], total, in_sems.at[0])]
        else:
            loads = [
                pltpu.make_async_copy(own(c), total.at[pl.ds(c * rows, rows)], in_sems.at[c])
                for c in range(cores)
            ]
        for index, ref in enumerate(received):
            loads.append(pltpu.make_async_copy(ref, terms[index], in_sems.at[cores + index]))
        for load in loads:
            load.start()
        for load in loads:
            load.wait()
        for col, term in zip(cols, terms):
            span = slice(col, col + term.shape[1])
            total[:, span] += term[...].astype(jnp.float32)
        copies = [
            pltpu.make_async_copy(total.at[pl.ds(c * rows, rows)], own(c), out_sems.at[c])
            for c in range(cores)
        ]
        for copy in copies:
            copy.start()
        for copy in copies:
            copy.wait()


def place(scores, where, kept, received, cols, start):
    count = scores.shape[-1]
    rows = received[0].shape[0]
    operands = [*kept, *received, scores]
    return pl.pallas_call(
        functools.partial(place_kernel, start, cols, len(kept)),
        in_specs=[in_smem] * 2 + [anywhere] * len(operands),
        out_specs=anywhere,
        out_shape=jax.ShapeDtypeStruct(scores.shape, jnp.float32),
        scratch_shapes=[
            pltpu.VMEM((rows, count), jnp.float32),
            pltpu.SemaphoreType.DMA((cores + len(received),)),
            pltpu.SemaphoreType.DMA((cores,)),
        ] + [pltpu.VMEM(term.shape, jnp.bfloat16) for term in received],
        input_output_aliases={1 + len(operands): 0},
        compiler_params=pltpu.CompilerParams(vmem_limit_bytes=12 * mib),
        cost_estimate=small,
        name="place",
    )(*where, *operands)


def cut_kernel(whole_ref, *refs):
    rows = refs[0].shape[0]
    for part, ref in enumerate(refs):
        ref[...] = whole_ref[part * rows:(part + 1) * rows, :]


def cut(whole, count):
    if count == 1:
        return [whole]
    piece = jax.ShapeDtypeStruct((whole.shape[0] // count, whole.shape[1]), whole.dtype)
    return pl.pallas_call(
        cut_kernel,
        in_specs=[in_vmem],
        out_specs=[in_vmem] * count,
        out_shape=[piece] * count,
        compiler_params=pltpu.CompilerParams(vmem_limit_bytes=6 * mib),
        cost_estimate=small,
        name="cut",
    )(whole)


def after(array, *others):
    return lax.optimization_barrier((array, *others))[0]


def shards(blks, owners, grad_codes, scale_exps, val_grads, fisher):
    chips = blks // cores
    chips_per_owner = chips // owners
    me = lax.axis_index("dim")
    blk = lax.axis_index("blk")
    chip, core = blk // cores, lax.rem(blk, cores)[None]
    own, width = val_grads.shape
    count = grad_codes.shape[0]
    fisher = fisher[None, :]
    shape = (chips_per_owner, cores, own, count)

    def shift(panel):
        pairs = [
            (z * cores + c, (z + 1) % chips * cores + c) for z in range(chips) for c in range(cores)
        ]
        return lax.ppermute(panel, "blk", pairs)

    def swap(parts):
        pairs = [(b, b ^ 1) for b in range(blks)]
        return [lax.ppermute(part, "blk", pairs) for part in parts]

    def exchange(send, by):
        received = []
        for step in range(1, owners):
            pairs = []
            for b in range(blks):
                owner = (b // cores - by) % chips // chips_per_owner
                pairs.append((b * owners + (owner + step) % owners, b * owners + owner))
            received.append(lax.ppermute(send, ("blk", "dim"), pairs))
        return received

    def whose(by):
        source = lax.rem(chip - by + chips, chips)
        mine = (source // chips_per_owner == me).astype(jnp.int32)[None]
        return mine, lax.rem(source, chips_per_owner)[None]

    hops = chips - 1
    flow = shift(val_grads)
    train, keep, send = first(core, val_grads, *swap([val_grads]), fisher, grad_codes, scale_exps)
    scores, kept = None, [keep]
    for hop in range(1, hops):
        received = exchange(send, hop - 1)
        panel = after(flow, send, *([] if scores is None else [scores]))
        if hop + 1 < hops:
            flow = shift(panel)
        else:
            low_piece, high_piece = cut(panel, 2)
            flow = shift(low_piece)
            panel = after(panel, low_piece)
        if hop > 1:
            panel = after(panel, *received)
        scores, send = multiply(
            scores, shape, whose(hop), core, [panel], swap([panel]), fisher, train, 0
        )
        received = [after(term, send) for term in received]
        scores = place(scores, whose(hop - 1), kept, received, [0] * len(received), 0)
        kept = []
    earlier = exchange(send, hops - 1)
    low_piece = after(flow, send, scores)
    flow = shift(after(high_piece, low_piece))
    scores, send = multiply(
        scores, shape, whose(hops), core, [low_piece], swap([low_piece]), fisher, train, 0
    )
    received = exchange(send, hops)
    high_piece = after(flow, send, *earlier)
    high_other = swap([high_piece])
    knee = count * 5 // 8
    halves = []
    for top, bottom in ((0, knee), (knee, count)):
        if top:
            high_piece = after(high_piece, send, *received)
        scores, send = multiply(
            scores, shape, whose(hops), core, [high_piece], high_other, fisher, train, own // 2,
            (top, bottom),
        )
        halves.append(exchange(send, hops))
    earlier = [after(term, send) for term in earlier]
    scores = place(scores, whose(hops - 1), [], earlier, [0] * len(earlier), 0)
    received = [after(term, scores) for term in received]
    scores = place(scores, whose(hops), [], received, [0] * len(received), 0)
    cols = [0] * len(received) + [knee] * len(received)
    scores = place(scores, whose(hops), [], halves[0] + halves[1], cols, own // 2)
    return scores.reshape(chips_per_owner * cores * own, count)


def solution(mesh):
    in_specs = (
        P(("groups", "blk"), "dim"),
        P(("groups", "blk"), "dim"),
        P(("groups", "blk"), "dim"),
        P("dim"),
    )
    out_specs = P("dim", ("groups", "blk"))
    body = functools.partial(shards, mesh.shape["blk"], mesh.shape["dim"])
    return jax.shard_map(body, mesh=mesh, in_specs=in_specs, out_specs=out_specs, check_vma=False)
```

```python
import functools

import jax
import jax.numpy as jnp
from jax import lax
from jax.experimental import pallas as pl
from jax.experimental.pallas import tpu as pltpu
from jax.sharding import PartitionSpec as P

damping = 0.05
lanes = 128
cores = 2
mib = 1 << 20
in_vmem = pl.BlockSpec(memory_space=pltpu.VMEM)
in_smem = pl.BlockSpec(memory_space=pltpu.SMEM)
anywhere = pl.BlockSpec(memory_space=pl.ANY)
small = pl.CostEstimate(flops=1, bytes_accessed=1, transcendentals=0)


def first_kernel(core_ref, mine_ref, other_ref, fisher_ref, codes_ref, exps_ref, train_ref, keep_ref,
                 send_ref, left, spread):
    rows, width = mine_ref.shape
    depth = min(width, 1024)
    core = core_ref[0]

    @pl.when(pl.program_id(0) == 0)
    def _():
        block = lax.broadcasted_iota(jnp.int32, spread.shape, 0)
        col = lax.broadcasted_iota(jnp.int32, spread.shape, 1)
        spread[...] = jnp.where(col // lanes == block, 1.0, 0.0).astype(jnp.bfloat16)
        for ref, place in ((mine_ref, core), (other_ref, 1 - core)):
            spot = pl.ds(pl.multiple_of(place * rows, rows), rows)
            for start in range(0, width, depth):
                cols = slice(start, start + depth)
                scale = 1.0 / (fisher_ref[:, cols] + damping)
                left[spot, cols] = (ref[:, cols].astype(jnp.float32) * scale).astype(jnp.bfloat16)

    exps = exps_ref[...]
    up = jnp.left_shift(1, jnp.maximum(exps, 0)).astype(jnp.float32)
    down = jnp.left_shift(1, jnp.maximum(-exps, 0)).astype(jnp.float32)
    factor = (up / down).astype(jnp.bfloat16)
    for start in range(0, width, depth):
        cols = slice(start, start + depth)
        wide = jnp.dot(factor, spread[:, cols], preferred_element_type=jnp.float32)
        train_ref[:, cols] = codes_ref[:, cols] * wide.astype(jnp.bfloat16)
    sums = lax.dot_general(
        left[...], train_ref[...], (((1,), (1,)), ((), ())), preferred_element_type=jnp.float32
    )
    keep_ref[...] = sums
    send_ref[...] = sums.astype(jnp.bfloat16)


def first(core, mine, other, fisher, codes, exps):
    rows, width = mine.shape
    count = codes.shape[0]
    blocks = width // lanes
    tile = min(count, 256)
    shape = (cores * rows, count)
    return pl.pallas_call(
        first_kernel,
        grid=(count // tile,),
        in_specs=[
            in_smem,
            pl.BlockSpec((rows, width), lambda i: (0, 0)),
            pl.BlockSpec((rows, width), lambda i: (0, 0)),
            pl.BlockSpec((1, width), lambda i: (0, 0)),
            pl.BlockSpec((tile, width), lambda i: (i, 0)),
            pl.BlockSpec((tile, blocks), lambda i: (i, 0)),
        ],
        out_specs=[
            pl.BlockSpec((tile, width), lambda i: (i, 0)),
            pl.BlockSpec((cores * rows, tile), lambda i: (0, i)),
            pl.BlockSpec((cores * rows, tile), lambda i: (0, i)),
        ],
        out_shape=[
            jax.ShapeDtypeStruct((count, width), jnp.bfloat16),
            jax.ShapeDtypeStruct(shape, jnp.float32),
            jax.ShapeDtypeStruct(shape, jnp.bfloat16),
        ],
        scratch_shapes=[
            pltpu.VMEM((cores * rows, width), jnp.bfloat16),
            pltpu.VMEM((blocks, width), jnp.bfloat16),
        ],
        compiler_params=pltpu.CompilerParams(vmem_limit_bytes=36 * mib),
        cost_estimate=small,
        name="first",
    )(core, mine, other, fisher, codes, exps)


def multiply_kernel(counts, start, top, mine_ref, spot_ref, core_ref, *refs):
    refs = list(refs)
    mine_refs, other_refs, _ = [[refs.pop(0) for _ in range(size)] for size in counts]
    fisher_ref, train_ref, scores_ref, send_ref = refs[:4]
    left, held, keep, send, train_sems, keep_sems, send_sems = refs[4:]
    rows = sum(ref.shape[0] for ref in mine_refs)
    slots, tile, width = held.shape
    tiles = keep_sems.shape[0]
    half = tile // 2
    depth = min(width, 1024)
    core = core_ref[0]

    def fetches(i):
        slot = lax.rem(i, slots)
        return [
            pltpu.make_async_copy(
                train_ref.at[pl.ds(pl.multiple_of(i * tile, tile) + top + part * half, half)],
                held.at[slot, pl.ds(part * half, half)],
                train_sems.at[slot, part],
            )
            for part in range(2)
        ]

    for i in range(min(slots, tiles)):
        for fetch in fetches(i):
            fetch.start()

    @pl.loop(0, width // depth)
    def _(k):
        cols = pl.ds(pl.multiple_of(k * depth, depth), depth)
        scale = 1.0 / (fisher_ref[:, cols] + damping)
        for group, place in ((mine_refs, core), (other_refs, 1 - core)):
            offset = 0
            for ref in group:
                spot = pl.ds(pl.multiple_of(place * rows, rows) + offset, ref.shape[0])
                left[spot, cols] = (ref[:, cols].astype(jnp.float32) * scale).astype(jnp.bfloat16)
                offset += ref.shape[0]

    def stores(i, of_mine):
        slot = lax.rem(i, 2)
        cols = pl.ds(pl.multiple_of(i * tile, tile), tile)
        if not of_mine:
            return [pltpu.make_async_copy(send.at[slot], send_ref.at[:, cols], send_sems.at[i])]
        return [
            pltpu.make_async_copy(
                keep.at[slot, pl.ds(c * rows, rows)],
                scores_ref.at[
                    spot_ref[0], c, pl.ds(start, rows),
                    pl.ds(pl.multiple_of(i * tile, tile) + top, tile),
                ],
                keep_sems.at[i, c],
            )
            for c in range(cores)
        ]

    def wait_stores(i):
        for flag in (0, 1):
            @pl.when(mine_ref[0] == flag)
            def _():
                for store in stores(i, flag):
                    store.wait()

    @pl.loop(0, tiles)
    def _(i):
        for fetch in fetches(i):
            fetch.wait()
        sums = lax.dot_general(
            left[...], held[lax.rem(i, slots)], (((1,), (1,)), ((), ())),
            preferred_element_type=jnp.float32,
        )

        @pl.when(i >= 2)
        def _():
            wait_stores(i - 2)

        @pl.when(mine_ref[0] == 1)
        def _():
            keep[lax.rem(i, 2)] = sums
            for store in stores(i, True):
                store.start()

        @pl.when(mine_ref[0] == 0)
        def _():
            send[lax.rem(i, 2)] = sums.astype(jnp.bfloat16)
            for store in stores(i, False):
                store.start()

        @pl.when(i + slots < tiles)
        def _():
            for fetch in fetches(i + slots):
                fetch.start()

    for i in range(max(tiles - 2, 0), tiles):
        wait_stores(i)


def multiply(scores, shape, where, core, mine, other, fisher, train, start, span=None):
    rows = sum(part.shape[0] for part in mine)
    width = mine[0].shape[1]
    top, bottom = span or (0, train.shape[0])
    count = bottom - top
    tile = min(count, 256)
    slots = 3
    block = (cores * rows, count)
    given = [] if scores is None else [scores]
    counts = (len(mine), len(other), len(given))
    return pl.pallas_call(
        functools.partial(multiply_kernel, counts, start, top),
        in_specs=[in_smem] * 3 + [in_vmem] * sum(counts[:2]) + [anywhere] * len(given) + [in_vmem, anywhere],
        out_specs=[anywhere] * 2,
        out_shape=[
            jax.ShapeDtypeStruct(shape, jnp.float32), jax.ShapeDtypeStruct(block, jnp.bfloat16),
        ],
        scratch_shapes=[
            pltpu.VMEM((cores * rows, width), jnp.bfloat16),
            pltpu.VMEM((slots, tile, width), jnp.bfloat16),
            pltpu.VMEM((2, cores * rows, tile), jnp.float32),
            pltpu.VMEM((2, cores * rows, tile), jnp.bfloat16),
            pltpu.SemaphoreType.DMA((slots, 2)),
            pltpu.SemaphoreType.DMA((count // tile, cores)),
            pltpu.SemaphoreType.DMA((count // tile,)),
        ],
        input_output_aliases={3 + len(mine) + len(other): 0} if given else {},
        compiler_params=pltpu.CompilerParams(vmem_limit_bytes=22 * mib),
        cost_estimate=small,
        name="multiply",
    )(*where, core, *mine, *other, *given, fisher, train)


def place_kernel(start, cols, kept, mine_ref, spot_ref, *refs):
    first_ref, received = refs[:kept], refs[kept:kept + len(cols)]
    scores_ref, total, in_sems, out_sems, *terms = refs[kept + len(cols) + 1:]
    rows = total.shape[0] // cores

    def own(c):
        return scores_ref.at[spot_ref[0], c, pl.ds(start, rows)]

    @pl.when(mine_ref[0] == 1)
    def _():
        if kept:
            loads = [pltpu.make_async_copy(first_ref[0], total, in_sems.at[0])]
        else:
            loads = [
                pltpu.make_async_copy(own(c), total.at[pl.ds(c * rows, rows)], in_sems.at[c])
                for c in range(cores)
            ]
        for index, ref in enumerate(received):
            loads.append(pltpu.make_async_copy(ref, terms[index], in_sems.at[cores + index]))
        for load in loads:
            load.start()
        for load in loads:
            load.wait()
        for col, term in zip(cols, terms):
            span = slice(col, col + term.shape[1])
            total[:, span] += term[...].astype(jnp.float32)
        copies = [
            pltpu.make_async_copy(total.at[pl.ds(c * rows, rows)], own(c), out_sems.at[c])
            for c in range(cores)
        ]
        for copy in copies:
            copy.start()
        for copy in copies:
            copy.wait()


def place(scores, where, kept, received, cols, start):
    count = scores.shape[-1]
    rows = received[0].shape[0]
    operands = [*kept, *received, scores]
    return pl.pallas_call(
        functools.partial(place_kernel, start, cols, len(kept)),
        in_specs=[in_smem] * 2 + [anywhere] * len(operands),
        out_specs=anywhere,
        out_shape=jax.ShapeDtypeStruct(scores.shape, jnp.float32),
        scratch_shapes=[
            pltpu.VMEM((rows, count), jnp.float32),
            pltpu.SemaphoreType.DMA((cores + len(received),)),
            pltpu.SemaphoreType.DMA((cores,)),
        ] + [pltpu.VMEM(term.shape, jnp.bfloat16) for term in received],
        input_output_aliases={1 + len(operands): 0},
        compiler_params=pltpu.CompilerParams(vmem_limit_bytes=12 * mib),
        cost_estimate=small,
        name="place",
    )(*where, *operands)


def cut_kernel(whole_ref, *refs):
    rows = refs[0].shape[0]
    for part, ref in enumerate(refs):
        ref[...] = whole_ref[part * rows:(part + 1) * rows, :]


def cut(whole, count):
    if count == 1:
        return [whole]
    piece = jax.ShapeDtypeStruct((whole.shape[0] // count, whole.shape[1]), whole.dtype)
    return pl.pallas_call(
        cut_kernel,
        in_specs=[in_vmem],
        out_specs=[in_vmem] * count,
        out_shape=[piece] * count,
        compiler_params=pltpu.CompilerParams(vmem_limit_bytes=6 * mib),
        cost_estimate=small,
        name="cut",
    )(whole)


def after(array, *others):
    return lax.optimization_barrier((array, *others))[0]


def shards(blks, owners, grad_codes, scale_exps, val_grads, fisher):
    chips = blks // cores
    chips_per_owner = chips // owners
    me = lax.axis_index("dim")
    blk = lax.axis_index("blk")
    chip, core = blk // cores, lax.rem(blk, cores)[None]
    own, width = val_grads.shape
    count = grad_codes.shape[0]
    fisher = fisher[None, :]
    shape = (chips_per_owner, cores, own, count)

    def shift(panel):
        pairs = [
            (z * cores + c, (z + 1) % chips * cores + c) for z in range(chips) for c in range(cores)
        ]
        return lax.ppermute(panel, "blk", pairs)

    def swap(parts):
        pairs = [(b, b ^ 1) for b in range(blks)]
        return [lax.ppermute(part, "blk", pairs) for part in parts]

    def exchange(send, by):
        received = []
        for step in range(1, owners):
            pairs = []
            for b in range(blks):
                owner = (b // cores - by) % chips // chips_per_owner
                pairs.append((b * owners + (owner + step) % owners, b * owners + owner))
            received.append(lax.ppermute(send, ("blk", "dim"), pairs))
        return received

    def whose(by):
        source = lax.rem(chip - by + chips, chips)
        mine = (source // chips_per_owner == me).astype(jnp.int32)[None]
        return mine, lax.rem(source, chips_per_owner)[None]

    hops = chips - 1
    flow = shift(val_grads)
    train, keep, send = first(core, val_grads, *swap([val_grads]), fisher, grad_codes, scale_exps)
    scores, kept = None, [keep]
    for hop in range(1, hops):
        received = exchange(send, hop - 1)
        panel = after(flow, send, *([] if scores is None else [scores]))
        if hop + 1 < hops:
            flow = shift(panel)
        else:
            low_piece, high_piece = cut(panel, 2)
            flow = shift(low_piece)
            panel = after(panel, low_piece)
        if hop > 1:
            panel = after(panel, *received)
        scores, send = multiply(
            scores, shape, whose(hop), core, [panel], swap([panel]), fisher, train, 0
        )
        received = [after(term, send) for term in received]
        scores = place(scores, whose(hop - 1), kept, received, [0] * len(received), 0)
        kept = []
    earlier = exchange(send, hops - 1)
    high_flow = shift(after(high_piece, send))
    low_piece = after(flow, send, scores)
    scores, send = multiply(
        scores, shape, whose(hops), core, [low_piece], swap(cut(low_piece, 2)), fisher, train, 0
    )
    received = exchange(send, hops)
    high_piece = after(high_flow, send, *earlier)
    high_other = swap([high_piece])
    knee = count * 5 // 8
    halves = []
    for top, bottom in ((0, knee), (knee, count)):
        if top:
            high_piece = after(high_piece, send, *received)
        scores, send = multiply(
            scores, shape, whose(hops), core, [high_piece], high_other, fisher, train, own // 2,
            (top, bottom),
        )
        halves.append(exchange(send, hops))
    earlier = [after(term, send) for term in earlier]
    scores = place(scores, whose(hops - 1), [], earlier, [0] * len(earlier), 0)
    received = [after(term, scores) for term in received]
    scores = place(scores, whose(hops), [], received, [0] * len(received), 0)
    cols = [0] * len(received) + [knee] * len(received)
    scores = place(scores, whose(hops), [], halves[0] + halves[1], cols, own // 2)
    return scores.reshape(chips_per_owner * cores * own, count)


def solution(mesh):
    in_specs = (
        P(("groups", "blk"), "dim"),
        P(("groups", "blk"), "dim"),
        P(("groups", "blk"), "dim"),
        P("dim"),
    )
    out_specs = P("dim", ("groups", "blk"))
    body = functools.partial(shards, mesh.shape["blk"], mesh.shape["dim"])
    return jax.shard_map(body, mesh=mesh, in_specs=in_specs, out_specs=out_specs, check_vma=False)
```

```python
import functools

import jax
import jax.numpy as jnp
from jax import lax
from jax.experimental import pallas as pl
from jax.experimental.pallas import tpu as pltpu
from jax.sharding import PartitionSpec as P

damping = 0.05
lanes = 128
cores = 2
mib = 1 << 20
in_vmem = pl.BlockSpec(memory_space=pltpu.VMEM)
in_smem = pl.BlockSpec(memory_space=pltpu.SMEM)
anywhere = pl.BlockSpec(memory_space=pl.ANY)
small = pl.CostEstimate(flops=1, bytes_accessed=1, transcendentals=0)


def first_kernel(core_ref, mine_ref, other_ref, fisher_ref, codes_ref, exps_ref, train_ref, keep_ref,
                 send_ref, left, spread):
    rows, width = mine_ref.shape
    depth = min(width, 1024)
    core = core_ref[0]

    @pl.when(pl.program_id(0) == 0)
    def _():
        block = lax.broadcasted_iota(jnp.int32, spread.shape, 0)
        col = lax.broadcasted_iota(jnp.int32, spread.shape, 1)
        spread[...] = jnp.where(col // lanes == block, 1.0, 0.0).astype(jnp.bfloat16)
        for ref, place in ((mine_ref, core), (other_ref, 1 - core)):
            spot = pl.ds(pl.multiple_of(place * rows, rows), rows)
            for start in range(0, width, depth):
                cols = slice(start, start + depth)
                scale = 1.0 / (fisher_ref[:, cols] + damping)
                left[spot, cols] = (ref[:, cols].astype(jnp.float32) * scale).astype(jnp.bfloat16)

    exps = exps_ref[...]
    up = jnp.left_shift(1, jnp.maximum(exps, 0)).astype(jnp.float32)
    down = jnp.left_shift(1, jnp.maximum(-exps, 0)).astype(jnp.float32)
    factor = (up / down).astype(jnp.bfloat16)
    for start in range(0, width, depth):
        cols = slice(start, start + depth)
        wide = jnp.dot(factor, spread[:, cols], preferred_element_type=jnp.float32)
        train_ref[:, cols] = codes_ref[:, cols] * wide.astype(jnp.bfloat16)
    sums = lax.dot_general(
        left[...], train_ref[...], (((1,), (1,)), ((), ())), preferred_element_type=jnp.float32
    )
    keep_ref[...] = sums
    send_ref[...] = sums.astype(jnp.bfloat16)


def first(core, mine, other, fisher, codes, exps):
    rows, width = mine.shape
    count = codes.shape[0]
    blocks = width // lanes
    tile = min(count, 256)
    shape = (cores * rows, count)
    return pl.pallas_call(
        first_kernel,
        grid=(count // tile,),
        in_specs=[
            in_smem,
            pl.BlockSpec((rows, width), lambda i: (0, 0)),
            pl.BlockSpec((rows, width), lambda i: (0, 0)),
            pl.BlockSpec((1, width), lambda i: (0, 0)),
            pl.BlockSpec((tile, width), lambda i: (i, 0)),
            pl.BlockSpec((tile, blocks), lambda i: (i, 0)),
        ],
        out_specs=[
            pl.BlockSpec((tile, width), lambda i: (i, 0)),
            pl.BlockSpec((cores * rows, tile), lambda i: (0, i)),
            pl.BlockSpec((cores * rows, tile), lambda i: (0, i)),
        ],
        out_shape=[
            jax.ShapeDtypeStruct((count, width), jnp.bfloat16),
            jax.ShapeDtypeStruct(shape, jnp.float32),
            jax.ShapeDtypeStruct(shape, jnp.bfloat16),
        ],
        scratch_shapes=[
            pltpu.VMEM((cores * rows, width), jnp.bfloat16),
            pltpu.VMEM((blocks, width), jnp.bfloat16),
        ],
        compiler_params=pltpu.CompilerParams(vmem_limit_bytes=36 * mib),
        cost_estimate=small,
        name="first",
    )(core, mine, other, fisher, codes, exps)


def multiply_kernel(counts, start, top, mine_ref, spot_ref, core_ref, *refs):
    refs = list(refs)
    mine_refs, other_refs, _ = [[refs.pop(0) for _ in range(size)] for size in counts]
    fisher_ref, train_ref, scores_ref, send_ref = refs[:4]
    left, held, keep, send, train_sems, keep_sems, send_sems = refs[4:]
    rows = sum(ref.shape[0] for ref in mine_refs)
    slots, tile, width = held.shape
    tiles = keep_sems.shape[0]
    parts = train_sems.shape[1]
    share = tile // parts
    depth = min(width, 1024)
    core = core_ref[0]

    def fetches(i):
        slot = lax.rem(i, slots)
        return [
            pltpu.make_async_copy(
                train_ref.at[pl.ds(pl.multiple_of(i * tile, tile) + top + part * share, share)],
                held.at[slot, pl.ds(part * share, share)],
                train_sems.at[slot, part],
            )
            for part in range(parts)
        ]

    for i in range(min(slots, tiles)):
        for fetch in fetches(i):
            fetch.start()

    @pl.loop(0, width // depth)
    def _(k):
        cols = pl.ds(pl.multiple_of(k * depth, depth), depth)
        scale = 1.0 / (fisher_ref[:, cols] + damping)
        for group, place in ((mine_refs, core), (other_refs, 1 - core)):
            offset = 0
            for ref in group:
                spot = pl.ds(pl.multiple_of(place * rows, rows) + offset, ref.shape[0])
                left[spot, cols] = (ref[:, cols].astype(jnp.float32) * scale).astype(jnp.bfloat16)
                offset += ref.shape[0]

    def stores(i, of_mine):
        slot = lax.rem(i, 2)
        cols = pl.ds(pl.multiple_of(i * tile, tile), tile)
        if not of_mine:
            return [pltpu.make_async_copy(send.at[slot], send_ref.at[:, cols], send_sems.at[i])]
        return [
            pltpu.make_async_copy(
                keep.at[slot, pl.ds(c * rows, rows)],
                scores_ref.at[
                    spot_ref[0], c, pl.ds(start, rows),
                    pl.ds(pl.multiple_of(i * tile, tile) + top, tile),
                ],
                keep_sems.at[i, c],
            )
            for c in range(cores)
        ]

    def wait_stores(i):
        for flag in (0, 1):
            @pl.when(mine_ref[0] == flag)
            def _():
                for store in stores(i, flag):
                    store.wait()

    @pl.loop(0, tiles)
    def _(i):
        for fetch in fetches(i):
            fetch.wait()
        sums = lax.dot_general(
            left[...], held[lax.rem(i, slots)], (((1,), (1,)), ((), ())),
            preferred_element_type=jnp.float32,
        )

        @pl.when(i >= 2)
        def _():
            wait_stores(i - 2)

        @pl.when(mine_ref[0] == 1)
        def _():
            keep[lax.rem(i, 2)] = sums
            for store in stores(i, True):
                store.start()

        @pl.when(mine_ref[0] == 0)
        def _():
            send[lax.rem(i, 2)] = sums.astype(jnp.bfloat16)
            for store in stores(i, False):
                store.start()

        @pl.when(i + slots < tiles)
        def _():
            for fetch in fetches(i + slots):
                fetch.start()

    for i in range(max(tiles - 2, 0), tiles):
        wait_stores(i)


def multiply(scores, shape, where, core, mine, other, fisher, train, start, span=None):
    rows = sum(part.shape[0] for part in mine)
    width = mine[0].shape[1]
    top, bottom = span or (0, train.shape[0])
    count = bottom - top
    tile = min(count, 256)
    slots = 3
    block = (cores * rows, count)
    given = [] if scores is None else [scores]
    counts = (len(mine), len(other), len(given))
    return pl.pallas_call(
        functools.partial(multiply_kernel, counts, start, top),
        in_specs=[in_smem] * 3 + [in_vmem] * sum(counts[:2]) + [anywhere] * len(given) + [in_vmem, anywhere],
        out_specs=[anywhere] * 2,
        out_shape=[
            jax.ShapeDtypeStruct(shape, jnp.float32), jax.ShapeDtypeStruct(block, jnp.bfloat16),
        ],
        scratch_shapes=[
            pltpu.VMEM((cores * rows, width), jnp.bfloat16),
            pltpu.VMEM((slots, tile, width), jnp.bfloat16),
            pltpu.VMEM((2, cores * rows, tile), jnp.float32),
            pltpu.VMEM((2, cores * rows, tile), jnp.bfloat16),
            pltpu.SemaphoreType.DMA((slots, 4)),
            pltpu.SemaphoreType.DMA((count // tile, cores)),
            pltpu.SemaphoreType.DMA((count // tile,)),
        ],
        input_output_aliases={3 + len(mine) + len(other): 0} if given else {},
        compiler_params=pltpu.CompilerParams(vmem_limit_bytes=22 * mib),
        cost_estimate=small,
        name="multiply",
    )(*where, core, *mine, *other, *given, fisher, train)


def place_kernel(start, cols, kept, mine_ref, spot_ref, *refs):
    first_ref, received = refs[:kept], refs[kept:kept + len(cols)]
    scores_ref, total, in_sems, out_sems, *terms = refs[kept + len(cols) + 1:]
    rows = total.shape[0] // cores

    def own(c):
        return scores_ref.at[spot_ref[0], c, pl.ds(start, rows)]

    @pl.when(mine_ref[0] == 1)
    def _():
        if kept:
            loads = [pltpu.make_async_copy(first_ref[0], total, in_sems.at[0])]
        else:
            loads = [
                pltpu.make_async_copy(own(c), total.at[pl.ds(c * rows, rows)], in_sems.at[c])
                for c in range(cores)
            ]
        for index, ref in enumerate(received):
            loads.append(pltpu.make_async_copy(ref, terms[index], in_sems.at[cores + index]))
        for load in loads:
            load.start()
        for load in loads:
            load.wait()
        for col, term in zip(cols, terms):
            span = slice(col, col + term.shape[1])
            total[:, span] += term[...].astype(jnp.float32)
        copies = [
            pltpu.make_async_copy(total.at[pl.ds(c * rows, rows)], own(c), out_sems.at[c])
            for c in range(cores)
        ]
        for copy in copies:
            copy.start()
        for copy in copies:
            copy.wait()


def place(scores, where, kept, received, cols, start):
    count = scores.shape[-1]
    rows = received[0].shape[0]
    operands = [*kept, *received, scores]
    return pl.pallas_call(
        functools.partial(place_kernel, start, cols, len(kept)),
        in_specs=[in_smem] * 2 + [anywhere] * len(operands),
        out_specs=anywhere,
        out_shape=jax.ShapeDtypeStruct(scores.shape, jnp.float32),
        scratch_shapes=[
            pltpu.VMEM((rows, count), jnp.float32),
            pltpu.SemaphoreType.DMA((cores + len(received),)),
            pltpu.SemaphoreType.DMA((cores,)),
        ] + [pltpu.VMEM(term.shape, jnp.bfloat16) for term in received],
        input_output_aliases={1 + len(operands): 0},
        compiler_params=pltpu.CompilerParams(vmem_limit_bytes=12 * mib),
        cost_estimate=small,
        name="place",
    )(*where, *operands)


def cut_kernel(whole_ref, *refs):
    rows = refs[0].shape[0]
    for part, ref in enumerate(refs):
        ref[...] = whole_ref[part * rows:(part + 1) * rows, :]


def cut(whole, count):
    if count == 1:
        return [whole]
    piece = jax.ShapeDtypeStruct((whole.shape[0] // count, whole.shape[1]), whole.dtype)
    return pl.pallas_call(
        cut_kernel,
        in_specs=[in_vmem],
        out_specs=[in_vmem] * count,
        out_shape=[piece] * count,
        compiler_params=pltpu.CompilerParams(vmem_limit_bytes=6 * mib),
        cost_estimate=small,
        name="cut",
    )(whole)


def after(array, *others):
    return lax.optimization_barrier((array, *others))[0]


def shards(blks, owners, grad_codes, scale_exps, val_grads, fisher):
    chips = blks // cores
    chips_per_owner = chips // owners
    me = lax.axis_index("dim")
    blk = lax.axis_index("blk")
    chip, core = blk // cores, lax.rem(blk, cores)[None]
    own, width = val_grads.shape
    count = grad_codes.shape[0]
    fisher = fisher[None, :]
    shape = (chips_per_owner, cores, own, count)

    ring = [*range(0, chips, 2), *reversed(range(1, chips, 2))]
    origin = [
        [ring[(ring.index(z) - hop) % chips] for z in range(chips)] for hop in range(chips)
    ]

    def shift(panel):
        pairs = [
            (ring[place] * cores + c, ring[(place + 1) % chips] * cores + c)
            for place in range(chips) for c in range(cores)
        ]
        return lax.ppermute(panel, "blk", pairs)

    def swap(parts):
        pairs = [(b, b ^ 1) for b in range(blks)]
        return [lax.ppermute(part, "blk", pairs) for part in parts]

    def exchange(send, by):
        received = []
        for step in range(1, owners):
            pairs = []
            for b in range(blks):
                owner = origin[by][b // cores] // chips_per_owner
                pairs.append((b * owners + (owner + step) % owners, b * owners + owner))
            received.append(lax.ppermute(send, ("blk", "dim"), pairs))
        return received

    def whose(by):
        source = sum(jnp.where(chip == z, origin[by][z], 0) for z in range(chips))
        mine = (source // chips_per_owner == me).astype(jnp.int32)[None]
        return mine, lax.rem(source, chips_per_owner)[None]

    hops = chips - 1
    flow = shift(val_grads)
    train, keep, send = first(core, val_grads, *swap([val_grads]), fisher, grad_codes, scale_exps)
    scores, kept = None, [keep]
    for hop in range(1, hops):
        received = exchange(send, hop - 1)
        panel = after(flow, send, *([] if scores is None else [scores]))
        if hop + 1 < hops:
            flow = shift(panel)
        else:
            low_piece, high_piece = cut(panel, 2)
            flow = shift(low_piece)
            panel = after(panel, low_piece)
        if hop > 1:
            panel = after(panel, *received)
        scores, send = multiply(
            scores, shape, whose(hop), core, [panel], swap([panel]), fisher, train, 0
        )
        received = [after(term, send) for term in received]
        scores = place(scores, whose(hop - 1), kept, received, [0] * len(received), 0)
        kept = []
    earlier = exchange(send, hops - 1)
    high_flow = shift(after(high_piece, send))
    low_piece = after(flow, send, scores)
    scores, send = multiply(
        scores, shape, whose(hops), core, [low_piece], swap(cut(low_piece, 2)), fisher, train, 0
    )
    received = exchange(send, hops)
    high_piece = after(high_flow, send, *earlier)
    high_other = swap([high_piece])
    scores, send = multiply(
        scores, shape, whose(hops), core, [high_piece], high_other, fisher, train, own // 2
    )
    last = exchange(send, hops)
    earlier = [after(term, send) for term in earlier]
    scores = place(scores, whose(hops - 1), [], earlier, [0] * len(earlier), 0)
    received = [after(term, scores) for term in received]
    scores = place(scores, whose(hops), [], received, [0] * len(received), 0)
    scores = place(scores, whose(hops), [], last, [0] * len(last), own // 2)
    return scores.reshape(chips_per_owner * cores * own, count)


def solution(mesh):
    in_specs = (
        P(("groups", "blk"), "dim"),
        P(("groups", "blk"), "dim"),
        P(("groups", "blk"), "dim"),
        P("dim"),
    )
    out_specs = P("dim", ("groups", "blk"))
    body = functools.partial(shards, mesh.shape["blk"], mesh.shape["dim"])
    return jax.shard_map(body, mesh=mesh, in_specs=in_specs, out_specs=out_specs, check_vma=False)
```

```python
import functools

import jax
import jax.numpy as jnp
from jax import lax
from jax.experimental import pallas as pl
from jax.experimental.pallas import tpu as pltpu
from jax.sharding import PartitionSpec as P

damping = 0.05
lanes = 128
cores = 2
mib = 1 << 20
in_vmem = pl.BlockSpec(memory_space=pltpu.VMEM)
in_smem = pl.BlockSpec(memory_space=pltpu.SMEM)
anywhere = pl.BlockSpec(memory_space=pl.ANY)
small = pl.CostEstimate(flops=1, bytes_accessed=1, transcendentals=0)


def first_kernel(core_ref, mine_ref, other_ref, fisher_ref, codes_ref, exps_ref, train_ref, keep_ref,
                 send_ref, left, spread):
    rows, width = mine_ref.shape
    depth = min(width, 1024)
    core = core_ref[0]

    @pl.when(pl.program_id(0) == 0)
    def _():
        block = lax.broadcasted_iota(jnp.int32, spread.shape, 0)
        col = lax.broadcasted_iota(jnp.int32, spread.shape, 1)
        spread[...] = jnp.where(col // lanes == block, 1.0, 0.0).astype(jnp.bfloat16)
        for ref, place in ((mine_ref, core), (other_ref, 1 - core)):
            spot = pl.ds(pl.multiple_of(place * rows, rows), rows)
            for start in range(0, width, depth):
                cols = slice(start, start + depth)
                scale = 1.0 / (fisher_ref[:, cols] + damping)
                left[spot, cols] = (ref[:, cols].astype(jnp.float32) * scale).astype(jnp.bfloat16)

    exps = exps_ref[...]
    up = jnp.left_shift(1, jnp.maximum(exps, 0)).astype(jnp.float32)
    down = jnp.left_shift(1, jnp.maximum(-exps, 0)).astype(jnp.float32)
    factor = (up / down).astype(jnp.bfloat16)
    for start in range(0, width, depth):
        cols = slice(start, start + depth)
        wide = jnp.dot(factor, spread[:, cols], preferred_element_type=jnp.float32)
        train_ref[:, cols] = codes_ref[:, cols] * wide.astype(jnp.bfloat16)
    sums = lax.dot_general(
        left[...], train_ref[...], (((1,), (1,)), ((), ())), preferred_element_type=jnp.float32
    )
    keep_ref[...] = sums
    send_ref[...] = sums.astype(jnp.bfloat16)


def first(core, mine, other, fisher, codes, exps):
    rows, width = mine.shape
    count = codes.shape[0]
    blocks = width // lanes
    tile = min(count, 256)
    shape = (cores * rows, count)
    return pl.pallas_call(
        first_kernel,
        grid=(count // tile,),
        in_specs=[
            in_smem,
            pl.BlockSpec((rows, width), lambda i: (0, 0)),
            pl.BlockSpec((rows, width), lambda i: (0, 0)),
            pl.BlockSpec((1, width), lambda i: (0, 0)),
            pl.BlockSpec((tile, width), lambda i: (i, 0)),
            pl.BlockSpec((tile, blocks), lambda i: (i, 0)),
        ],
        out_specs=[
            pl.BlockSpec((tile, width), lambda i: (i, 0)),
            pl.BlockSpec((cores * rows, tile), lambda i: (0, i)),
            pl.BlockSpec((cores * rows, tile), lambda i: (0, i)),
        ],
        out_shape=[
            jax.ShapeDtypeStruct((count, width), jnp.bfloat16),
            jax.ShapeDtypeStruct(shape, jnp.float32),
            jax.ShapeDtypeStruct(shape, jnp.bfloat16),
        ],
        scratch_shapes=[
            pltpu.VMEM((cores * rows, width), jnp.bfloat16),
            pltpu.VMEM((blocks, width), jnp.bfloat16),
        ],
        compiler_params=pltpu.CompilerParams(vmem_limit_bytes=36 * mib),
        cost_estimate=small,
        name="first",
    )(core, mine, other, fisher, codes, exps)


def multiply_kernel(counts, start, top, mine_ref, spot_ref, core_ref, *refs):
    refs = list(refs)
    mine_refs, other_refs, _ = [[refs.pop(0) for _ in range(size)] for size in counts]
    fisher_ref, train_ref, scores_ref, send_ref = refs[:4]
    left, held, keep, send, train_sems, keep_sems, send_sems = refs[4:]
    rows = sum(ref.shape[0] for ref in mine_refs)
    slots, tile, width = held.shape
    tiles = keep_sems.shape[0]
    parts = train_sems.shape[1]
    share = tile // parts
    depth = min(width, 1024)
    core = core_ref[0]

    def fetches(i):
        slot = lax.rem(i, slots)
        return [
            pltpu.make_async_copy(
                train_ref.at[pl.ds(pl.multiple_of(i * tile, tile) + top + part * share, share)],
                held.at[slot, pl.ds(part * share, share)],
                train_sems.at[slot, part],
            )
            for part in range(parts)
        ]

    for i in range(min(slots, tiles)):
        for fetch in fetches(i):
            fetch.start()

    @pl.loop(0, width // depth)
    def _(k):
        cols = pl.ds(pl.multiple_of(k * depth, depth), depth)
        scale = 1.0 / (fisher_ref[:, cols] + damping)
        for group, place in ((mine_refs, core), (other_refs, 1 - core)):
            offset = 0
            for ref in group:
                spot = pl.ds(pl.multiple_of(place * rows, rows) + offset, ref.shape[0])
                left[spot, cols] = (ref[:, cols].astype(jnp.float32) * scale).astype(jnp.bfloat16)
                offset += ref.shape[0]

    def stores(i, of_mine):
        slot = lax.rem(i, 2)
        cols = pl.ds(pl.multiple_of(i * tile, tile), tile)
        if not of_mine:
            return [pltpu.make_async_copy(send.at[slot], send_ref.at[:, cols], send_sems.at[i])]
        return [
            pltpu.make_async_copy(
                keep.at[slot, pl.ds(c * rows, rows)],
                scores_ref.at[
                    spot_ref[0], c, pl.ds(start, rows),
                    pl.ds(pl.multiple_of(i * tile, tile) + top, tile),
                ],
                keep_sems.at[i, c],
            )
            for c in range(cores)
        ]

    def wait_stores(i):
        for flag in (0, 1):
            @pl.when(mine_ref[0] == flag)
            def _():
                for store in stores(i, flag):
                    store.wait()

    @pl.loop(0, tiles)
    def _(i):
        for fetch in fetches(i):
            fetch.wait()
        sums = lax.dot_general(
            left[...], held[lax.rem(i, slots)], (((1,), (1,)), ((), ())),
            preferred_element_type=jnp.float32,
        )

        @pl.when(i >= 2)
        def _():
            wait_stores(i - 2)

        @pl.when(mine_ref[0] == 1)
        def _():
            keep[lax.rem(i, 2)] = sums
            for store in stores(i, True):
                store.start()

        @pl.when(mine_ref[0] == 0)
        def _():
            send[lax.rem(i, 2)] = sums.astype(jnp.bfloat16)
            for store in stores(i, False):
                store.start()

        @pl.when(i + slots < tiles)
        def _():
            for fetch in fetches(i + slots):
                fetch.start()

    for i in range(max(tiles - 2, 0), tiles):
        wait_stores(i)


def multiply(scores, shape, where, core, mine, other, fisher, train, start, span=None):
    rows = sum(part.shape[0] for part in mine)
    width = mine[0].shape[1]
    top, bottom = span or (0, train.shape[0])
    count = bottom - top
    tile = min(count, 256)
    slots = 3
    block = (cores * rows, count)
    grant = 4 * block[0] * width + 2 * slots * tile * width + 12 * block[0] * tile + 2 * mib
    given = [] if scores is None else [scores]
    counts = (len(mine), len(other), len(given))
    return pl.pallas_call(
        functools.partial(multiply_kernel, counts, start, top),
        in_specs=[in_smem] * 3 + [in_vmem] * sum(counts[:2]) + [anywhere] * len(given) + [in_vmem, anywhere],
        out_specs=[anywhere] * 2,
        out_shape=[
            jax.ShapeDtypeStruct(shape, jnp.float32), jax.ShapeDtypeStruct(block, jnp.bfloat16),
        ],
        scratch_shapes=[
            pltpu.VMEM((cores * rows, width), jnp.bfloat16),
            pltpu.VMEM((slots, tile, width), jnp.bfloat16),
            pltpu.VMEM((2, cores * rows, tile), jnp.float32),
            pltpu.VMEM((2, cores * rows, tile), jnp.bfloat16),
            pltpu.SemaphoreType.DMA((slots, 4)),
            pltpu.SemaphoreType.DMA((count // tile, cores)),
            pltpu.SemaphoreType.DMA((count // tile,)),
        ],
        input_output_aliases={3 + len(mine) + len(other): 0} if given else {},
        compiler_params=pltpu.CompilerParams(vmem_limit_bytes=grant),
        cost_estimate=small,
        name="multiply",
    )(*where, core, *mine, *other, *given, fisher, train)


def place_kernel(start, cols, kept, mine_ref, spot_ref, *refs):
    first_ref, received = refs[:kept], refs[kept:kept + len(cols)]
    scores_ref, total, in_sems, out_sems, *terms = refs[kept + len(cols) + 1:]
    rows = total.shape[0] // cores

    def own(c):
        return scores_ref.at[spot_ref[0], c, pl.ds(start, rows)]

    @pl.when(mine_ref[0] == 1)
    def _():
        if kept:
            loads = [pltpu.make_async_copy(first_ref[0], total, in_sems.at[0])]
        else:
            loads = [
                pltpu.make_async_copy(own(c), total.at[pl.ds(c * rows, rows)], in_sems.at[c])
                for c in range(cores)
            ]
        for index, ref in enumerate(received):
            loads.append(pltpu.make_async_copy(ref, terms[index], in_sems.at[cores + index]))
        for load in loads:
            load.start()
        for load in loads:
            load.wait()
        for col, term in zip(cols, terms):
            span = slice(col, col + term.shape[1])
            total[:, span] += term[...].astype(jnp.float32)
        copies = [
            pltpu.make_async_copy(total.at[pl.ds(c * rows, rows)], own(c), out_sems.at[c])
            for c in range(cores)
        ]
        for copy in copies:
            copy.start()
        for copy in copies:
            copy.wait()


def place(scores, where, kept, received, cols, start):
    count = scores.shape[-1]
    rows = received[0].shape[0]
    operands = [*kept, *received, scores]
    return pl.pallas_call(
        functools.partial(place_kernel, start, cols, len(kept)),
        in_specs=[in_smem] * 2 + [anywhere] * len(operands),
        out_specs=anywhere,
        out_shape=jax.ShapeDtypeStruct(scores.shape, jnp.float32),
        scratch_shapes=[
            pltpu.VMEM((rows, count), jnp.float32),
            pltpu.SemaphoreType.DMA((cores + len(received),)),
            pltpu.SemaphoreType.DMA((cores,)),
        ] + [pltpu.VMEM(term.shape, jnp.bfloat16) for term in received],
        input_output_aliases={1 + len(operands): 0},
        compiler_params=pltpu.CompilerParams(vmem_limit_bytes=12 * mib),
        cost_estimate=small,
        name="place",
    )(*where, *operands)


def cut_kernel(whole_ref, *refs):
    rows = refs[0].shape[0]
    for part, ref in enumerate(refs):
        ref[...] = whole_ref[part * rows:(part + 1) * rows, :]


def cut(whole, count):
    if count == 1:
        return [whole]
    piece = jax.ShapeDtypeStruct((whole.shape[0] // count, whole.shape[1]), whole.dtype)
    return pl.pallas_call(
        cut_kernel,
        in_specs=[in_vmem],
        out_specs=[in_vmem] * count,
        out_shape=[piece] * count,
        compiler_params=pltpu.CompilerParams(vmem_limit_bytes=6 * mib),
        cost_estimate=small,
        name="cut",
    )(whole)


def after(array, *others):
    return lax.optimization_barrier((array, *others))[0]


def shards(blks, owners, grad_codes, scale_exps, val_grads, fisher):
    chips = blks // cores
    chips_per_owner = chips // owners
    me = lax.axis_index("dim")
    blk = lax.axis_index("blk")
    chip, core = blk // cores, lax.rem(blk, cores)[None]
    own, width = val_grads.shape
    count = grad_codes.shape[0]
    fisher = fisher[None, :]
    shape = (chips_per_owner, cores, own, count)

    ring = [*range(0, chips, 2), *reversed(range(1, chips, 2))]
    origin = [
        [ring[(ring.index(z) - hop) % chips] for z in range(chips)] for hop in range(chips)
    ]

    def shift(panel):
        pairs = [
            (ring[place] * cores + c, ring[(place + 1) % chips] * cores + c)
            for place in range(chips) for c in range(cores)
        ]
        return lax.ppermute(panel, "blk", pairs)

    def swap(parts):
        pairs = [(b, b ^ 1) for b in range(blks)]
        return [lax.ppermute(part, "blk", pairs) for part in parts]

    def exchange(send, by):
        received = []
        for step in range(1, owners):
            pairs = []
            for b in range(blks):
                owner = origin[by][b // cores] // chips_per_owner
                pairs.append((b * owners + (owner + step) % owners, b * owners + owner))
            received.append(lax.ppermute(send, ("blk", "dim"), pairs))
        return received

    def whose(by):
        source = sum(jnp.where(chip == z, origin[by][z], 0) for z in range(chips))
        mine = (source // chips_per_owner == me).astype(jnp.int32)[None]
        return mine, lax.rem(source, chips_per_owner)[None]

    hops = chips - 1
    flow = shift(val_grads)
    train, keep, send = first(core, val_grads, *swap([val_grads]), fisher, grad_codes, scale_exps)
    scores, kept = None, [keep]
    for hop in range(1, hops):
        received = exchange(send, hop - 1)
        panel = after(flow, send, *([] if scores is None else [scores]))
        if hop + 1 < hops:
            flow = shift(panel)
        else:
            low_piece, high_piece = cut(panel, 2)
            flow = shift(low_piece)
            panel = after(panel, low_piece)
        if hop > 1:
            panel = after(panel, *received)
        scores, send = multiply(
            scores, shape, whose(hop), core, [panel], swap([panel]), fisher, train, 0
        )
        received = [after(term, send) for term in received]
        scores = place(scores, whose(hop - 1), kept, received, [0] * len(received), 0)
        kept = []
    earlier = exchange(send, hops - 1)
    high_flow = shift(after(high_piece, send))
    low_piece = after(flow, send, scores)
    scores, send = multiply(
        scores, shape, whose(hops), core, [low_piece], swap(cut(low_piece, 2)), fisher, train, 0
    )
    received = exchange(send, hops)
    high_piece = after(high_flow, send, *earlier)
    high_other = swap([high_piece])
    knee = count * 5 // 8
    halves = []
    for top, bottom in ((0, knee), (knee, count)):
        if top:
            high_piece = after(high_piece, send, *received)
        scores, send = multiply(
            scores, shape, whose(hops), core, [high_piece], high_other, fisher, train, own // 2,
            (top, bottom),
        )
        halves.append(exchange(send, hops))
    earlier = [after(term, send) for term in earlier]
    scores = place(scores, whose(hops - 1), [], earlier, [0] * len(earlier), 0)
    received = [after(term, scores) for term in received]
    scores = place(scores, whose(hops), [], received, [0] * len(received), 0)
    cols = [0] * len(halves[0]) + [knee] * len(halves[1])
    scores = place(scores, whose(hops), [], halves[0] + halves[1], cols, own // 2)
    return scores.reshape(chips_per_owner * cores * own, count)


def solution(mesh):
    in_specs = (
        P(("groups", "blk"), "dim"),
        P(("groups", "blk"), "dim"),
        P(("groups", "blk"), "dim"),
        P("dim"),
    )
    out_specs = P("dim", ("groups", "blk"))
    body = functools.partial(shards, mesh.shape["blk"], mesh.shape["dim"])
    return jax.shard_map(body, mesh=mesh, in_specs=in_specs, out_specs=out_specs, check_vma=False)
```

```python
import functools

import jax
import jax.numpy as jnp
from jax import lax
from jax.experimental import pallas as pl
from jax.experimental.pallas import tpu as pltpu
from jax.sharding import PartitionSpec as P

damping = 0.05
lanes = 128
cores = 2
mib = 1 << 20
in_vmem = pl.BlockSpec(memory_space=pltpu.VMEM)
in_smem = pl.BlockSpec(memory_space=pltpu.SMEM)
anywhere = pl.BlockSpec(memory_space=pl.ANY)
small = pl.CostEstimate(flops=1, bytes_accessed=1, transcendentals=0)


def first_kernel(core_ref, mine_ref, other_ref, fisher_ref, codes_ref, exps_ref, train_ref, keep_ref,
                 send_ref, left, spread):
    rows, width = mine_ref.shape
    depth = min(width, 1024)
    core = core_ref[0]

    @pl.when(pl.program_id(0) == 0)
    def _():
        block = lax.broadcasted_iota(jnp.int32, spread.shape, 0)
        col = lax.broadcasted_iota(jnp.int32, spread.shape, 1)
        spread[...] = jnp.where(col // lanes == block, 1.0, 0.0).astype(jnp.bfloat16)
        for ref, place in ((mine_ref, core), (other_ref, 1 - core)):
            spot = pl.ds(pl.multiple_of(place * rows, rows), rows)
            for start in range(0, width, depth):
                cols = slice(start, start + depth)
                scale = 1.0 / (fisher_ref[:, cols] + damping)
                left[spot, cols] = (ref[:, cols].astype(jnp.float32) * scale).astype(jnp.bfloat16)

    exps = exps_ref[...]
    up = jnp.left_shift(1, jnp.maximum(exps, 0)).astype(jnp.float32)
    down = jnp.left_shift(1, jnp.maximum(-exps, 0)).astype(jnp.float32)
    factor = (up / down).astype(jnp.bfloat16)
    for start in range(0, width, depth):
        cols = slice(start, start + depth)
        wide = jnp.dot(factor, spread[:, cols], preferred_element_type=jnp.float32)
        train_ref[:, cols] = codes_ref[:, cols] * wide.astype(jnp.bfloat16)
    sums = lax.dot_general(
        left[...], train_ref[...], (((1,), (1,)), ((), ())), preferred_element_type=jnp.float32
    )
    keep_ref[...] = sums
    send_ref[...] = sums.astype(jnp.bfloat16)


def first(core, mine, other, fisher, codes, exps):
    rows, width = mine.shape
    count = codes.shape[0]
    blocks = width // lanes
    tile = min(count, 256)
    shape = (cores * rows, count)
    return pl.pallas_call(
        first_kernel,
        grid=(count // tile,),
        in_specs=[
            in_smem,
            pl.BlockSpec((rows, width), lambda i: (0, 0)),
            pl.BlockSpec((rows, width), lambda i: (0, 0)),
            pl.BlockSpec((1, width), lambda i: (0, 0)),
            pl.BlockSpec((tile, width), lambda i: (i, 0)),
            pl.BlockSpec((tile, blocks), lambda i: (i, 0)),
        ],
        out_specs=[
            pl.BlockSpec((tile, width), lambda i: (i, 0)),
            pl.BlockSpec((cores * rows, tile), lambda i: (0, i)),
            pl.BlockSpec((cores * rows, tile), lambda i: (0, i)),
        ],
        out_shape=[
            jax.ShapeDtypeStruct((count, width), jnp.bfloat16),
            jax.ShapeDtypeStruct(shape, jnp.float32),
            jax.ShapeDtypeStruct(shape, jnp.bfloat16),
        ],
        scratch_shapes=[
            pltpu.VMEM((cores * rows, width), jnp.bfloat16),
            pltpu.VMEM((blocks, width), jnp.bfloat16),
        ],
        compiler_params=pltpu.CompilerParams(vmem_limit_bytes=36 * mib),
        cost_estimate=small,
        name="first",
    )(core, mine, other, fisher, codes, exps)


def multiply_kernel(counts, start, top, mine_ref, spot_ref, core_ref, *refs):
    refs = list(refs)
    mine_refs, other_refs, _ = [[refs.pop(0) for _ in range(size)] for size in counts]
    fisher_ref, train_ref, scores_ref, send_ref = refs[:4]
    left, held, keep, send, train_sems, keep_sems, send_sems = refs[4:]
    rows = sum(ref.shape[0] for ref in mine_refs)
    slots, tile, width = held.shape
    tiles = keep_sems.shape[0]
    parts = train_sems.shape[1]
    share = tile // parts
    depth = min(width, 1024)
    core = core_ref[0]

    def fetches(i):
        slot = lax.rem(i, slots)
        return [
            pltpu.make_async_copy(
                train_ref.at[pl.ds(pl.multiple_of(i * tile, tile) + top + part * share, share)],
                held.at[slot, pl.ds(part * share, share)],
                train_sems.at[slot, part],
            )
            for part in range(parts)
        ]

    for i in range(min(slots, tiles)):
        for fetch in fetches(i):
            fetch.start()

    @pl.loop(0, width // depth)
    def _(k):
        cols = pl.ds(pl.multiple_of(k * depth, depth), depth)
        scale = 1.0 / (fisher_ref[:, cols] + damping)
        for group, place in ((mine_refs, core), (other_refs, 1 - core)):
            offset = 0
            for ref in group:
                spot = pl.ds(pl.multiple_of(place * rows, rows) + offset, ref.shape[0])
                left[spot, cols] = (ref[:, cols].astype(jnp.float32) * scale).astype(jnp.bfloat16)
                offset += ref.shape[0]

    def stores(i, of_mine):
        slot = lax.rem(i, 2)
        cols = pl.ds(pl.multiple_of(i * tile, tile), tile)
        if not of_mine:
            return [pltpu.make_async_copy(send.at[slot], send_ref.at[:, cols], send_sems.at[i])]
        return [
            pltpu.make_async_copy(
                keep.at[slot, pl.ds(c * rows, rows)],
                scores_ref.at[
                    spot_ref[0], c, pl.ds(start, rows),
                    pl.ds(pl.multiple_of(i * tile, tile) + top, tile),
                ],
                keep_sems.at[i, c],
            )
            for c in range(cores)
        ]

    def wait_stores(i):
        for flag in (0, 1):
            @pl.when(mine_ref[0] == flag)
            def _():
                for store in stores(i, flag):
                    store.wait()

    @pl.loop(0, tiles)
    def _(i):
        for fetch in fetches(i):
            fetch.wait()
        block = held[lax.rem(i, slots)]
        if cores * rows <= 128:
            sums = lax.dot_general(
                block, left[...], (((1,), (1,)), ((), ())), preferred_element_type=jnp.float32
            ).T
        else:
            sums = lax.dot_general(
                left[...], block, (((1,), (1,)), ((), ())), preferred_element_type=jnp.float32
            )

        @pl.when(i >= 2)
        def _():
            wait_stores(i - 2)

        @pl.when(mine_ref[0] == 1)
        def _():
            keep[lax.rem(i, 2)] = sums
            for store in stores(i, True):
                store.start()

        @pl.when(mine_ref[0] == 0)
        def _():
            send[lax.rem(i, 2)] = sums.astype(jnp.bfloat16)
            for store in stores(i, False):
                store.start()

        @pl.when(i + slots < tiles)
        def _():
            for fetch in fetches(i + slots):
                fetch.start()

    for i in range(max(tiles - 2, 0), tiles):
        wait_stores(i)


def multiply(scores, shape, where, core, mine, other, fisher, train, start, span=None):
    rows = sum(part.shape[0] for part in mine)
    width = mine[0].shape[1]
    top, bottom = span or (0, train.shape[0])
    count = bottom - top
    tile = min(count, 256)
    slots = 3
    block = (cores * rows, count)
    given = [] if scores is None else [scores]
    counts = (len(mine), len(other), len(given))
    return pl.pallas_call(
        functools.partial(multiply_kernel, counts, start, top),
        in_specs=[in_smem] * 3 + [in_vmem] * sum(counts[:2]) + [anywhere] * len(given) + [in_vmem, anywhere],
        out_specs=[anywhere] * 2,
        out_shape=[
            jax.ShapeDtypeStruct(shape, jnp.float32), jax.ShapeDtypeStruct(block, jnp.bfloat16),
        ],
        scratch_shapes=[
            pltpu.VMEM((cores * rows, width), jnp.bfloat16),
            pltpu.VMEM((slots, tile, width), jnp.bfloat16),
            pltpu.VMEM((2, cores * rows, tile), jnp.float32),
            pltpu.VMEM((2, cores * rows, tile), jnp.bfloat16),
            pltpu.SemaphoreType.DMA((slots, 4)),
            pltpu.SemaphoreType.DMA((count // tile, cores)),
            pltpu.SemaphoreType.DMA((count // tile,)),
        ],
        input_output_aliases={3 + len(mine) + len(other): 0} if given else {},
        compiler_params=pltpu.CompilerParams(vmem_limit_bytes=22 * mib),
        cost_estimate=small,
        name="multiply",
    )(*where, core, *mine, *other, *given, fisher, train)


def place_kernel(start, cols, kept, mine_ref, spot_ref, *refs):
    first_ref, received = refs[:kept], refs[kept:kept + len(cols)]
    scores_ref, total, in_sems, out_sems, *terms = refs[kept + len(cols) + 1:]
    rows = total.shape[0] // cores

    def own(c):
        return scores_ref.at[spot_ref[0], c, pl.ds(start, rows)]

    @pl.when(mine_ref[0] == 1)
    def _():
        if kept:
            loads = [pltpu.make_async_copy(first_ref[0], total, in_sems.at[0])]
        else:
            loads = [
                pltpu.make_async_copy(own(c), total.at[pl.ds(c * rows, rows)], in_sems.at[c])
                for c in range(cores)
            ]
        for index, ref in enumerate(received):
            loads.append(pltpu.make_async_copy(ref, terms[index], in_sems.at[cores + index]))
        for load in loads:
            load.start()
        for load in loads:
            load.wait()
        for col, term in zip(cols, terms):
            span = slice(col, col + term.shape[1])
            total[:, span] += term[...].astype(jnp.float32)
        copies = [
            pltpu.make_async_copy(total.at[pl.ds(c * rows, rows)], own(c), out_sems.at[c])
            for c in range(cores)
        ]
        for copy in copies:
            copy.start()
        for copy in copies:
            copy.wait()


def place(scores, where, kept, received, cols, start):
    count = scores.shape[-1]
    rows = received[0].shape[0]
    operands = [*kept, *received, scores]
    return pl.pallas_call(
        functools.partial(place_kernel, start, cols, len(kept)),
        in_specs=[in_smem] * 2 + [anywhere] * len(operands),
        out_specs=anywhere,
        out_shape=jax.ShapeDtypeStruct(scores.shape, jnp.float32),
        scratch_shapes=[
            pltpu.VMEM((rows, count), jnp.float32),
            pltpu.SemaphoreType.DMA((cores + len(received),)),
            pltpu.SemaphoreType.DMA((cores,)),
        ] + [pltpu.VMEM(term.shape, jnp.bfloat16) for term in received],
        input_output_aliases={1 + len(operands): 0},
        compiler_params=pltpu.CompilerParams(vmem_limit_bytes=12 * mib),
        cost_estimate=small,
        name="place",
    )(*where, *operands)


def cut_kernel(whole_ref, *refs):
    rows = refs[0].shape[0]
    for part, ref in enumerate(refs):
        ref[...] = whole_ref[part * rows:(part + 1) * rows, :]


def cut(whole, count):
    if count == 1:
        return [whole]
    piece = jax.ShapeDtypeStruct((whole.shape[0] // count, whole.shape[1]), whole.dtype)
    return pl.pallas_call(
        cut_kernel,
        in_specs=[in_vmem],
        out_specs=[in_vmem] * count,
        out_shape=[piece] * count,
        compiler_params=pltpu.CompilerParams(vmem_limit_bytes=6 * mib),
        cost_estimate=small,
        name="cut",
    )(whole)


def after(array, *others):
    return lax.optimization_barrier((array, *others))[0]


def shards(blks, owners, grad_codes, scale_exps, val_grads, fisher):
    chips = blks // cores
    chips_per_owner = chips // owners
    me = lax.axis_index("dim")
    blk = lax.axis_index("blk")
    chip, core = blk // cores, lax.rem(blk, cores)[None]
    own, width = val_grads.shape
    count = grad_codes.shape[0]
    fisher = fisher[None, :]
    shape = (chips_per_owner, cores, own, count)

    ring = [*range(0, chips, 2), *reversed(range(1, chips, 2))]
    origin = [
        [ring[(ring.index(z) - hop) % chips] for z in range(chips)] for hop in range(chips)
    ]

    def shift(panel):
        pairs = [
            (ring[place] * cores + c, ring[(place + 1) % chips] * cores + c)
            for place in range(chips) for c in range(cores)
        ]
        return lax.ppermute(panel, "blk", pairs)

    def swap(parts):
        pairs = [(b, b ^ 1) for b in range(blks)]
        return [lax.ppermute(part, "blk", pairs) for part in parts]

    def exchange(send, by):
        received = []
        for step in range(1, owners):
            pairs = []
            for b in range(blks):
                owner = origin[by][b // cores] // chips_per_owner
                pairs.append((b * owners + (owner + step) % owners, b * owners + owner))
            received.append(lax.ppermute(send, ("blk", "dim"), pairs))
        return received

    def whose(by):
        source = sum(jnp.where(chip == z, origin[by][z], 0) for z in range(chips))
        mine = (source // chips_per_owner == me).astype(jnp.int32)[None]
        return mine, lax.rem(source, chips_per_owner)[None]

    hops = chips - 1
    flow = shift(val_grads)
    train, keep, send = first(core, val_grads, *swap([val_grads]), fisher, grad_codes, scale_exps)
    scores, kept = None, [keep]
    for hop in range(1, hops):
        received = exchange(send, hop - 1)
        panel = after(flow, send, *([] if scores is None else [scores]))
        if hop + 1 < hops:
            flow = shift(panel)
        else:
            low_piece, high_piece = cut(panel, 2)
            flow = shift(low_piece)
            panel = after(panel, low_piece)
        if hop > 1:
            panel = after(panel, *received)
        scores, send = multiply(
            scores, shape, whose(hop), core, [panel], swap([panel]), fisher, train, 0
        )
        received = [after(term, send) for term in received]
        scores = place(scores, whose(hop - 1), kept, received, [0] * len(received), 0)
        kept = []
    earlier = exchange(send, hops - 1)
    high_flow = shift(after(high_piece, send))
    low_piece = after(flow, send, scores)
    scores, send = multiply(
        scores, shape, whose(hops), core, [low_piece], swap(cut(low_piece, 2)), fisher, train, 0
    )
    received = exchange(send, hops)
    high_piece = after(high_flow, send, *earlier)
    high_other = swap([high_piece])
    knee = count * 5 // 8
    halves = []
    for top, bottom in ((0, knee), (knee, count)):
        if top:
            high_piece = after(high_piece, send, *received)
        scores, send = multiply(
            scores, shape, whose(hops), core, [high_piece], high_other, fisher, train, own // 2,
            (top, bottom),
        )
        halves.append(exchange(send, hops))
    earlier = [after(term, send) for term in earlier]
    scores = place(scores, whose(hops - 1), [], earlier, [0] * len(earlier), 0)
    received = [after(term, scores) for term in received]
    scores = place(scores, whose(hops), [], received, [0] * len(received), 0)
    cols = [0] * len(halves[0]) + [knee] * len(halves[1])
    scores = place(scores, whose(hops), [], halves[0] + halves[1], cols, own // 2)
    return scores.reshape(chips_per_owner * cores * own, count)


def solution(mesh):
    in_specs = (
        P(("groups", "blk"), "dim"),
        P(("groups", "blk"), "dim"),
        P(("groups", "blk"), "dim"),
        P("dim"),
    )
    out_specs = P("dim", ("groups", "blk"))
    body = functools.partial(shards, mesh.shape["blk"], mesh.shape["dim"])
    return jax.shard_map(body, mesh=mesh, in_specs=in_specs, out_specs=out_specs, check_vma=False)
```

```python
import functools

import jax
import jax.numpy as jnp
from jax import lax
from jax.experimental import pallas as pl
from jax.experimental.pallas import tpu as pltpu
from jax.sharding import PartitionSpec as P

damping = 0.05
lanes = 128
cores = 2
mib = 1 << 20
in_vmem = pl.BlockSpec(memory_space=pltpu.VMEM)
in_smem = pl.BlockSpec(memory_space=pltpu.SMEM)
anywhere = pl.BlockSpec(memory_space=pl.ANY)
small = pl.CostEstimate(flops=1, bytes_accessed=1, transcendentals=0)


def first_kernel(core_ref, mine_ref, other_ref, fisher_ref, codes_ref, exps_ref, train_ref, keep_ref,
                 send_ref, left, spread):
    rows, width = mine_ref.shape
    depth = min(width, 1024)
    core = core_ref[0]

    @pl.when(pl.program_id(0) == 0)
    def _():
        block = lax.broadcasted_iota(jnp.int32, spread.shape, 0)
        col = lax.broadcasted_iota(jnp.int32, spread.shape, 1)
        spread[...] = jnp.where(col // lanes == block, 1.0, 0.0).astype(jnp.bfloat16)
        for ref, place in ((mine_ref, core), (other_ref, 1 - core)):
            spot = pl.ds(pl.multiple_of(place * rows, rows), rows)
            for start in range(0, width, depth):
                cols = slice(start, start + depth)
                scale = 1.0 / (fisher_ref[:, cols] + damping)
                left[spot, cols] = (ref[:, cols].astype(jnp.float32) * scale).astype(jnp.bfloat16)

    exps = exps_ref[...]
    up = jnp.left_shift(1, jnp.maximum(exps, 0)).astype(jnp.float32)
    down = jnp.left_shift(1, jnp.maximum(-exps, 0)).astype(jnp.float32)
    factor = (up / down).astype(jnp.bfloat16)
    for start in range(0, width, depth):
        cols = slice(start, start + depth)
        wide = jnp.dot(factor, spread[:, cols], preferred_element_type=jnp.float32)
        train_ref[:, cols] = codes_ref[:, cols] * wide.astype(jnp.bfloat16)
    sums = lax.dot_general(
        left[...], train_ref[...], (((1,), (1,)), ((), ())), preferred_element_type=jnp.float32
    )
    keep_ref[...] = sums
    send_ref[...] = sums.astype(jnp.bfloat16)


def first(core, mine, other, fisher, codes, exps):
    rows, width = mine.shape
    count = codes.shape[0]
    blocks = width // lanes
    tile = min(count, 256)
    shape = (cores * rows, count)
    return pl.pallas_call(
        first_kernel,
        grid=(count // tile,),
        in_specs=[
            in_smem,
            pl.BlockSpec((rows, width), lambda i: (0, 0)),
            pl.BlockSpec((rows, width), lambda i: (0, 0)),
            pl.BlockSpec((1, width), lambda i: (0, 0)),
            pl.BlockSpec((tile, width), lambda i: (i, 0)),
            pl.BlockSpec((tile, blocks), lambda i: (i, 0)),
        ],
        out_specs=[
            pl.BlockSpec((tile, width), lambda i: (i, 0)),
            pl.BlockSpec((cores * rows, tile), lambda i: (0, i)),
            pl.BlockSpec((cores * rows, tile), lambda i: (0, i)),
        ],
        out_shape=[
            jax.ShapeDtypeStruct((count, width), jnp.bfloat16),
            jax.ShapeDtypeStruct(shape, jnp.float32),
            jax.ShapeDtypeStruct(shape, jnp.bfloat16),
        ],
        scratch_shapes=[
            pltpu.VMEM((cores * rows, width), jnp.bfloat16),
            pltpu.VMEM((blocks, width), jnp.bfloat16),
        ],
        compiler_params=pltpu.CompilerParams(vmem_limit_bytes=36 * mib),
        cost_estimate=small,
        name="first",
    )(core, mine, other, fisher, codes, exps)


def multiply_kernel(counts, start, top, mine_ref, spot_ref, core_ref, *refs):
    refs = list(refs)
    mine_refs, other_refs, _ = [[refs.pop(0) for _ in range(size)] for size in counts]
    fisher_ref, train_ref, scores_ref, send_ref = refs[:4]
    left, held, keep, send, train_sems, keep_sems, send_sems = refs[4:]
    rows = sum(ref.shape[0] for ref in mine_refs)
    slots, tile, width = held.shape
    tiles = keep_sems.shape[0]
    parts = train_sems.shape[1]
    share = tile // parts
    depth = min(width, 1024)
    core = core_ref[0]

    def fetches(i):
        slot = lax.rem(i, slots)
        return [
            pltpu.make_async_copy(
                train_ref.at[pl.ds(pl.multiple_of(i * tile, tile) + top + part * share, share)],
                held.at[slot, pl.ds(part * share, share)],
                train_sems.at[slot, part],
            )
            for part in range(parts)
        ]

    for i in range(min(slots, tiles)):
        for fetch in fetches(i):
            fetch.start()

    @pl.loop(0, width // depth)
    def _(k):
        cols = pl.ds(pl.multiple_of(k * depth, depth), depth)
        scale = 1.0 / (fisher_ref[:, cols] + damping)
        for group, place in ((mine_refs, core), (other_refs, 1 - core)):
            offset = 0
            for ref in group:
                spot = pl.ds(pl.multiple_of(place * rows, rows) + offset, ref.shape[0])
                left[spot, cols] = (ref[:, cols].astype(jnp.float32) * scale).astype(jnp.bfloat16)
                offset += ref.shape[0]

    def stores(i, of_mine):
        slot = lax.rem(i, 2)
        cols = pl.ds(pl.multiple_of(i * tile, tile), tile)
        if not of_mine:
            return [pltpu.make_async_copy(send.at[slot], send_ref.at[:, cols], send_sems.at[i])]
        return [
            pltpu.make_async_copy(
                keep.at[slot, pl.ds(c * rows, rows)],
                scores_ref.at[
                    spot_ref[0], c, pl.ds(start, rows),
                    pl.ds(pl.multiple_of(i * tile, tile) + top, tile),
                ],
                keep_sems.at[i, c],
            )
            for c in range(cores)
        ]

    def wait_stores(i):
        for flag in (0, 1):
            @pl.when(mine_ref[0] == flag)
            def _():
                for store in stores(i, flag):
                    store.wait()

    @pl.loop(0, tiles)
    def _(i):
        for fetch in fetches(i):
            fetch.wait()
        block = held[lax.rem(i, slots)]
        if cores * rows <= 128:
            sums = lax.dot_general(
                block, left[...], (((1,), (1,)), ((), ())), preferred_element_type=jnp.float32
            ).T
        else:
            sums = lax.dot_general(
                left[...], block, (((1,), (1,)), ((), ())), preferred_element_type=jnp.float32
            )

        @pl.when(i >= 2)
        def _():
            wait_stores(i - 2)

        @pl.when(mine_ref[0] == 1)
        def _():
            keep[lax.rem(i, 2)] = sums
            for store in stores(i, True):
                store.start()

        @pl.when(mine_ref[0] == 0)
        def _():
            send[lax.rem(i, 2)] = sums.astype(jnp.bfloat16)
            for store in stores(i, False):
                store.start()

        @pl.when(i + slots < tiles)
        def _():
            for fetch in fetches(i + slots):
                fetch.start()

    for i in range(max(tiles - 2, 0), tiles):
        wait_stores(i)


def multiply(scores, shape, where, core, mine, other, fisher, train, start, span=None):
    rows = sum(part.shape[0] for part in mine)
    width = mine[0].shape[1]
    top, bottom = span or (0, train.shape[0])
    count = bottom - top
    tile = min(count, 256)
    slots = 3
    block = (cores * rows, count)
    given = [] if scores is None else [scores]
    counts = (len(mine), len(other), len(given))
    return pl.pallas_call(
        functools.partial(multiply_kernel, counts, start, top),
        in_specs=[in_smem] * 3 + [in_vmem] * sum(counts[:2]) + [anywhere] * len(given) + [in_vmem, anywhere],
        out_specs=[anywhere] * 2,
        out_shape=[
            jax.ShapeDtypeStruct(shape, jnp.float32), jax.ShapeDtypeStruct(block, jnp.bfloat16),
        ],
        scratch_shapes=[
            pltpu.VMEM((cores * rows, width), jnp.bfloat16),
            pltpu.VMEM((slots, tile, width), jnp.bfloat16),
            pltpu.VMEM((2, cores * rows, tile), jnp.float32),
            pltpu.VMEM((2, cores * rows, tile), jnp.bfloat16),
            pltpu.SemaphoreType.DMA((slots, 4)),
            pltpu.SemaphoreType.DMA((count // tile, cores)),
            pltpu.SemaphoreType.DMA((count // tile,)),
        ],
        input_output_aliases={3 + len(mine) + len(other): 0} if given else {},
        compiler_params=pltpu.CompilerParams(vmem_limit_bytes=22 * mib),
        cost_estimate=small,
        name="multiply",
    )(*where, core, *mine, *other, *given, fisher, train)


def place_kernel(start, cols, kept, mine_ref, spot_ref, *refs):
    first_ref, received = refs[:kept], refs[kept:kept + len(cols)]
    scores_ref, total, in_sems, out_sems, *terms = refs[kept + len(cols) + 1:]
    rows = total.shape[0] // cores

    def own(c):
        return scores_ref.at[spot_ref[0], c, pl.ds(start, rows)]

    @pl.when(mine_ref[0] == 1)
    def _():
        if kept:
            loads = [pltpu.make_async_copy(first_ref[0], total, in_sems.at[0])]
        else:
            loads = [
                pltpu.make_async_copy(own(c), total.at[pl.ds(c * rows, rows)], in_sems.at[c])
                for c in range(cores)
            ]
        for index, ref in enumerate(received):
            loads.append(pltpu.make_async_copy(ref, terms[index], in_sems.at[cores + index]))
        for load in loads:
            load.start()
        for load in loads:
            load.wait()
        for col, term in zip(cols, terms):
            span = slice(col, col + term.shape[1])
            total[:, span] += term[...].astype(jnp.float32)
        copies = [
            pltpu.make_async_copy(total.at[pl.ds(c * rows, rows)], own(c), out_sems.at[c])
            for c in range(cores)
        ]
        for copy in copies:
            copy.start()
        for copy in copies:
            copy.wait()


def place(scores, where, kept, received, cols, start):
    count = scores.shape[-1]
    rows = received[0].shape[0]
    operands = [*kept, *received, scores]
    return pl.pallas_call(
        functools.partial(place_kernel, start, cols, len(kept)),
        in_specs=[in_smem] * 2 + [anywhere] * len(operands),
        out_specs=anywhere,
        out_shape=jax.ShapeDtypeStruct(scores.shape, jnp.float32),
        scratch_shapes=[
            pltpu.VMEM((rows, count), jnp.float32),
            pltpu.SemaphoreType.DMA((cores + len(received),)),
            pltpu.SemaphoreType.DMA((cores,)),
        ] + [pltpu.VMEM(term.shape, jnp.bfloat16) for term in received],
        input_output_aliases={1 + len(operands): 0},
        compiler_params=pltpu.CompilerParams(vmem_limit_bytes=12 * mib),
        cost_estimate=small,
        name="place",
    )(*where, *operands)


def cut_kernel(whole_ref, *refs):
    rows = refs[0].shape[0]
    for part, ref in enumerate(refs):
        ref[...] = whole_ref[part * rows:(part + 1) * rows, :]


def cut(whole, count):
    if count == 1:
        return [whole]
    piece = jax.ShapeDtypeStruct((whole.shape[0] // count, whole.shape[1]), whole.dtype)
    return pl.pallas_call(
        cut_kernel,
        in_specs=[in_vmem],
        out_specs=[in_vmem] * count,
        out_shape=[piece] * count,
        compiler_params=pltpu.CompilerParams(vmem_limit_bytes=6 * mib),
        cost_estimate=small,
        name="cut",
    )(whole)


def after(array, *others):
    return lax.optimization_barrier((array, *others))[0]


def shards(blks, owners, grad_codes, scale_exps, val_grads, fisher):
    chips = blks // cores
    chips_per_owner = chips // owners
    me = lax.axis_index("dim")
    blk = lax.axis_index("blk")
    chip, core = blk // cores, lax.rem(blk, cores)[None]
    own, width = val_grads.shape
    count = grad_codes.shape[0]
    fisher = fisher[None, :]
    shape = (chips_per_owner, cores, own, count)

    ring = [*range(0, chips, 2), *reversed(range(1, chips, 2))]
    origin = [
        [ring[(ring.index(z) - hop) % chips] for z in range(chips)] for hop in range(chips)
    ]

    def shift(panel, by=1):
        pairs = [
            (ring[place] * cores + c, ring[(place + by) % chips] * cores + c)
            for place in range(chips) for c in range(cores)
        ]
        return lax.ppermute(panel, "blk", pairs)

    def swap(parts):
        pairs = [(b, b ^ 1) for b in range(blks)]
        return [lax.ppermute(part, "blk", pairs) for part in parts]

    def exchange(send, by):
        received = []
        for step in range(1, owners):
            pairs = []
            for b in range(blks):
                owner = origin[by][b // cores] // chips_per_owner
                pairs.append((b * owners + (owner + step) % owners, b * owners + owner))
            received.append(lax.ppermute(send, ("blk", "dim"), pairs))
        return received

    def whose(by):
        source = sum(jnp.where(chip == z, origin[by][z], 0) for z in range(chips))
        mine = (source // chips_per_owner == me).astype(jnp.int32)[None]
        return mine, lax.rem(source, chips_per_owner)[None]

    hops = chips - 1
    flow = shift(val_grads)
    train, keep, send = first(core, val_grads, *swap([val_grads]), fisher, grad_codes, scale_exps)
    low_piece, high_piece = cut(after(val_grads, send), 2)
    scores, kept = None, [keep]
    for hop in range(1, hops):
        received = exchange(send, hop - 1)
        panel = after(flow, send, *([] if scores is None else [scores, low_piece]))
        if hop + 1 < hops:
            flow = shift(panel)
        else:
            flow = shift(after(low_piece, panel), -1)
        if hop > 1:
            panel = after(panel, *received)
        scores, send = multiply(
            scores, shape, whose(hop), core, [panel], swap([panel]), fisher, train, 0
        )
        received = [after(term, send) for term in received]
        scores = place(scores, whose(hop - 1), kept, received, [0] * len(received), 0)
        kept = []
    earlier = exchange(send, hops - 1)
    high_flow = shift(after(high_piece, send), -1)
    low_piece = after(flow, send, scores)
    scores, send = multiply(
        scores, shape, whose(hops), core, [low_piece], swap(cut(low_piece, 2)), fisher, train, 0
    )
    received = exchange(send, hops)
    high_piece = after(high_flow, send, *earlier)
    high_other = swap(cut(high_piece, max(1, min(4, high_piece.shape[0] // 16))))
    knee = count * 5 // 8
    halves = []
    for top, bottom in ((0, knee), (knee, count)):
        if top:
            high_piece = after(high_piece, send, *received)
        scores, send = multiply(
            scores, shape, whose(hops), core, [high_piece], high_other, fisher, train, own // 2,
            (top, bottom),
        )
        halves.append(exchange(send, hops))
    earlier = [after(term, send) for term in earlier]
    scores = place(scores, whose(hops - 1), [], earlier, [0] * len(earlier), 0)
    received = [after(term, scores) for term in received]
    scores = place(scores, whose(hops), [], received, [0] * len(received), 0)
    cols = [0] * len(halves[0]) + [knee] * len(halves[1])
    scores = place(scores, whose(hops), [], halves[0] + halves[1], cols, own // 2)
    return scores.reshape(chips_per_owner * cores * own, count)


def solution(mesh):
    in_specs = (
        P(("groups", "blk"), "dim"),
        P(("groups", "blk"), "dim"),
        P(("groups", "blk"), "dim"),
        P("dim"),
    )
    out_specs = P("dim", ("groups", "blk"))
    body = functools.partial(shards, mesh.shape["blk"], mesh.shape["dim"])
    return jax.shard_map(body, mesh=mesh, in_specs=in_specs, out_specs=out_specs, check_vma=False)
```

```python
import functools

import jax
import jax.numpy as jnp
from jax import lax
from jax.experimental import pallas as pl
from jax.experimental.pallas import tpu as pltpu
from jax.sharding import PartitionSpec as P

damping = 0.05
lanes = 128
cores = 2
mib = 1 << 20
in_vmem = pl.BlockSpec(memory_space=pltpu.VMEM)
in_smem = pl.BlockSpec(memory_space=pltpu.SMEM)
anywhere = pl.BlockSpec(memory_space=pl.ANY)
small = pl.CostEstimate(flops=1, bytes_accessed=1, transcendentals=0)


def first_kernel(core_ref, mine_ref, other_ref, fisher_ref, codes_ref, exps_ref, train_ref, keep_ref,
                 send_ref, left, spread):
    rows, width = mine_ref.shape
    depth = min(width, 1024)
    core = core_ref[0]

    @pl.when(pl.program_id(0) == 0)
    def _():
        block = lax.broadcasted_iota(jnp.int32, spread.shape, 0)
        col = lax.broadcasted_iota(jnp.int32, spread.shape, 1)
        spread[...] = jnp.where(col // lanes == block, 1.0, 0.0).astype(jnp.bfloat16)
        for ref, place in ((mine_ref, core), (other_ref, 1 - core)):
            spot = pl.ds(pl.multiple_of(place * rows, rows), rows)
            for start in range(0, width, depth):
                cols = slice(start, start + depth)
                scale = 1.0 / (fisher_ref[:, cols] + damping)
                left[spot, cols] = (ref[:, cols].astype(jnp.float32) * scale).astype(jnp.bfloat16)

    exps = exps_ref[...]
    up = jnp.left_shift(1, jnp.maximum(exps, 0)).astype(jnp.float32)
    down = jnp.left_shift(1, jnp.maximum(-exps, 0)).astype(jnp.float32)
    factor = (up / down).astype(jnp.bfloat16)
    for start in range(0, width, depth):
        cols = slice(start, start + depth)
        wide = jnp.dot(factor, spread[:, cols], preferred_element_type=jnp.float32)
        train_ref[:, cols] = codes_ref[:, cols] * wide.astype(jnp.bfloat16)
    sums = lax.dot_general(
        left[...], train_ref[...], (((1,), (1,)), ((), ())), preferred_element_type=jnp.float32
    )
    keep_ref[...] = sums
    send_ref[...] = sums.astype(jnp.bfloat16)


def first(core, mine, other, fisher, codes, exps):
    rows, width = mine.shape
    count = codes.shape[0]
    blocks = width // lanes
    tile = min(count, 256)
    shape = (cores * rows, count)
    return pl.pallas_call(
        first_kernel,
        grid=(count // tile,),
        in_specs=[
            in_smem,
            pl.BlockSpec((rows, width), lambda i: (0, 0)),
            pl.BlockSpec((rows, width), lambda i: (0, 0)),
            pl.BlockSpec((1, width), lambda i: (0, 0)),
            pl.BlockSpec((tile, width), lambda i: (i, 0)),
            pl.BlockSpec((tile, blocks), lambda i: (i, 0)),
        ],
        out_specs=[
            pl.BlockSpec((tile, width), lambda i: (i, 0)),
            pl.BlockSpec((cores * rows, tile), lambda i: (0, i)),
            pl.BlockSpec((cores * rows, tile), lambda i: (0, i)),
        ],
        out_shape=[
            jax.ShapeDtypeStruct((count, width), jnp.bfloat16),
            jax.ShapeDtypeStruct(shape, jnp.float32),
            jax.ShapeDtypeStruct(shape, jnp.bfloat16),
        ],
        scratch_shapes=[
            pltpu.VMEM((cores * rows, width), jnp.bfloat16),
            pltpu.VMEM((blocks, width), jnp.bfloat16),
        ],
        compiler_params=pltpu.CompilerParams(vmem_limit_bytes=36 * mib),
        cost_estimate=small,
        name="first",
    )(core, mine, other, fisher, codes, exps)


def multiply_kernel(counts, start, top, mine_ref, spot_ref, core_ref, *refs):
    refs = list(refs)
    mine_refs, other_refs, _ = [[refs.pop(0) for _ in range(size)] for size in counts]
    fisher_ref, train_ref, scores_ref, send_ref = refs[:4]
    left, held, keep, send, train_sems, keep_sems, send_sems = refs[4:]
    rows = sum(ref.shape[0] for ref in mine_refs)
    slots, tile, width = held.shape
    tiles = keep_sems.shape[0]
    parts = train_sems.shape[1]
    share = tile // parts
    depth = min(width, 1024)
    core = core_ref[0]

    def fetches(i):
        slot = lax.rem(i, slots)
        return [
            pltpu.make_async_copy(
                train_ref.at[pl.ds(pl.multiple_of(i * tile, tile) + top + part * share, share)],
                held.at[slot, pl.ds(part * share, share)],
                train_sems.at[slot, part],
            )
            for part in range(parts)
        ]

    for i in range(min(slots, tiles)):
        for fetch in fetches(i):
            fetch.start()

    @pl.loop(0, width // depth)
    def _(k):
        cols = pl.ds(pl.multiple_of(k * depth, depth), depth)
        scale = 1.0 / (fisher_ref[:, cols] + damping)
        for group, place in ((mine_refs, core), (other_refs, 1 - core)):
            offset = 0
            for ref in group:
                spot = pl.ds(pl.multiple_of(place * rows, rows) + offset, ref.shape[0])
                left[spot, cols] = (ref[:, cols].astype(jnp.float32) * scale).astype(jnp.bfloat16)
                offset += ref.shape[0]

    def stores(i, of_mine):
        slot = lax.rem(i, 2)
        cols = pl.ds(pl.multiple_of(i * tile, tile), tile)
        if not of_mine:
            return [pltpu.make_async_copy(send.at[slot], send_ref.at[:, cols], send_sems.at[i])]
        return [
            pltpu.make_async_copy(
                keep.at[slot, pl.ds(c * rows, rows)],
                scores_ref.at[
                    spot_ref[0], c, pl.ds(start, rows),
                    pl.ds(pl.multiple_of(i * tile, tile) + top, tile),
                ],
                keep_sems.at[i, c],
            )
            for c in range(cores)
        ]

    def wait_stores(i):
        for flag in (0, 1):
            @pl.when(mine_ref[0] == flag)
            def _():
                for store in stores(i, flag):
                    store.wait()

    @pl.loop(0, tiles)
    def _(i):
        for fetch in fetches(i):
            fetch.wait()
        block = held[lax.rem(i, slots)]
        if cores * rows <= 128:
            sums = lax.dot_general(
                block, left[...], (((1,), (1,)), ((), ())), preferred_element_type=jnp.float32
            ).T
        else:
            sums = lax.dot_general(
                left[...], block, (((1,), (1,)), ((), ())), preferred_element_type=jnp.float32
            )

        @pl.when(i >= 2)
        def _():
            wait_stores(i - 2)

        @pl.when(mine_ref[0] == 1)
        def _():
            keep[lax.rem(i, 2)] = sums
            for store in stores(i, True):
                store.start()

        @pl.when(mine_ref[0] == 0)
        def _():
            send[lax.rem(i, 2)] = sums.astype(jnp.bfloat16)
            for store in stores(i, False):
                store.start()

        @pl.when(i + slots < tiles)
        def _():
            for fetch in fetches(i + slots):
                fetch.start()

    for i in range(max(tiles - 2, 0), tiles):
        wait_stores(i)


def multiply(scores, shape, where, core, mine, other, fisher, train, start, span=None):
    rows = sum(part.shape[0] for part in mine)
    width = mine[0].shape[1]
    top, bottom = span or (0, train.shape[0])
    count = bottom - top
    tile = min(count, 256)
    slots = 3
    block = (cores * rows, count)
    given = [] if scores is None else [scores]
    counts = (len(mine), len(other), len(given))
    return pl.pallas_call(
        functools.partial(multiply_kernel, counts, start, top),
        in_specs=[in_smem] * 3 + [in_vmem] * sum(counts[:2]) + [anywhere] * len(given) + [in_vmem, anywhere],
        out_specs=[anywhere] * 2,
        out_shape=[
            jax.ShapeDtypeStruct(shape, jnp.float32), jax.ShapeDtypeStruct(block, jnp.bfloat16),
        ],
        scratch_shapes=[
            pltpu.VMEM((cores * rows, width), jnp.bfloat16),
            pltpu.VMEM((slots, tile, width), jnp.bfloat16),
            pltpu.VMEM((2, cores * rows, tile), jnp.float32),
            pltpu.VMEM((2, cores * rows, tile), jnp.bfloat16),
            pltpu.SemaphoreType.DMA((slots, 4)),
            pltpu.SemaphoreType.DMA((count // tile, cores)),
            pltpu.SemaphoreType.DMA((count // tile,)),
        ],
        input_output_aliases={3 + len(mine) + len(other): 0} if given else {},
        compiler_params=pltpu.CompilerParams(vmem_limit_bytes=22 * mib),
        cost_estimate=small,
        name="multiply",
    )(*where, core, *mine, *other, *given, fisher, train)


def place_kernel(start, cols, kept, mine_ref, spot_ref, *refs):
    first_ref, received = refs[:kept], refs[kept:kept + len(cols)]
    scores_ref, total, in_sems, out_sems, *terms = refs[kept + len(cols) + 1:]
    rows = total.shape[0] // cores

    def own(c):
        return scores_ref.at[spot_ref[0], c, pl.ds(start, rows)]

    @pl.when(mine_ref[0] == 1)
    def _():
        if kept:
            loads = [pltpu.make_async_copy(first_ref[0], total, in_sems.at[0])]
        else:
            loads = [
                pltpu.make_async_copy(own(c), total.at[pl.ds(c * rows, rows)], in_sems.at[c])
                for c in range(cores)
            ]
        for index, ref in enumerate(received):
            loads.append(pltpu.make_async_copy(ref, terms[index], in_sems.at[cores + index]))
        for load in loads:
            load.start()
        for load in loads:
            load.wait()
        for col, term in zip(cols, terms):
            span = slice(col, col + term.shape[1])
            total[:, span] += term[...].astype(jnp.float32)
        copies = [
            pltpu.make_async_copy(total.at[pl.ds(c * rows, rows)], own(c), out_sems.at[c])
            for c in range(cores)
        ]
        for copy in copies:
            copy.start()
        for copy in copies:
            copy.wait()


def place(scores, where, kept, received, cols, start):
    count = scores.shape[-1]
    rows = received[0].shape[0]
    operands = [*kept, *received, scores]
    return pl.pallas_call(
        functools.partial(place_kernel, start, cols, len(kept)),
        in_specs=[in_smem] * 2 + [anywhere] * len(operands),
        out_specs=anywhere,
        out_shape=jax.ShapeDtypeStruct(scores.shape, jnp.float32),
        scratch_shapes=[
            pltpu.VMEM((rows, count), jnp.float32),
            pltpu.SemaphoreType.DMA((cores + len(received),)),
            pltpu.SemaphoreType.DMA((cores,)),
        ] + [pltpu.VMEM(term.shape, jnp.bfloat16) for term in received],
        input_output_aliases={1 + len(operands): 0},
        compiler_params=pltpu.CompilerParams(vmem_limit_bytes=12 * mib),
        cost_estimate=small,
        name="place",
    )(*where, *operands)


def cut_kernel(whole_ref, *refs):
    rows = refs[0].shape[0]
    for part, ref in enumerate(refs):
        ref[...] = whole_ref[part * rows:(part + 1) * rows, :]


def cut(whole, count):
    if count == 1:
        return [whole]
    piece = jax.ShapeDtypeStruct((whole.shape[0] // count, whole.shape[1]), whole.dtype)
    return pl.pallas_call(
        cut_kernel,
        in_specs=[in_vmem],
        out_specs=[in_vmem] * count,
        out_shape=[piece] * count,
        compiler_params=pltpu.CompilerParams(vmem_limit_bytes=6 * mib),
        cost_estimate=small,
        name="cut",
    )(whole)


def after(array, *others):
    return lax.optimization_barrier((array, *others))[0]


def shards(blks, owners, grad_codes, scale_exps, val_grads, fisher):
    chips = blks // cores
    chips_per_owner = chips // owners
    me = lax.axis_index("dim")
    blk = lax.axis_index("blk")
    chip, core = blk // cores, lax.rem(blk, cores)[None]
    own, width = val_grads.shape
    count = grad_codes.shape[0]
    fisher = fisher[None, :]
    shape = (chips_per_owner, cores, own, count)

    ring = [*range(0, chips, 2), *reversed(range(1, chips, 2))]
    origin = [
        [ring[(ring.index(z) - hop) % chips] for z in range(chips)] for hop in range(chips)
    ]

    def shift(panel, by=1):
        pairs = [
            (ring[place] * cores + c, ring[(place + by) % chips] * cores + c)
            for place in range(chips) for c in range(cores)
        ]
        return lax.ppermute(panel, "blk", pairs)

    def swap(parts):
        pairs = [(b, b ^ 1) for b in range(blks)]
        return [lax.ppermute(part, "blk", pairs) for part in parts]

    def exchange(send, by):
        received = []
        for step in range(1, owners):
            pairs = []
            for b in range(blks):
                owner = origin[by][b // cores] // chips_per_owner
                pairs.append((b * owners + (owner + step) % owners, b * owners + owner))
            received.append(lax.ppermute(send, ("blk", "dim"), pairs))
        return received

    def whose(by):
        source = sum(jnp.where(chip == z, origin[by][z], 0) for z in range(chips))
        mine = (source // chips_per_owner == me).astype(jnp.int32)[None]
        return mine, lax.rem(source, chips_per_owner)[None]

    hops = chips - 1
    flow = shift(val_grads)
    train, keep, send = first(core, val_grads, *swap([val_grads]), fisher, grad_codes, scale_exps)
    low_piece, high_piece = cut(after(val_grads, send), 2)
    scores, kept = None, [keep]
    for hop in range(1, hops):
        received = exchange(send, hop - 1)
        panel = after(flow, send, low_piece, *([] if scores is None else [scores]))
        if hop + 1 < hops:
            flow = shift(panel)
        else:
            flow = shift(after(low_piece, panel), -1)
        if hop > 1:
            panel = after(panel, *received)
        scores, send = multiply(
            scores, shape, whose(hop), core, [panel], swap([panel]), fisher, train, 0
        )
        received = [after(term, send) for term in received]
        scores = place(scores, whose(hop - 1), kept, received, [0] * len(received), 0)
        kept = []
    earlier = exchange(send, hops - 1)
    high_flow = shift(after(high_piece, send), -1)
    low_piece = after(flow, send, scores)
    scores, send = multiply(
        scores, shape, whose(hops), core, [low_piece], swap(cut(low_piece, 2)), fisher, train, 0
    )
    received = exchange(send, hops)
    high_piece = after(high_flow, send, *earlier)
    high_other = swap(cut(high_piece, max(1, min(4, high_piece.shape[0] // 16))))
    knee = count * 3 // 4
    halves = []
    for top, bottom in ((0, knee), (knee, count)):
        if top:
            high_piece = after(high_piece, send, *received)
        scores, send = multiply(
            scores, shape, whose(hops), core, [high_piece], high_other, fisher, train, own // 2,
            (top, bottom),
        )
        halves.append(exchange(send, hops))
    earlier = [after(term, send) for term in earlier]
    scores = place(scores, whose(hops - 1), [], earlier, [0] * len(earlier), 0)
    received = [after(term, scores) for term in received]
    scores = place(scores, whose(hops), [], received, [0] * len(received), 0)
    cols = [0] * len(halves[0]) + [knee] * len(halves[1])
    scores = place(scores, whose(hops), [], halves[0] + halves[1], cols, own // 2)
    return scores.reshape(chips_per_owner * cores * own, count)


def solution(mesh):
    in_specs = (
        P(("groups", "blk"), "dim"),
        P(("groups", "blk"), "dim"),
        P(("groups", "blk"), "dim"),
        P("dim"),
    )
    out_specs = P("dim", ("groups", "blk"))
    body = functools.partial(shards, mesh.shape["blk"], mesh.shape["dim"])
    return jax.shard_map(body, mesh=mesh, in_specs=in_specs, out_specs=out_specs, check_vma=False)
```

```python
import functools

import jax
import jax.numpy as jnp
from jax import lax
from jax.experimental import pallas as pl
from jax.experimental.pallas import tpu as pltpu
from jax.sharding import PartitionSpec as P

damping = 0.05
lanes = 128
cores = 2
mib = 1 << 20
in_vmem = pl.BlockSpec(memory_space=pltpu.VMEM)
in_smem = pl.BlockSpec(memory_space=pltpu.SMEM)
anywhere = pl.BlockSpec(memory_space=pl.ANY)
small = pl.CostEstimate(flops=1, bytes_accessed=1, transcendentals=0)


def first_kernel(core_ref, mine_ref, other_ref, fisher_ref, codes_ref, exps_ref, train_ref, keep_ref,
                 send_ref, left, spread):
    rows, width = mine_ref.shape
    depth = min(width, 1024)
    core = core_ref[0]

    @pl.when(pl.program_id(0) == 0)
    def _():
        block = lax.broadcasted_iota(jnp.int32, spread.shape, 0)
        col = lax.broadcasted_iota(jnp.int32, spread.shape, 1)
        spread[...] = jnp.where(col // lanes == block, 1.0, 0.0).astype(jnp.bfloat16)
        for ref, place in ((mine_ref, core), (other_ref, 1 - core)):
            spot = pl.ds(pl.multiple_of(place * rows, rows), rows)
            for start in range(0, width, depth):
                cols = slice(start, start + depth)
                scale = 1.0 / (fisher_ref[:, cols] + damping)
                left[spot, cols] = (ref[:, cols].astype(jnp.float32) * scale).astype(jnp.bfloat16)

    exps = exps_ref[...]
    up = jnp.left_shift(1, jnp.maximum(exps, 0)).astype(jnp.float32)
    down = jnp.left_shift(1, jnp.maximum(-exps, 0)).astype(jnp.float32)
    factor = (up / down).astype(jnp.bfloat16)
    for start in range(0, width, depth):
        cols = slice(start, start + depth)
        wide = jnp.dot(factor, spread[:, cols], preferred_element_type=jnp.float32)
        train_ref[:, cols] = codes_ref[:, cols] * wide.astype(jnp.bfloat16)
    sums = lax.dot_general(
        left[...], train_ref[...], (((1,), (1,)), ((), ())), preferred_element_type=jnp.float32
    )
    keep_ref[...] = sums
    send_ref[...] = sums.astype(jnp.bfloat16)


def first(core, mine, other, fisher, codes, exps):
    rows, width = mine.shape
    count = codes.shape[0]
    blocks = width // lanes
    tile = min(count, 256)
    shape = (cores * rows, count)
    return pl.pallas_call(
        first_kernel,
        grid=(count // tile,),
        in_specs=[
            in_smem,
            pl.BlockSpec((rows, width), lambda i: (0, 0)),
            pl.BlockSpec((rows, width), lambda i: (0, 0)),
            pl.BlockSpec((1, width), lambda i: (0, 0)),
            pl.BlockSpec((tile, width), lambda i: (i, 0)),
            pl.BlockSpec((tile, blocks), lambda i: (i, 0)),
        ],
        out_specs=[
            pl.BlockSpec((tile, width), lambda i: (i, 0)),
            pl.BlockSpec((cores * rows, tile), lambda i: (0, i)),
            pl.BlockSpec((cores * rows, tile), lambda i: (0, i)),
        ],
        out_shape=[
            jax.ShapeDtypeStruct((count, width), jnp.bfloat16),
            jax.ShapeDtypeStruct(shape, jnp.float32),
            jax.ShapeDtypeStruct(shape, jnp.bfloat16),
        ],
        scratch_shapes=[
            pltpu.VMEM((cores * rows, width), jnp.bfloat16),
            pltpu.VMEM((blocks, width), jnp.bfloat16),
        ],
        compiler_params=pltpu.CompilerParams(vmem_limit_bytes=36 * mib),
        cost_estimate=small,
        name="first",
    )(core, mine, other, fisher, codes, exps)


def multiply_kernel(counts, start, top, mine_ref, spot_ref, core_ref, *refs):
    refs = list(refs)
    mine_refs, other_refs, _ = [[refs.pop(0) for _ in range(size)] for size in counts]
    fisher_ref, train_ref, scores_ref, send_ref = refs[:4]
    left, held, keep, send, train_sems, keep_sems, send_sems = refs[4:]
    rows = sum(ref.shape[0] for ref in mine_refs)
    slots, tile, width = held.shape
    tiles = keep_sems.shape[0]
    parts = train_sems.shape[1]
    share = tile // parts
    depth = min(width, 1024)
    core = core_ref[0]

    def fetches(i):
        slot = lax.rem(i, slots)
        return [
            pltpu.make_async_copy(
                train_ref.at[pl.ds(pl.multiple_of(i * tile, tile) + top + part * share, share)],
                held.at[slot, pl.ds(part * share, share)],
                train_sems.at[slot, part],
            )
            for part in range(parts)
        ]

    for i in range(min(slots, tiles)):
        for fetch in fetches(i):
            fetch.start()

    @pl.loop(0, width // depth)
    def _(k):
        cols = pl.ds(pl.multiple_of(k * depth, depth), depth)
        scale = 1.0 / (fisher_ref[:, cols] + damping)
        for group, place in ((mine_refs, core), (other_refs, 1 - core)):
            offset = 0
            for ref in group:
                spot = pl.ds(pl.multiple_of(place * rows, rows) + offset, ref.shape[0])
                left[spot, cols] = (ref[:, cols].astype(jnp.float32) * scale).astype(jnp.bfloat16)
                offset += ref.shape[0]

    def stores(i, of_mine):
        slot = lax.rem(i, 2)
        cols = pl.ds(pl.multiple_of(i * tile, tile), tile)
        if not of_mine:
            return [pltpu.make_async_copy(send.at[slot], send_ref.at[:, cols], send_sems.at[i])]
        return [
            pltpu.make_async_copy(
                keep.at[slot, pl.ds(c * rows, rows)],
                scores_ref.at[
                    spot_ref[0], c, pl.ds(start, rows),
                    pl.ds(pl.multiple_of(i * tile, tile) + top, tile),
                ],
                keep_sems.at[i, c],
            )
            for c in range(cores)
        ]

    def wait_stores(i):
        for flag in (0, 1):
            @pl.when(mine_ref[0] == flag)
            def _():
                for store in stores(i, flag):
                    store.wait()

    @pl.loop(0, tiles)
    def _(i):
        for fetch in fetches(i):
            fetch.wait()
        block = held[lax.rem(i, slots)]
        if cores * rows <= 128:
            sums = lax.dot_general(
                block, left[...], (((1,), (1,)), ((), ())), preferred_element_type=jnp.float32
            ).T
        else:
            sums = lax.dot_general(
                left[...], block, (((1,), (1,)), ((), ())), preferred_element_type=jnp.float32
            )

        @pl.when(i >= 2)
        def _():
            wait_stores(i - 2)

        @pl.when(mine_ref[0] == 1)
        def _():
            keep[lax.rem(i, 2)] = sums
            for store in stores(i, True):
                store.start()

        @pl.when(mine_ref[0] == 0)
        def _():
            send[lax.rem(i, 2)] = sums.astype(jnp.bfloat16)
            for store in stores(i, False):
                store.start()

        @pl.when(i + slots < tiles)
        def _():
            for fetch in fetches(i + slots):
                fetch.start()

    for i in range(max(tiles - 2, 0), tiles):
        wait_stores(i)


def multiply(scores, shape, where, core, mine, other, fisher, train, start, span=None):
    rows = sum(part.shape[0] for part in mine)
    width = mine[0].shape[1]
    top, bottom = span or (0, train.shape[0])
    count = bottom - top
    tile = min(count, 256)
    slots = 4 if cores * rows <= 128 else 3
    block = (cores * rows, count)
    given = [] if scores is None else [scores]
    counts = (len(mine), len(other), len(given))
    return pl.pallas_call(
        functools.partial(multiply_kernel, counts, start, top),
        in_specs=[in_smem] * 3 + [in_vmem] * sum(counts[:2]) + [anywhere] * len(given) + [in_vmem, anywhere],
        out_specs=[anywhere] * 2,
        out_shape=[
            jax.ShapeDtypeStruct(shape, jnp.float32), jax.ShapeDtypeStruct(block, jnp.bfloat16),
        ],
        scratch_shapes=[
            pltpu.VMEM((cores * rows, width), jnp.bfloat16),
            pltpu.VMEM((slots, tile, width), jnp.bfloat16),
            pltpu.VMEM((2, cores * rows, tile), jnp.float32),
            pltpu.VMEM((2, cores * rows, tile), jnp.bfloat16),
            pltpu.SemaphoreType.DMA((slots, 4)),
            pltpu.SemaphoreType.DMA((count // tile, cores)),
            pltpu.SemaphoreType.DMA((count // tile,)),
        ],
        input_output_aliases={3 + len(mine) + len(other): 0} if given else {},
        compiler_params=pltpu.CompilerParams(vmem_limit_bytes=22 * mib),
        cost_estimate=small,
        name="multiply",
    )(*where, core, *mine, *other, *given, fisher, train)


def place_kernel(start, cols, kept, mine_ref, spot_ref, *refs):
    first_ref, received = refs[:kept], refs[kept:kept + len(cols)]
    scores_ref, total, in_sems, out_sems, *terms = refs[kept + len(cols) + 1:]
    rows = total.shape[0] // cores

    def own(c):
        return scores_ref.at[spot_ref[0], c, pl.ds(start, rows)]

    @pl.when(mine_ref[0] == 1)
    def _():
        if kept:
            loads = [pltpu.make_async_copy(first_ref[0], total, in_sems.at[0])]
        else:
            loads = [
                pltpu.make_async_copy(own(c), total.at[pl.ds(c * rows, rows)], in_sems.at[c])
                for c in range(cores)
            ]
        for index, ref in enumerate(received):
            loads.append(pltpu.make_async_copy(ref, terms[index], in_sems.at[cores + index]))
        for load in loads:
            load.start()
        for load in loads:
            load.wait()
        for col, term in zip(cols, terms):
            span = slice(col, col + term.shape[1])
            total[:, span] += term[...].astype(jnp.float32)
        copies = [
            pltpu.make_async_copy(total.at[pl.ds(c * rows, rows)], own(c), out_sems.at[c])
            for c in range(cores)
        ]
        for copy in copies:
            copy.start()
        for copy in copies:
            copy.wait()


def place(scores, where, kept, received, cols, start):
    count = scores.shape[-1]
    rows = received[0].shape[0]
    operands = [*kept, *received, scores]
    return pl.pallas_call(
        functools.partial(place_kernel, start, cols, len(kept)),
        in_specs=[in_smem] * 2 + [anywhere] * len(operands),
        out_specs=anywhere,
        out_shape=jax.ShapeDtypeStruct(scores.shape, jnp.float32),
        scratch_shapes=[
            pltpu.VMEM((rows, count), jnp.float32),
            pltpu.SemaphoreType.DMA((cores + len(received),)),
            pltpu.SemaphoreType.DMA((cores,)),
        ] + [pltpu.VMEM(term.shape, jnp.bfloat16) for term in received],
        input_output_aliases={1 + len(operands): 0},
        compiler_params=pltpu.CompilerParams(vmem_limit_bytes=12 * mib),
        cost_estimate=small,
        name="place",
    )(*where, *operands)


def cut_kernel(whole_ref, *refs):
    rows = refs[0].shape[0]
    for part, ref in enumerate(refs):
        ref[...] = whole_ref[part * rows:(part + 1) * rows, :]


def cut(whole, count):
    if count == 1:
        return [whole]
    piece = jax.ShapeDtypeStruct((whole.shape[0] // count, whole.shape[1]), whole.dtype)
    return pl.pallas_call(
        cut_kernel,
        in_specs=[in_vmem],
        out_specs=[in_vmem] * count,
        out_shape=[piece] * count,
        compiler_params=pltpu.CompilerParams(vmem_limit_bytes=6 * mib),
        cost_estimate=small,
        name="cut",
    )(whole)


def after(array, *others):
    return lax.optimization_barrier((array, *others))[0]


def shards(blks, owners, grad_codes, scale_exps, val_grads, fisher):
    chips = blks // cores
    chips_per_owner = chips // owners
    me = lax.axis_index("dim")
    blk = lax.axis_index("blk")
    chip, core = blk // cores, lax.rem(blk, cores)[None]
    own, width = val_grads.shape
    count = grad_codes.shape[0]
    fisher = fisher[None, :]
    shape = (chips_per_owner, cores, own, count)

    ring = [*range(0, chips, 2), *reversed(range(1, chips, 2))]
    origin = [
        [ring[(ring.index(z) - hop) % chips] for z in range(chips)] for hop in range(chips)
    ]

    def shift(panel, by=1):
        pairs = [
            (ring[place] * cores + c, ring[(place + by) % chips] * cores + c)
            for place in range(chips) for c in range(cores)
        ]
        return lax.ppermute(panel, "blk", pairs)

    def swap(parts):
        pairs = [(b, b ^ 1) for b in range(blks)]
        return [lax.ppermute(part, "blk", pairs) for part in parts]

    def exchange(send, by):
        received = []
        for step in range(1, owners):
            pairs = []
            for b in range(blks):
                owner = origin[by][b // cores] // chips_per_owner
                pairs.append((b * owners + (owner + step) % owners, b * owners + owner))
            received.append(lax.ppermute(send, ("blk", "dim"), pairs))
        return received

    def whose(by):
        source = sum(jnp.where(chip == z, origin[by][z], 0) for z in range(chips))
        mine = (source // chips_per_owner == me).astype(jnp.int32)[None]
        return mine, lax.rem(source, chips_per_owner)[None]

    hops = chips - 1
    flow = shift(val_grads)
    train, keep, send = first(core, val_grads, *swap([val_grads]), fisher, grad_codes, scale_exps)
    low_piece, high_piece = cut(after(val_grads, send), 2)
    scores, kept = None, [keep]
    for hop in range(1, hops):
        received = exchange(send, hop - 1)
        panel = after(flow, send, low_piece, *([] if scores is None else [scores]))
        if hop + 1 < hops:
            flow = shift(panel)
        else:
            flow = shift(after(low_piece, panel), -1)
        if hop > 1:
            panel = after(panel, *received)
        scores, send = multiply(
            scores, shape, whose(hop), core, [panel], swap([panel]), fisher, train, 0
        )
        received = [after(term, send) for term in received]
        scores = place(scores, whose(hop - 1), kept, received, [0] * len(received), 0)
        kept = []
    earlier = exchange(send, hops - 1)
    high_flow = shift(after(high_piece, send), -1)
    low_piece = after(flow, send, scores)
    scores, send = multiply(
        scores, shape, whose(hops), core, [low_piece], swap(cut(low_piece, 2)), fisher, train, 0
    )
    received = exchange(send, hops)
    high_piece = after(high_flow, send, *earlier)
    high_other = swap(cut(high_piece, max(1, min(4, high_piece.shape[0] // 16))))
    knee = count * 5 // 8
    halves = []
    for top, bottom in ((0, knee), (knee, count)):
        if top:
            high_piece = after(high_piece, send, *received)
        scores, send = multiply(
            scores, shape, whose(hops), core, [high_piece], high_other, fisher, train, own // 2,
            (top, bottom),
        )
        halves.append(exchange(send, hops))
    earlier = [after(term, send) for term in earlier]
    scores = place(scores, whose(hops - 1), [], earlier, [0] * len(earlier), 0)
    received = [after(term, scores) for term in received]
    scores = place(scores, whose(hops), [], received, [0] * len(received), 0)
    cols = [0] * len(halves[0]) + [knee] * len(halves[1])
    scores = place(scores, whose(hops), [], halves[0] + halves[1], cols, own // 2)
    return scores.reshape(chips_per_owner * cores * own, count)


def solution(mesh):
    in_specs = (
        P(("groups", "blk"), "dim"),
        P(("groups", "blk"), "dim"),
        P(("groups", "blk"), "dim"),
        P("dim"),
    )
    out_specs = P("dim", ("groups", "blk"))
    body = functools.partial(shards, mesh.shape["blk"], mesh.shape["dim"])
    return jax.shard_map(body, mesh=mesh, in_specs=in_specs, out_specs=out_specs, check_vma=False)
```

```python
import functools

import jax
import jax.numpy as jnp
from jax import lax
from jax.experimental import pallas as pl
from jax.experimental.pallas import tpu as pltpu
from jax.sharding import PartitionSpec as P

damping = 0.05
lanes = 128
cores = 2
mib = 1 << 20
in_vmem = pl.BlockSpec(memory_space=pltpu.VMEM)
in_smem = pl.BlockSpec(memory_space=pltpu.SMEM)
anywhere = pl.BlockSpec(memory_space=pl.ANY)
small = pl.CostEstimate(flops=1, bytes_accessed=1, transcendentals=0)


def first_kernel(core_ref, mine_ref, other_ref, fisher_ref, codes_ref, exps_ref, train_ref, keep_ref,
                 send_ref, left, spread):
    rows, width = mine_ref.shape
    depth = min(width, 1024)
    core = core_ref[0]

    @pl.when(pl.program_id(0) == 0)
    def _():
        block = lax.broadcasted_iota(jnp.int32, spread.shape, 0)
        col = lax.broadcasted_iota(jnp.int32, spread.shape, 1)
        spread[...] = jnp.where(col // lanes == block, 1.0, 0.0).astype(jnp.bfloat16)
        for ref, place in ((mine_ref, core), (other_ref, 1 - core)):
            spot = pl.ds(pl.multiple_of(place * rows, rows), rows)
            for start in range(0, width, depth):
                cols = slice(start, start + depth)
                scale = 1.0 / (fisher_ref[:, cols] + damping)
                left[spot, cols] = (ref[:, cols].astype(jnp.float32) * scale).astype(jnp.bfloat16)

    exps = exps_ref[...]
    up = jnp.left_shift(1, jnp.maximum(exps, 0)).astype(jnp.float32)
    down = jnp.left_shift(1, jnp.maximum(-exps, 0)).astype(jnp.float32)
    factor = (up / down).astype(jnp.bfloat16)
    for start in range(0, width, depth):
        cols = slice(start, start + depth)
        wide = jnp.dot(factor, spread[:, cols], preferred_element_type=jnp.float32)
        train_ref[:, cols] = codes_ref[:, cols] * wide.astype(jnp.bfloat16)
    sums = lax.dot_general(
        left[...], train_ref[...], (((1,), (1,)), ((), ())), preferred_element_type=jnp.float32
    )
    keep_ref[...] = sums
    send_ref[...] = sums.astype(jnp.bfloat16)


def first(core, mine, other, fisher, codes, exps):
    rows, width = mine.shape
    count = codes.shape[0]
    blocks = width // lanes
    tile = min(count, 256)
    shape = (cores * rows, count)
    return pl.pallas_call(
        first_kernel,
        grid=(count // tile,),
        in_specs=[
            in_smem,
            pl.BlockSpec((rows, width), lambda i: (0, 0)),
            pl.BlockSpec((rows, width), lambda i: (0, 0)),
            pl.BlockSpec((1, width), lambda i: (0, 0)),
            pl.BlockSpec((tile, width), lambda i: (i, 0)),
            pl.BlockSpec((tile, blocks), lambda i: (i, 0)),
        ],
        out_specs=[
            pl.BlockSpec((tile, width), lambda i: (i, 0)),
            pl.BlockSpec((cores * rows, tile), lambda i: (0, i)),
            pl.BlockSpec((cores * rows, tile), lambda i: (0, i)),
        ],
        out_shape=[
            jax.ShapeDtypeStruct((count, width), jnp.bfloat16),
            jax.ShapeDtypeStruct(shape, jnp.float32),
            jax.ShapeDtypeStruct(shape, jnp.bfloat16),
        ],
        scratch_shapes=[
            pltpu.VMEM((cores * rows, width), jnp.bfloat16),
            pltpu.VMEM((blocks, width), jnp.bfloat16),
        ],
        compiler_params=pltpu.CompilerParams(vmem_limit_bytes=36 * mib),
        cost_estimate=small,
        name="first",
    )(core, mine, other, fisher, codes, exps)


def multiply_kernel(counts, start, top, mine_ref, spot_ref, core_ref, *refs):
    refs = list(refs)
    mine_refs, other_refs, _ = [[refs.pop(0) for _ in range(size)] for size in counts]
    fisher_ref, train_ref, scores_ref, send_ref = refs[:4]
    left, held, keep, send, train_sems, keep_sems, send_sems = refs[4:]
    rows = sum(ref.shape[0] for ref in mine_refs)
    slots, tile, width = held.shape
    tiles = keep_sems.shape[0]
    parts = train_sems.shape[1]
    share = tile // parts
    depth = min(width, 1024)
    core = core_ref[0]

    def fetches(i):
        slot = lax.rem(i, slots)
        return [
            pltpu.make_async_copy(
                train_ref.at[pl.ds(pl.multiple_of(i * tile, tile) + top + part * share, share)],
                held.at[slot, pl.ds(part * share, share)],
                train_sems.at[slot, part],
            )
            for part in range(parts)
        ]

    for i in range(min(slots, tiles)):
        for fetch in fetches(i):
            fetch.start()

    @pl.loop(0, width // depth)
    def _(k):
        cols = pl.ds(pl.multiple_of(k * depth, depth), depth)
        scale = 1.0 / (fisher_ref[:, cols] + damping)
        for group, place in ((mine_refs, core), (other_refs, 1 - core)):
            offset = 0
            for ref in group:
                spot = pl.ds(pl.multiple_of(place * rows, rows) + offset, ref.shape[0])
                left[spot, cols] = (ref[:, cols].astype(jnp.float32) * scale).astype(jnp.bfloat16)
                offset += ref.shape[0]

    def stores(i, of_mine):
        slot = lax.rem(i, 2)
        cols = pl.ds(pl.multiple_of(i * tile, tile), tile)
        if not of_mine:
            return [pltpu.make_async_copy(send.at[slot], send_ref.at[:, cols], send_sems.at[i])]
        return [
            pltpu.make_async_copy(
                keep.at[slot, pl.ds(c * rows, rows)],
                scores_ref.at[
                    spot_ref[0], c, pl.ds(start, rows),
                    pl.ds(pl.multiple_of(i * tile, tile) + top, tile),
                ],
                keep_sems.at[i, c],
            )
            for c in range(cores)
        ]

    def wait_stores(i):
        for flag in (0, 1):
            @pl.when(mine_ref[0] == flag)
            def _():
                for store in stores(i, flag):
                    store.wait()

    @pl.loop(0, tiles)
    def _(i):
        for fetch in fetches(i):
            fetch.wait()
        block = held[lax.rem(i, slots)]
        if cores * rows <= 256:
            sums = lax.dot_general(
                block, left[...], (((1,), (1,)), ((), ())), preferred_element_type=jnp.float32
            ).T
        else:
            sums = lax.dot_general(
                left[...], block, (((1,), (1,)), ((), ())), preferred_element_type=jnp.float32
            )

        @pl.when(i >= 2)
        def _():
            wait_stores(i - 2)

        @pl.when(mine_ref[0] == 1)
        def _():
            keep[lax.rem(i, 2)] = sums
            for store in stores(i, True):
                store.start()

        @pl.when(mine_ref[0] == 0)
        def _():
            send[lax.rem(i, 2)] = sums.astype(jnp.bfloat16)
            for store in stores(i, False):
                store.start()

        @pl.when(i + slots < tiles)
        def _():
            for fetch in fetches(i + slots):
                fetch.start()

    for i in range(max(tiles - 2, 0), tiles):
        wait_stores(i)


def multiply(scores, shape, where, core, mine, other, fisher, train, start, span=None):
    rows = sum(part.shape[0] for part in mine)
    width = mine[0].shape[1]
    top, bottom = span or (0, train.shape[0])
    count = bottom - top
    tile = min(count, 256)
    slots = 3
    block = (cores * rows, count)
    given = [] if scores is None else [scores]
    counts = (len(mine), len(other), len(given))
    return pl.pallas_call(
        functools.partial(multiply_kernel, counts, start, top),
        in_specs=[in_smem] * 3 + [in_vmem] * sum(counts[:2]) + [anywhere] * len(given) + [in_vmem, anywhere],
        out_specs=[anywhere] * 2,
        out_shape=[
            jax.ShapeDtypeStruct(shape, jnp.float32), jax.ShapeDtypeStruct(block, jnp.bfloat16),
        ],
        scratch_shapes=[
            pltpu.VMEM((cores * rows, width), jnp.bfloat16),
            pltpu.VMEM((slots, tile, width), jnp.bfloat16),
            pltpu.VMEM((2, cores * rows, tile), jnp.float32),
            pltpu.VMEM((2, cores * rows, tile), jnp.bfloat16),
            pltpu.SemaphoreType.DMA((slots, 4)),
            pltpu.SemaphoreType.DMA((count // tile, cores)),
            pltpu.SemaphoreType.DMA((count // tile,)),
        ],
        input_output_aliases={3 + len(mine) + len(other): 0} if given else {},
        compiler_params=pltpu.CompilerParams(vmem_limit_bytes=22 * mib),
        cost_estimate=small,
        name="multiply",
    )(*where, core, *mine, *other, *given, fisher, train)


def place_kernel(start, cols, kept, mine_ref, spot_ref, *refs):
    first_ref, received = refs[:kept], refs[kept:kept + len(cols)]
    scores_ref, total, in_sems, out_sems, *terms = refs[kept + len(cols) + 1:]
    rows = total.shape[0] // cores

    def own(c):
        return scores_ref.at[spot_ref[0], c, pl.ds(start, rows)]

    @pl.when(mine_ref[0] == 1)
    def _():
        if kept:
            loads = [pltpu.make_async_copy(first_ref[0], total, in_sems.at[0])]
        else:
            loads = [
                pltpu.make_async_copy(own(c), total.at[pl.ds(c * rows, rows)], in_sems.at[c])
                for c in range(cores)
            ]
        for index, ref in enumerate(received):
            loads.append(pltpu.make_async_copy(ref, terms[index], in_sems.at[cores + index]))
        for load in loads:
            load.start()
        for load in loads:
            load.wait()
        for col, term in zip(cols, terms):
            span = slice(col, col + term.shape[1])
            total[:, span] += term[...].astype(jnp.float32)
        copies = [
            pltpu.make_async_copy(total.at[pl.ds(c * rows, rows)], own(c), out_sems.at[c])
            for c in range(cores)
        ]
        for copy in copies:
            copy.start()
        for copy in copies:
            copy.wait()


def place(scores, where, kept, received, cols, start):
    count = scores.shape[-1]
    rows = received[0].shape[0]
    operands = [*kept, *received, scores]
    return pl.pallas_call(
        functools.partial(place_kernel, start, cols, len(kept)),
        in_specs=[in_smem] * 2 + [anywhere] * len(operands),
        out_specs=anywhere,
        out_shape=jax.ShapeDtypeStruct(scores.shape, jnp.float32),
        scratch_shapes=[
            pltpu.VMEM((rows, count), jnp.float32),
            pltpu.SemaphoreType.DMA((cores + len(received),)),
            pltpu.SemaphoreType.DMA((cores,)),
        ] + [pltpu.VMEM(term.shape, jnp.bfloat16) for term in received],
        input_output_aliases={1 + len(operands): 0},
        compiler_params=pltpu.CompilerParams(vmem_limit_bytes=12 * mib),
        cost_estimate=small,
        name="place",
    )(*where, *operands)


def cut_kernel(whole_ref, *refs):
    rows = refs[0].shape[0]
    for part, ref in enumerate(refs):
        ref[...] = whole_ref[part * rows:(part + 1) * rows, :]


def cut(whole, count):
    if count == 1:
        return [whole]
    piece = jax.ShapeDtypeStruct((whole.shape[0] // count, whole.shape[1]), whole.dtype)
    return pl.pallas_call(
        cut_kernel,
        in_specs=[in_vmem],
        out_specs=[in_vmem] * count,
        out_shape=[piece] * count,
        compiler_params=pltpu.CompilerParams(vmem_limit_bytes=6 * mib),
        cost_estimate=small,
        name="cut",
    )(whole)


def after(array, *others):
    return lax.optimization_barrier((array, *others))[0]


def shards(blks, owners, grad_codes, scale_exps, val_grads, fisher):
    chips = blks // cores
    chips_per_owner = chips // owners
    me = lax.axis_index("dim")
    blk = lax.axis_index("blk")
    chip, core = blk // cores, lax.rem(blk, cores)[None]
    own, width = val_grads.shape
    count = grad_codes.shape[0]
    fisher = fisher[None, :]
    shape = (chips_per_owner, cores, own, count)

    ring = [*range(0, chips, 2), *reversed(range(1, chips, 2))]
    origin = [
        [ring[(ring.index(z) - hop) % chips] for z in range(chips)] for hop in range(chips)
    ]

    def shift(panel, by=1):
        pairs = [
            (ring[place] * cores + c, ring[(place + by) % chips] * cores + c)
            for place in range(chips) for c in range(cores)
        ]
        return lax.ppermute(panel, "blk", pairs)

    def swap(parts):
        pairs = [(b, b ^ 1) for b in range(blks)]
        return [lax.ppermute(part, "blk", pairs) for part in parts]

    def exchange(send, by):
        received = []
        for step in range(1, owners):
            pairs = []
            for b in range(blks):
                owner = origin[by][b // cores] // chips_per_owner
                pairs.append((b * owners + (owner + step) % owners, b * owners + owner))
            received.append(lax.ppermute(send, ("blk", "dim"), pairs))
        return received

    def whose(by):
        source = sum(jnp.where(chip == z, origin[by][z], 0) for z in range(chips))
        mine = (source // chips_per_owner == me).astype(jnp.int32)[None]
        return mine, lax.rem(source, chips_per_owner)[None]

    hops = chips - 1
    flow = shift(val_grads)
    train, keep, send = first(core, val_grads, *swap([val_grads]), fisher, grad_codes, scale_exps)
    low_piece, high_piece = cut(after(val_grads, send), 2)
    scores, kept = None, [keep]
    for hop in range(1, hops):
        received = exchange(send, hop - 1)
        panel = after(flow, send, *([] if scores is None else [scores, low_piece]))
        if hop + 1 < hops:
            flow = shift(panel)
        else:
            flow = shift(after(low_piece, panel), -1)
        if hop > 1:
            panel = after(panel, *received)
        scores, send = multiply(
            scores, shape, whose(hop), core, [panel], swap([panel]), fisher, train, 0
        )
        received = [after(term, send) for term in received]
        scores = place(scores, whose(hop - 1), kept, received, [0] * len(received), 0)
        kept = []
    earlier = exchange(send, hops - 1)
    high_flow = shift(after(high_piece, send), -1)
    low_piece = after(flow, send, scores)
    scores, send = multiply(
        scores, shape, whose(hops), core, [low_piece], swap(cut(low_piece, 2)), fisher, train, 0
    )
    received = exchange(send, hops)
    high_piece = after(high_flow, send, *earlier)
    high_other = swap(cut(high_piece, max(1, min(4, high_piece.shape[0] // 16))))
    knee = count * 5 // 8
    halves = []
    for top, bottom in ((0, knee), (knee, count)):
        if top:
            high_piece = after(high_piece, send, *received)
        scores, send = multiply(
            scores, shape, whose(hops), core, [high_piece], high_other, fisher, train, own // 2,
            (top, bottom),
        )
        halves.append(exchange(send, hops))
    earlier = [after(term, send) for term in earlier]
    scores = place(scores, whose(hops - 1), [], earlier, [0] * len(earlier), 0)
    received = [after(term, scores) for term in received]
    scores = place(scores, whose(hops), [], received, [0] * len(received), 0)
    cols = [0] * len(halves[0]) + [knee] * len(halves[1])
    scores = place(scores, whose(hops), [], halves[0] + halves[1], cols, own // 2)
    return scores.reshape(chips_per_owner * cores * own, count)


def solution(mesh):
    in_specs = (
        P(("groups", "blk"), "dim"),
        P(("groups", "blk"), "dim"),
        P(("groups", "blk"), "dim"),
        P("dim"),
    )
    out_specs = P("dim", ("groups", "blk"))
    body = functools.partial(shards, mesh.shape["blk"], mesh.shape["dim"])
    return jax.shard_map(body, mesh=mesh, in_specs=in_specs, out_specs=out_specs, check_vma=False)
```
